32 devices in a mesh: dp: 4 (over y, x), ctx: 8 (over z, core).
Axes of the slice: x: 2, y: 2, z: 4, core: 2. Of those that a mesh axis runs over, the one named last changes fastest.
Arguments:
- tokens: bfloat16 [16, 1024, 1024], P('dp', 'ctx'), may hold values from -6 to 6
- cotangent: bfloat16 [16, 1024, 1024], P('dp', 'ctx'), may hold values from -6 to 6
- lengths: int32 [16], P('dp'), may hold values from 256 to 1024, as said below
- weights: float32 [12288, 1024], P('ctx'), may hold values from -1 to 1
- vectors: float32 [12288], P('ctx'), may hold values from -1.2 to 1.5
- first_weights: float32 [12288, 1024], P('ctx'), may hold values from -384 to 384
- second_weights: float32 [12288, 1024], P('ctx'), may hold values from 0.8192 to 81.92
- first_vectors: float32 [12288], P('ctx'), may hold values from -384 to 384
- second_vectors: float32 [12288], P('ctx'), may hold values from 0.8192 to 81.92
Outputs:
- layer_out: bfloat16 [16, 1024, 1024], P('dp', 'ctx')
- grad_tokens: bfloat16 [16, 1024, 1024], P('dp', 'ctx')
- grad_weights: float32 [12288, 1024], P('ctx')
- grad_vectors: float32 [12288], P('ctx')
- weight_change: float32 [12288, 1024], P('ctx')
- vector_change: float32 [12288], P('ctx')
- new_first_weights: float32 [12288, 1024], P('ctx')
- new_second_weights: float32 [12288, 1024], P('ctx')
- new_first_vectors: float32 [12288], P('ctx')
- new_second_vectors: float32 [12288], P('ctx')
The draws below stay inside these ranges and needn't reach their ends.
Inputs may be any that keep to these rules, and one draw needn't show every extreme that they name: `lengths`: in each run of 4 sequences that share an index of dp, one, drawn, has length 1024.
All inputs are finite; a program needn't handle non-finite values.
Results may differ from the reference program's by a relative error of at most 0.018.
Values may be sent and summed in bfloat16 or wider, within the bound.
No kernel may reach another device: no remote copies, remote signals or barrier semaphores. Data moves between devices by JAX's collectives and lax.ppermute only.
A program may use at most 320 MiB of HBM per device.

```python
import math
import jax
import jax.numpy as jnp
from jax import lax

D = 1024
FF = 4096
H = 16
HD = 64
SLOT = 1024
STEP = 10
SEQS_GROUP = 4
SEQS = 16
ROWS_W = 12288
VEC = 12288


def draw_lengths(key, part):
    key = jax.random.fold_in(key, 13)
    first_key, second_key = jax.random.split(key)
    groups = SEQS // SEQS_GROUP
    lengths_base = jax.random.randint(first_key, (groups, SEQS_GROUP), SLOT // 4, SLOT + 1)
    chosen = jax.random.randint(second_key, (groups, 1), 0, SEQS_GROUP)
    columns = jnp.arange(SEQS_GROUP, dtype=jnp.int32)[None, :]
    return jnp.where(columns == chosen, SLOT, lengths_base).reshape(SEQS).astype(jnp.int32)


def draw_weights(key, part):
    key = jax.random.fold_in(key, 11)
    normal_part = jax.random.truncated_normal(key, -4.0, 4.0, (ROWS_W, D), jnp.float32)
    row_index = jnp.arange(ROWS_W, dtype=jnp.int32)[:, None]
    out_scale = min(0.25, math.sqrt(SLOT / 16.0) / math.sqrt(D))
    scale_rows = jnp.where(row_index < 3 * D, 1.3 / math.sqrt(D), jnp.where(row_index < 4 * D, out_scale, jnp.where(row_index < 4 * D + FF, 1.0 / math.sqrt(D), 1.0 / math.sqrt(FF))))
    return (normal_part * scale_rows).astype(jnp.float32)


def draw_vectors(key, part):
    key = jax.random.fold_in(key, 12)
    first_key, second_key = jax.random.split(key)
    normal_part = 0.3 * jax.random.truncated_normal(first_key, -4.0, 4.0, (VEC,), jnp.float32)
    gain_part = jax.random.uniform(second_key, (VEC,), jnp.float32, 0.5, 1.5)
    position = jnp.arange(VEC, dtype=jnp.int32)
    is_gain = (position >= 4 * D + FF) & (position < 5 * D + FF) | (position >= 6 * D + FF) & (position < 7 * D + FF)
    return jnp.where(is_gain, gain_part, normal_part).astype(jnp.float32)


def steps_of(rng, extent, cuts, least, top_value):
    factor_of, own = 1.0, jax.random.fold_in(rng, 6)
    for dim, blocks in cuts:
        heights = jnp.exp(jax.random.uniform(jax.random.fold_in(own, dim), (blocks,), jnp.float32, least / len(cuts), top_value / len(cuts)))
        factor_of = factor_of * jnp.repeat(heights, extent[dim] // blocks).reshape([-1 if axis == dim else 1 for axis in range(len(extent))])
    return factor_of


def noise(rng, shape, width, bound, cuts=(), kind=jnp.bfloat16):
    values = width * jax.random.normal(rng, shape, jnp.float32)
    if cuts:
        values = values * steps_of(rng, shape, cuts, -0.22, 0.18)
    return jnp.clip(values, -bound, bound).astype(kind)


def setup_inputs(seed: int = 0) -> dict:
    seeds = jax.random.split(jax.random.key(seed), 10)
    tokens = noise(seeds[0], (SEQS, SLOT, D), 1.0, 6.0, ((0, 4), (1, 8)))
    cotangent = noise(seeds[1], (SEQS, SLOT, D), 1.0, 6.0, ((0, 4), (1, 8)))
    lengths = draw_lengths(jax.random.fold_in(seeds[9], 71), 0)
    weights = draw_weights(jax.random.fold_in(seeds[9], 71), 0)
    vectors = draw_vectors(jax.random.fold_in(seeds[9], 71), 0)
    first_weights = noise(seeds[5], (ROWS_W, D), (0.5 * (SEQS * SLOT) ** 0.5), 384.0, ((0, 8),), jnp.float32)
    second_weights = jnp.clip(jnp.exp(math.log(81.92) - 4.6051702 * jax.random.uniform(seeds[6], (ROWS_W, D), jnp.float32) ** steps_of(seeds[6], (ROWS_W, D), ((0, 8),), -0.2, 0.2)), 0.8192, 81.92)
    first_vectors = noise(seeds[7], (VEC,), (0.5 * (SEQS * SLOT) ** 0.5), 384.0, ((0, 8),), jnp.float32)
    second_vectors = jnp.clip(jnp.exp(math.log(81.92) - 4.6051702 * jax.random.uniform(seeds[8], (VEC,), jnp.float32) ** steps_of(seeds[8], (VEC,), ((0, 8),), -0.2, 0.2)), 0.8192, 81.92)
    return {"tokens": tokens, "cotangent": cotangent, "lengths": lengths, "weights": weights, "vectors": vectors, "first_weights": first_weights, "second_weights": second_weights, "first_vectors": first_vectors, "second_vectors": second_vectors}


@jax.custom_vjp
def low(v):
    return lax.optimization_barrier(v.astype(jnp.bfloat16)).astype(jnp.float32)

@jax.custom_vjp
def low_back(v):
    return v

def low_keep(v):
    return (low(v), None)

def low_pass(kept, grad):
    return (grad,)

def back_keep(v):
    return (v, None)

def back_low(kept, grad):
    return (low(grad),)
low.defvjp(low_keep, low_pass)
low_back.defvjp(back_keep, back_low)
HIGHEST = lax.Precision.HIGHEST
LEARN_RATE = 0.003

def matmul(operand, matrix):
    return jnp.dot(operand, matrix, precision=HIGHEST, preferred_element_type=jnp.float32)

def rounded(inputs):
    return low(low_back(inputs))

def layer_norm(inputs, gain_vec, shift_vec):
    centre = lax.optimization_barrier(jnp.mean(inputs, axis=-1, keepdims=True))
    shifted = inputs - centre
    spread = lax.optimization_barrier(jnp.mean(shifted * shifted, axis=-1, keepdims=True))
    return shifted * lax.rsqrt(spread + 1e-05) * gain_vec + shift_vec

def attend_one(inputs):
    queries, keys_in, values_in, allowed = inputs
    scores = jnp.einsum('qhd,khd->hqk', queries, keys_in, precision=HIGHEST) / math.sqrt(HD)
    scores = low_back(scores)
    scores = jnp.where(allowed[None, None, :], scores, -1e+30)
    highest = lax.optimization_barrier(jnp.max(scores, axis=-1, keepdims=True))
    weights_exp = jnp.exp(scores - highest)
    probabilities = weights_exp / lax.optimization_barrier(jnp.sum(weights_exp, axis=-1, keepdims=True))
    return jnp.einsum('hqk,khd->qhd', low(probabilities), values_in, precision=HIGHEST)

def layer_forward(tokens_in, lengths_in, weights_in, vectors_in):
    matrices = low(weights_in)
    vector_set = low(vectors_in)
    groups = tokens_in.shape[0]
    flat_rows = tokens_in.reshape(groups * SLOT, D)
    merged = matmul(flat_rows, matrices[:3 * D].T)
    queries = rounded(merged[:, :D] + vector_set[:D])
    keys_all = rounded(merged[:, D:2 * D])
    values_all = rounded(merged[:, 2 * D:] + vector_set[D:2 * D])
    head_shape = (groups, SLOT, H, HD)
    allowed = jnp.arange(SLOT, dtype=jnp.int32)[None, :] < lengths_in[:, None]
    attended = lax.map(jax.checkpoint(attend_one), (queries.reshape(head_shape), keys_all.reshape(head_shape), values_all.reshape(head_shape), allowed))
    heads_out = rounded(attended.reshape(groups * SLOT, D))
    branch = low_back(matmul(heads_out, matrices[3 * D:4 * D].T) + vector_set[2 * D:3 * D])
    normed_one = low(layer_norm(flat_rows + branch, vector_set[4 * D + FF:5 * D + FF], vector_set[5 * D + FF:6 * D + FF]))
    gate_in = low_back(matmul(normed_one, matrices[4 * D:4 * D + FF].T) + vector_set[3 * D:3 * D + FF])
    hidden = low(jax.nn.gelu(gate_in, approximate=False))
    feed_out = low_back(matmul(hidden, matrices[4 * D + FF:]) + vector_set[3 * D + FF:4 * D + FF])
    result = layer_norm(normed_one + feed_out, vector_set[6 * D + FF:7 * D + FF], vector_set[7 * D + FF:])
    return result.reshape(groups, SLOT, D)

def adamw_update(parameter, gradient, first_old, second_old, decay_rate):
    step_float = float(STEP)
    first_new = 0.9 * first_old + 0.1 * gradient
    second_new = 0.999 * second_old + 0.001 * gradient * gradient
    first_fix = first_new / (1.0 - 0.9 ** step_float)
    second_fix = second_new / (1.0 - 0.999 ** step_float)
    update = first_fix / (jnp.sqrt(second_fix) + 1e-08)
    return (-LEARN_RATE * (update + decay_rate * parameter), first_new, second_new)

def reference(tokens, cotangent, lengths, weights, vectors, first_weights, second_weights, first_vectors, second_vectors):
    groups = SEQS // SEQS_GROUP
    token_blocks = tokens.astype(jnp.float32).reshape(groups, SEQS_GROUP, SLOT, D)
    grad_blocks = cotangent.astype(jnp.float32).reshape(groups, SEQS_GROUP, SLOT, D)
    length_blocks = lengths.reshape(groups, SEQS_GROUP)

    def one_group(totals, block_item):
        total_w, total_v = totals
        block_rows, block_grad, block_len = block_item
        live_rows = (jnp.arange(SLOT, dtype=jnp.int32)[None, :] < block_len[:, None]).astype(jnp.float32)

        def layer_only(block_in, matrix_set, vector_part):
            return layer_forward(block_in, block_len, matrix_set, vector_part)
        result, pullback = jax.vjp(layer_only, block_rows, weights, vectors)
        grad_in, grad_mats, grad_vecs = pullback(block_grad * live_rows[:, :, None])
        return ((total_w + grad_mats, total_v + grad_vecs), (result.astype(jnp.bfloat16), grad_in.astype(jnp.bfloat16)))
    zero_init = (jnp.zeros((ROWS_W, D), jnp.float32), jnp.zeros((VEC,), jnp.float32))
    (grad_weights, grad_vectors), (layer_out, grad_tokens) = lax.scan(one_group, zero_init, (token_blocks, grad_blocks, length_blocks))
    weight_change, new_first_weights, new_second_weights = adamw_update(weights, grad_weights, first_weights, second_weights, 0.01)
    vector_change, new_first_vectors, new_second_vectors = adamw_update(vectors, grad_vectors, first_vectors, second_vectors, 0.0)
    return (layer_out.reshape(SEQS, SLOT, D), grad_tokens.reshape(SEQS, SLOT, D), grad_weights, grad_vectors, weight_change, vector_change, new_first_weights, new_second_weights, new_first_vectors, new_second_vectors)
```

```python
import math

import jax
import jax.numpy as jnp
from jax import lax
from jax.sharding import Mesh
from jax.sharding import PartitionSpec as P

D = 1024
FF = 4096
H = 16
HD = 64
STEP = 10
EPSILON = 1e-05
LEARN_RATE = 0.003
BF = jnp.bfloat16
F32 = jnp.float32
HALF = D // 2
BLOCK = 512


def rows_dot(operand, matrix):
    return lax.dot_general(operand, matrix, (((1,), (1,)), ((), ())), preferred_element_type=F32)


def cols_dot(operand, matrix):
    return lax.dot_general(operand, matrix, (((0,), (0,)), ((), ())), preferred_element_type=F32)


def plain_dot(operand, matrix):
    return lax.dot_general(operand, matrix, (((1,), (0,)), ((), ())), preferred_element_type=F32)


def swap(value):
    return lax.ppermute(value, "core", [(0, 1), (1, 0)])


def exchange(axis, bit, value):
    count = lax.axis_size(axis)
    return lax.ppermute(value, axis, [(i, i ^ bit) for i in range(count)])


def sum_all(value):
    for axis in ("core", "z", "dp"):
        bit = 1
        while bit < lax.axis_size(axis):
            value = value + exchange(axis, bit, value)
            bit *= 2
    return value


def layer_norm(inputs, gain_vec, shift_vec):
    centre = jnp.mean(inputs, axis=-1, keepdims=True)
    shifted = inputs - centre
    inverse = lax.rsqrt(jnp.mean(shifted * shifted, axis=-1, keepdims=True) + EPSILON)
    normed = shifted * inverse
    return (normed * gain_vec + shift_vec, normed, inverse)


def norm_back(grad_out, normed, inverse, gain_vec):
    scaled = grad_out * gain_vec
    inner_term = (
        scaled
        - jnp.mean(scaled, axis=-1, keepdims=True)
        - normed * jnp.mean(scaled * normed, axis=-1, keepdims=True)
    )
    return (inverse * inner_term, jnp.sum(grad_out * normed, axis=0), jnp.sum(grad_out, axis=0))


def to_chips(blocks, z):
    count = lax.axis_size("z")
    parts = []
    for shift in range(count):
        part = lax.dynamic_index_in_dim(blocks, (z + shift) % count, 0, keepdims=False)
        if shift:
            part = lax.ppermute(part, "z", [(i, (i + shift) % count) for i in range(count)])
        parts.append(part)
    return jnp.concatenate(parts, axis=0)


def from_chips(rows, z):
    count = lax.axis_size("z")
    blocks = rows.reshape(count, -1, rows.shape[-1])
    result = jnp.zeros_like(blocks)
    for shift in range(count):
        part = blocks[shift]
        if shift:
            part = lax.ppermute(part, "z", [(i, (i - shift) % count) for i in range(count)])
        result = lax.dynamic_update_index_in_dim(result, part, (z + shift) % count, 0)
    return result


def quadrants(matrix):
    half = matrix.shape[0] // 2
    return jnp.concatenate(
        [
            jnp.concatenate([matrix[:half, :half], matrix[half:, :half]], axis=1),
            jnp.concatenate([matrix[:half, half:], matrix[half:, half:]], axis=1),
        ],
        axis=0,
    )


def is_out_projection(z, core):
    return jnp.logical_and(z == 1, core == 0)


def pack_weights(weights, z, core):
    low = weights.astype(BF)
    top = jnp.where(is_out_projection(z, core), quadrants(low[:D]), low[:D])
    first, middle, last = top[:BLOCK], top[BLOCK:], low[D:]
    other = swap(middle)
    return jnp.where(
        core == 0,
        jnp.concatenate([first, last, other], axis=0),
        jnp.concatenate([other, first, last], axis=0),
    )


def unpack_grads(packed, z, core):
    a, b, c = packed[:BLOCK], packed[BLOCK : 2 * BLOCK], packed[2 * BLOCK :]
    middle = swap(jnp.where(core == 0, c, a))
    first, last = jnp.where(core == 0, a, b), jnp.where(core == 0, b, c)
    top = jnp.concatenate([first, middle], axis=0)
    top = jnp.where(is_out_projection(z, core), quadrants(top), top)
    return jnp.concatenate([top, last], axis=0).astype(F32)


def gather_weights(packed):
    count = lax.axis_size("dp")
    rows = packed.shape[0] // count
    piece = lax.dynamic_slice_in_dim(packed, lax.axis_index("dp") * rows, rows, 0)
    return lax.all_gather(piece, ("z", "dp"), axis=0, tiled=True)


def reduce_grads(blocks):
    whole = jnp.concatenate(blocks, axis=0)
    piece = lax.psum_scatter(whole, ("z", "dp"), scatter_dimension=0, tiled=True)
    return lax.all_gather(piece, "dp", axis=0, tiled=True)


def attention_scores(queries, keys, allowed):
    scores = jnp.einsum("qhd,khd->hqk", queries, keys, preferred_element_type=F32) / math.sqrt(HD)
    return jnp.where(allowed[None, None, :], scores, -1e30)


def attention_forward(queries, keys, values, allowed):
    rows, width = queries.shape
    heads = width // HD
    scores = attention_scores(queries.reshape(rows, heads, HD), keys.reshape(rows, heads, HD), allowed)
    highest = jnp.max(scores, axis=-1, keepdims=True)
    terms = jnp.exp(scores - highest)
    total = jnp.sum(terms, axis=-1, keepdims=True)
    probs = (terms / total).astype(BF)
    out = jnp.einsum(
        "hqk,khd->qhd", probs, values.reshape(rows, heads, HD), preferred_element_type=F32
    )
    return out.astype(BF).reshape(rows, width), highest + jnp.log(total)


def attention_backward(queries, keys, values, allowed, log_total, grad_out):
    rows, width = queries.shape
    heads = width // HD
    shape = (rows, heads, HD)
    queries, keys, values, grad_out = (
        item.reshape(shape) for item in (queries, keys, values, grad_out)
    )
    factor = 1.0 / math.sqrt(HD)
    probs = jnp.exp(attention_scores(queries, keys, allowed) - log_total)
    grad_probs = jnp.einsum("qhd,khd->hqk", grad_out, values, preferred_element_type=F32)
    row_sums = jnp.sum(grad_probs * probs, axis=-1, keepdims=True)
    grad_scores = (probs * (grad_probs - row_sums)).astype(BF)
    dq = jnp.einsum("hqk,khd->qhd", grad_scores, keys, preferred_element_type=F32) * factor
    dk = jnp.einsum("hqk,qhd->khd", grad_scores, queries, preferred_element_type=F32) * factor
    dv = jnp.einsum("hqk,qhd->khd", probs.astype(BF), grad_out, preferred_element_type=F32)
    return jnp.concatenate([item.astype(BF).reshape(rows, width) for item in (dq, dk, dv)], axis=1)


def adamw_update(parameter, gradient, first_old, second_old, decay_rate):
    step_float = float(STEP)
    first_new = 0.9 * first_old + 0.1 * gradient
    second_new = 0.999 * second_old + 0.001 * gradient * gradient
    first_fix = first_new / (1.0 - 0.9**step_float)
    second_fix = second_new / (1.0 - 0.999**step_float)
    update = first_fix / (jnp.sqrt(second_fix) + 1e-08)
    return (-LEARN_RATE * (update + decay_rate * parameter), first_new, second_new)


def share(partial):
    return partial[:HALF] + swap(partial[HALF:].astype(BF)).astype(F32)


def both(rows):
    return jnp.concatenate([rows, swap(rows)], axis=0)


def core_part(vector, core, pieces):
    return vector.reshape(pieces, 2, -1)[:, core].reshape(-1)


def spread_part(vector, core, pieces):
    parts = vector.reshape(pieces, 1, -1)
    mine = (jnp.arange(2) == core)[None, :, None]
    return jnp.where(mine, parts, 0.0).reshape(-1)


def shards(
    tokens,
    cotangent,
    lengths,
    weights,
    vectors,
    first_weights,
    second_weights,
    first_vectors,
    second_vectors,
):
    z, core = lax.axis_index("z"), lax.axis_index("core")
    count = lax.axis_size("z")
    per_device = tokens.shape[1]
    rows = count * per_device
    length = lengths[z]
    block = jnp.arange(count, dtype=jnp.int32)[:, None]
    inner = jnp.arange(per_device, dtype=jnp.int32)[None, :]
    chip_of = (z - block) % count
    here = ((chip_of * 2 + core) * per_device + inner).reshape(rows)
    there = ((chip_of * 2 + 1 - core) * per_device + inner).reshape(rows)
    allowed = jnp.concatenate([here, there]) < length
    live = (here < length).astype(F32)[:, None]

    vec = lax.all_gather(vectors.astype(BF), ("z", "core"), axis=0, tiled=True).astype(F32)
    bounds = [0, D, 2 * D, 3 * D, 3 * D + FF] + [(n + 4) * D + FF for n in range(6)]
    bias_q, bias_v, bias_o, bias_up, bias_down, gain_one, shift_one, gain_two, shift_two = (
        vec[bounds[n] : bounds[n + 1]] for n in range(9)
    )
    bias_q, bias_v = core_part(bias_q, core, 1), core_part(bias_v, core, 1)
    bias_up = core_part(bias_up, core, FF // (2 * BLOCK))

    whole = gather_weights(pack_weights(weights, z, core))
    w_qkv = whole[: 3 * HALF]
    w_out = whole[3 * HALF : 4 * HALF]
    w_up = whole[4 * HALF : 4 * HALF + FF // 2]
    w_down = whole[4 * HALF + FF // 2 :]

    x_mine = to_chips(tokens, z)
    x = both(x_mine)
    merged = rows_dot(x, w_qkv)
    queries = (merged[:, :HALF] + bias_q).astype(BF)
    keys = merged[:, HALF : 2 * HALF].astype(BF)
    values = (merged[:, 2 * HALF :] + bias_v).astype(BF)
    heads_out, log_total = attention_forward(queries, keys, values, allowed)

    branch = jnp.concatenate(
        [rows_dot(heads_out, w_out[:, :HALF]), rows_dot(heads_out, w_out[:, HALF:])], axis=1
    )
    normed_in, normed_one, inverse_one = layer_norm(
        x_mine.astype(F32) + share(branch) + bias_o, gain_one, shift_one
    )
    u_mine = normed_in.astype(BF)
    u = both(u_mine)
    gate_in = rows_dot(u, w_up) + bias_up
    cdf = 0.5 * (1.0 + lax.erf(gate_in * (1.0 / math.sqrt(2.0))))
    slope = cdf + gate_in * jnp.exp(-0.5 * gate_in * gate_in) * (1.0 / math.sqrt(2.0 * math.pi))
    hidden = (gate_in * cdf).astype(BF)
    feed = share(plain_dot(hidden, w_down)) + bias_down
    result, normed_two, inverse_two = layer_norm(u_mine.astype(F32) + feed, gain_two, shift_two)
    layer_out = from_chips(result.astype(BF), z)

    grad_out = to_chips(cotangent, z).astype(F32) * live
    grad_two, grad_gain_two, grad_shift_two = norm_back(grad_out, normed_two, inverse_two, gain_two)
    df_mine = grad_two.astype(BF)
    df = both(df_mine)
    grad_bias_down = jnp.sum(df_mine.astype(F32), axis=0)
    dz = (rows_dot(df, w_down) * slope).astype(BF)
    grad_down = cols_dot(hidden, df).astype(BF)
    grad_up = cols_dot(dz, u).astype(BF)
    grad_bias_up = jnp.sum(dz.astype(F32), axis=0)
    du = share(plain_dot(dz, w_up)) + grad_two
    grad_one, grad_gain_one, grad_shift_one = norm_back(du, normed_one, inverse_one, gain_one)
    da_mine = grad_one.astype(BF)
    da = both(da_mine)
    grad_bias_o = jnp.sum(da_mine.astype(F32), axis=0)
    do = (plain_dot(da[:, :HALF], w_out[:, :HALF]) + plain_dot(da[:, HALF:], w_out[:, HALF:])).astype(BF)
    grad_wo = jnp.concatenate(
        [cols_dot(da[:, :HALF], heads_out), cols_dot(da[:, HALF:], heads_out)], axis=1
    ).astype(BF)
    d_merged = attention_backward(queries, keys, values, allowed, log_total, do)
    grad_qkv = cols_dot(d_merged, x).astype(BF)
    column_sums = jnp.sum(d_merged.astype(F32), axis=0)
    grad_rows = share(plain_dot(d_merged, w_qkv)) + grad_one
    grad_tokens = from_chips(grad_rows.astype(BF), z)

    vector_grad = jnp.concatenate(
        [
            spread_part(column_sums[:HALF], core, 1),
            spread_part(column_sums[2 * HALF :], core, 1),
            grad_bias_o,
            spread_part(grad_bias_up, core, FF // (2 * BLOCK)),
            grad_bias_down,
            grad_gain_one,
            grad_shift_one,
            grad_gain_two,
            grad_shift_two,
        ]
    )
    vector_sum = sum_all(vector_grad)
    shard_v = lax.dynamic_slice_in_dim(
        vector_sum, (z * 2 + core) * vectors.shape[0], vectors.shape[0], 0
    )
    shard_w = unpack_grads(reduce_grads([grad_qkv, grad_wo, grad_up, grad_down]), z, core)

    weight_change, new_first_weights, new_second_weights = adamw_update(
        weights, shard_w, first_weights, second_weights, 0.01
    )
    vector_change, new_first_vectors, new_second_vectors = adamw_update(
        vectors, shard_v, first_vectors, second_vectors, 0.0
    )
    return (
        layer_out,
        grad_tokens,
        shard_w,
        shard_v,
        weight_change,
        vector_change,
        new_first_weights,
        new_second_weights,
        new_first_vectors,
        new_second_vectors,
    )


def solution(mesh):
    chips = Mesh(
        mesh.devices.reshape(mesh.shape["dp"], mesh.shape["ctx"] // 2, 2), ("dp", "z", "core")
    )
    ctx = ("z", "core")
    activations, matrix, vector = P("dp", ctx, None), P(ctx, None), P(ctx)
    return jax.shard_map(
        shards,
        mesh=chips,
        in_specs=(activations, activations, P("dp"), matrix, vector, matrix, matrix, vector, vector),
        out_specs=(
            activations,
            activations,
            matrix,
            vector,
            matrix,
            vector,
            matrix,
            matrix,
            vector,
            vector,
        ),
        check_vma=False,
    )
```

```python
import math

import jax
import jax.numpy as jnp
from jax import lax
from jax.experimental import pallas as pl
from jax.experimental.pallas import tpu as pltpu
from jax.sharding import Mesh
from jax.sharding import PartitionSpec as P

D = 1024
FF = 4096
HD = 64
PAIR = 2 * HD
STEP = 10
EPSILON = 1e-05
LEARN_RATE = 0.003
BF = jnp.bfloat16
F32 = jnp.float32
HALF = D // 2
BLOCK = 512
EXTRA = 16
QUARTERS = 4
PIECE = 3 * PAIR + EXTRA
MIB = 2**20


def rows_dot(operand, matrix):
    return lax.dot_general(operand, matrix, (((1,), (1,)), ((), ())), preferred_element_type=F32)


def cols_dot(operand, matrix):
    return lax.dot_general(operand, matrix, (((0,), (0,)), ((), ())), preferred_element_type=F32)


def plain_dot(operand, matrix):
    return lax.dot_general(operand, matrix, (((1,), (0,)), ((), ())), preferred_element_type=F32)


def swap(value):
    return lax.ppermute(value, "core", [(0, 1), (1, 0)])


def layer_norm(inputs, gain_vec, shift_vec):
    centre = jnp.mean(inputs, axis=-1, keepdims=True)
    shifted = inputs - centre
    inverse = lax.rsqrt(jnp.mean(shifted * shifted, axis=-1, keepdims=True) + EPSILON)
    normed = shifted * inverse
    return (normed * gain_vec + shift_vec, normed, inverse)


def norm_back(grad_out, normed, inverse, gain_vec):
    scaled = grad_out * gain_vec
    inner_term = (
        scaled
        - jnp.mean(scaled, axis=-1, keepdims=True)
        - normed * jnp.mean(scaled * normed, axis=-1, keepdims=True)
    )
    return (inverse * inner_term, jnp.sum(grad_out * normed, axis=0), jnp.sum(grad_out, axis=0))


def to_chips(blocks, z):
    count = lax.axis_size("z")
    parts = []
    for shift in range(count):
        part = lax.dynamic_index_in_dim(blocks, (z + shift) % count, 0, keepdims=False)
        if shift:
            part = lax.ppermute(part, "z", [(i, (i + shift) % count) for i in range(count)])
        parts.append(part)
    return jnp.concatenate(parts, axis=0)


def from_chips(rows, z):
    count = lax.axis_size("z")
    blocks = rows.reshape(count, -1, rows.shape[-1])
    result = blocks
    for shift in range(count):
        part = blocks[shift]
        if shift:
            part = lax.ppermute(part, "z", [(i, (i - shift) % count) for i in range(count)])
        result = lax.dynamic_update_index_in_dim(result, part, (z + shift) % count, 0)
    return result


def is_out_projection(z, core):
    return jnp.logical_and(z == 1, core == 0)


def gather_weights(weights, vectors, z, core):
    count = lax.axis_size("dp")
    rows = BLOCK // count
    low = weights.astype(BF)
    top = jnp.where(is_out_projection(z, core), low[:D].T, low[:D])
    vector = jnp.pad(vectors.astype(BF), (0, 2 * D - vectors.shape[0])).reshape(2, D)
    vector = jnp.pad(vector, ((0, EXTRA - 2), (0, 0)))
    other = swap(jnp.concatenate([top[BLOCK:], vector], axis=0))
    pair = jnp.stack([vector, other[BLOCK:]])
    pair = jnp.where(core == 0, pair, pair[::-1]).reshape(2, -1)[:, : vectors.shape[0]]
    pair = jnp.pad(pair.reshape(-1, D), ((0, EXTRA - 3), (0, 0)))
    start = lax.axis_index("dp") * rows
    if count > QUARTERS:
        spare = EXTRA * QUARTERS // count
        pair = lax.dynamic_slice_in_dim(pair, (start % PAIR) // rows * spare, spare, 0)
    first, last, middle = (
        lax.dynamic_slice_in_dim(item, start, rows, 0) for item in (top, low[D:], other)
    )
    piece = jnp.where(
        core == 0,
        jnp.concatenate([first, last, middle, pair], axis=0),
        jnp.concatenate([middle, first, last, pair], axis=0),
    )
    whole = lax.all_gather(piece, ("z", "dp"), axis=0, tiled=True)
    if count == QUARTERS:
        whole = whole.reshape(-1, PIECE, D)
    else:
        whole = whole.reshape(-1, count // QUARTERS, piece.shape[0], D)
        blocks = whole[:, :, : 3 * rows].reshape(-1, count // QUARTERS, 3, rows, D).swapaxes(1, 2)
        spare = whole[:, :, 3 * rows :].reshape(-1, EXTRA, D)
        whole = jnp.concatenate([blocks.reshape(-1, 3 * PAIR, D), spare], axis=1)
    found = whole.reshape(-1, QUARTERS, PIECE, D)[:, 0, 3 * PAIR : 3 * PAIR + 3]
    return whole, found.reshape(-1).astype(F32)


def sum_over_dp(grads):
    count = lax.axis_size("dp") // QUARTERS
    if count > 1:
        grads = grads.reshape(QUARTERS, -1, count, PAIR // count, D).swapaxes(1, 2)
    return lax.psum_scatter(grads.reshape(-1, D), "dp", scatter_dimension=0, tiled=True)


def by_hand():
    return lax.axis_size("dp") == 4 and lax.axis_size("z") == 4


def plus(first, second):
    return (first.astype(F32) + second.astype(F32)).astype(BF)


def across(bit, value):
    return lax.ppermute(value, "dp", [(i, i ^ bit) for i in range(4)])


def at(value, index, axis):
    return lax.dynamic_index_in_dim(value, index, axis, keepdims=False)


def reduce_late(late, sum_ff):
    d = lax.axis_index("dp")
    x, y = d % 2, d // 2
    late = late.reshape(2, 2, -1, D)
    a, b = late[..., :HALF], late[..., HALF:]
    got_a, got_b = across(1, at(a, 1 - x, 1)), across(2, at(b, 1 - y, 0))
    got_a, got_b, a, b, sum_ff = lax.optimization_barrier((got_a, got_b, a, b, sum_ff))
    a, b = at(a, x, 1), at(b, y, 0)
    far_a = across(2, plus(at(a, 1 - y, 0), at(got_a, 1 - y, 0)))
    far_b = across(1, plus(at(b, 1 - x, 0), at(got_b, 1 - x, 0)))
    far_a, far_b, a, b = lax.optimization_barrier((far_a, far_b, a, b))
    a = plus(plus(at(a, y, 0), at(got_a, y, 0)), far_a)
    b = plus(plus(at(b, x, 0), at(got_b, x, 0)), far_b)
    return jnp.concatenate([a, b], axis=-1), sum_ff


def gather_pieces(piece, grad_tokens):
    d = lax.axis_index("dp")
    a, b = piece[:, :HALF], piece[:, HALF:]
    pair = jnp.stack([a, b])
    got_x, got_y = across(1, pair), across(2, pair)
    got_x, got_y, pair = lax.optimization_barrier((got_x, got_y, pair))
    far_a, far_b = across(2, got_x[0]), across(1, got_y[1])
    far_a, far_b, pair, grad_tokens = lax.optimization_barrier((far_a, far_b, pair, grad_tokens))
    result = jnp.zeros((4, *piece.shape), BF)
    far = jnp.stack([far_a, far_b])
    for index, value in enumerate((pair, got_x, got_y, far)):
        for half in range(2):
            result = lax.dynamic_update_slice(
                result, value[half][None], (d ^ index, 0, half * HALF)
            )
    return result, grad_tokens


def lanes_of(shape, head):
    lane = lax.broadcasted_iota(jnp.int32, shape, 1)
    return (lane >= HD) if head else (lane < HD), lane - HD * (1 - head)


def split_three(value):
    high = value.astype(BF).astype(F32)
    mid = (value - high).astype(BF).astype(F32)
    return high, mid, (value - high - mid).astype(BF).astype(F32)


def spread_lanes(place, values):
    result = jnp.zeros(place.shape, F32)
    for lane, value in enumerate(values):
        result = jnp.where(place == lane, value, result)
    return result


def whole_block(shape):
    return pl.BlockSpec(shape, lambda *_: (0,) * len(shape))


SCALAR = pl.BlockSpec(memory_space=pltpu.SMEM)
NO_COST = pl.CostEstimate(flops=1, bytes_accessed=1, transcendentals=0)


def qkv_kernel(core_ref, x_ref, w_ref, vector_ref, out_ref):
    quarter = pl.program_id(0)
    row = core_ref[0] * QUARTERS + quarter
    bias_q = vector_ref[pl.ds(row, 1), :]
    bias_v = vector_ref[pl.ds(D // PAIR + row, 1), :]
    bias = jnp.concatenate([bias_q, jnp.zeros_like(bias_q), bias_v], axis=1)
    out_ref[...] = (rows_dot(x_ref[...], w_ref[0]) + bias).astype(BF)


def project(core, x, whole, vec):
    rows = x.shape[0]
    return pl.pallas_call(
        qkv_kernel,
        grid=(QUARTERS,),
        in_specs=[
            SCALAR,
            whole_block(x.shape),
            pl.BlockSpec((1, 3 * PAIR, D), lambda quarter: (quarter, 0, 0)),
            whole_block(vec.shape),
        ],
        out_specs=pl.BlockSpec((rows, 3 * PAIR), lambda quarter: (0, quarter)),
        out_shape=jax.ShapeDtypeStruct((rows, 3 * HALF), BF),
        cost_estimate=NO_COST,
        compiler_params=pltpu.CompilerParams(vmem_limit_bytes=40 * MIB),
    )(core, x, whole, vec)


def forward_kernel(q_ref, k_ref, v_ref, key_ref, o_ref, extra_ref):
    q, k, v, key_extra = q_ref[...], k_ref[...], v_ref[...], key_ref[...]
    outs, extras = [], []
    for head in range(2):
        in_q, place_q = lanes_of(q.shape, head)
        in_k, place_k = lanes_of(k.shape, head)
        keys = jnp.where(in_k, k, key_extra)
        queries = jnp.where(in_q, q * BF(0.125), jnp.where(place_q == 0, BF(1), BF(0)))
        values = jnp.where(in_k, v, jnp.where(place_k == 0, BF(1), BF(0)))
        scores = rows_dot(queries, keys)
        highest = jnp.max(scores, axis=1, keepdims=True)
        terms = jnp.exp(scores - highest).astype(BF)
        out = plain_dot(terms, values)
        column = HD * (1 - head)
        total = out[:, column : column + 1]
        outs.append(out * (1.0 / total))
        parts = split_three(-(highest + jnp.log(total)))
        extras.append(spread_lanes(place_q, (1.0, *parts)))
    in_first, _ = lanes_of(q.shape, 0)
    o_ref[...] = jnp.where(in_first, outs[0], outs[1]).astype(BF)
    extra_ref[...] = jnp.where(in_first, extras[1], extras[0]).astype(BF)


def attention_forward(merged, key_extra, step):
    rows = merged.shape[0]
    some = pl.BlockSpec((step, PAIR), lambda pair, part: (part, 3 * pair))
    ours = pl.BlockSpec((step, PAIR), lambda pair, part: (part, pair))
    keys = pl.BlockSpec((rows, PAIR), lambda pair, part: (0, 3 * pair + 1))
    values = pl.BlockSpec((rows, PAIR), lambda pair, part: (0, 3 * pair + 2))
    return pl.pallas_call(
        forward_kernel,
        grid=(HALF // PAIR, rows // step),
        in_specs=[some, keys, values, whole_block(key_extra.shape)],
        out_specs=[ours, ours],
        out_shape=[jax.ShapeDtypeStruct((rows, HALF), BF)] * 2,
        cost_estimate=NO_COST,
        compiler_params=pltpu.CompilerParams(vmem_limit_bytes=48 * MIB),
    )(merged, merged, merged, key_extra)


def backward_kernel(
    q_ref, extra_ref, k_ref, v_ref, key_ref, o_ref, do_ref, out_ref, dk_sum, dv_sum
):
    part = pl.program_id(1)
    q, extra, k, v = q_ref[...], extra_ref[...], k_ref[...], v_ref[...]
    key_extra, do = key_ref[...], do_ref[...]
    product = do.astype(F32) * o_ref[...].astype(F32)
    zero = BF(0)
    dq = dk = dv = 0.0
    for head in range(2):
        in_q, place_q = lanes_of(q.shape, head)
        in_k, place_k = lanes_of(k.shape, head)
        scaled = jnp.where(in_q, q * BF(0.125), zero)
        queries = jnp.where(in_q, scaled, extra)
        keys = jnp.where(in_k, k, key_extra)
        only_k = jnp.where(in_k, k, zero)
        only_do = jnp.where(in_q, do, zero)
        row_sum = jnp.sum(jnp.where(in_q, product, 0.0), axis=1, keepdims=True)
        grads = jnp.where(in_q, do, spread_lanes(place_q, split_three(-row_sum)).astype(BF))
        ones = jnp.where((place_k >= 0) & (place_k < 3), BF(1), zero)
        values = jnp.where(in_k, v, ones)
        probs = jnp.exp(rows_dot(keys, queries))
        grad_scores = (probs * rows_dot(values, grads)).astype(BF)
        dv = dv + plain_dot(probs.astype(BF), only_do)
        dk = dk + plain_dot(grad_scores, scaled)
        dq = dq + cols_dot(grad_scores, only_k)
    step = q.shape[0]
    out_ref[pl.ds(part * step, step), :PAIR] = (dq * 0.125).astype(BF)

    @pl.when(part == 0)
    def _():
        dk_sum[...] = dk
        dv_sum[...] = dv

    @pl.when(part > 0)
    def _():
        dk_sum[...] += dk
        dv_sum[...] += dv

    @pl.when(part == pl.num_programs(1) - 1)
    def _():
        out_ref[:, PAIR : 2 * PAIR] = dk_sum[...].astype(BF)
        out_ref[:, 2 * PAIR :] = dv_sum[...].astype(BF)


def attention_backward(merged, extra, key_extra, heads_out, grad_out, step):
    rows = merged.shape[0]
    some = pl.BlockSpec((step, PAIR), lambda pair, part: (part, 3 * pair))
    ours = pl.BlockSpec((step, PAIR), lambda pair, part: (part, pair))
    keys = pl.BlockSpec((rows, PAIR), lambda pair, part: (0, 3 * pair + 1))
    values = pl.BlockSpec((rows, PAIR), lambda pair, part: (0, 3 * pair + 2))
    return pl.pallas_call(
        backward_kernel,
        grid=(HALF // PAIR, rows // step),
        in_specs=[some, ours, keys, values, whole_block(key_extra.shape), ours, ours],
        out_specs=pl.BlockSpec((rows, 3 * PAIR), lambda pair, part: (0, pair)),
        out_shape=jax.ShapeDtypeStruct((rows, 3 * HALF), BF),
        scratch_shapes=[pltpu.VMEM((rows, PAIR), F32)] * 2,
        cost_estimate=NO_COST,
        compiler_params=pltpu.CompilerParams(vmem_limit_bytes=56 * MIB),
    )(merged, extra, merged, merged, key_extra, heads_out, grad_out)


def key_lanes(allowed):
    lane = jnp.arange(PAIR)[None, :] % HD
    bias = jnp.where(allowed, 0.0, -1e30)[:, None]
    return jnp.where(lane == 0, bias, jnp.where(lane < 4, 1.0, 0.0)).astype(BF)


def weight_block(chip, part, count=1):
    return pl.BlockSpec(
        (1, count * PAIR, D), lambda quarter: (chip * QUARTERS + quarter, part // count, 0)
    )


UP_BLOCKS = (weight_block(1, 1), weight_block(1, 2), weight_block(2, 0, 2))
DOWN_BLOCKS = (weight_block(2, 2), weight_block(3, 0, 3))


def joined(refs):
    return jnp.concatenate([ref[0] for ref in refs], axis=0)


def feed_forward_kernel(
    core_ref, u_ref, up0, up1, up2, down0, down1, vector_ref,
    hidden_ref, slope_ref, mine_ref, other_ref, total,
):
    quarter = pl.program_id(0)
    rows = [
        vector_ref[pl.ds(3 * D // PAIR + (2 * n + core_ref[0]) * QUARTERS + quarter, 1), :]
        for n in range(4)
    ]
    z = rows_dot(u_ref[...], joined((up0, up1, up2))) + jnp.concatenate(rows, axis=1)
    cdf = 0.5 * (1.0 + lax.erf(z * (1.0 / math.sqrt(2.0))))
    slope = cdf + z * jnp.exp(-0.5 * z * z) * (1.0 / math.sqrt(2.0 * math.pi))
    hidden = (z * cdf).astype(BF)
    hidden_ref[...] = hidden
    slope_ref[...] = slope.astype(BF)
    part = plain_dot(hidden, joined((down0, down1)))

    @pl.when(quarter == 0)
    def _():
        total[...] = part

    @pl.when(quarter > 0)
    def _():
        total[...] += part

    @pl.when(quarter == QUARTERS - 1)
    def _():
        half = mine_ref.shape[0]
        mine_ref[...] = total[:half]
        other_ref[...] = total[half:].astype(BF)


def feed_forward(core, u, whole, vec):
    rows = u.shape[0]
    columns = pl.BlockSpec((rows, BLOCK), lambda quarter: (0, quarter))
    half = (rows // 2, D)
    return pl.pallas_call(
        feed_forward_kernel,
        grid=(QUARTERS,),
        in_specs=[SCALAR, whole_block(u.shape), *UP_BLOCKS, *DOWN_BLOCKS, whole_block(vec.shape)],
        out_specs=[columns, columns, whole_block(half), whole_block(half)],
        out_shape=[
            jax.ShapeDtypeStruct((rows, FF // 2), BF),
            jax.ShapeDtypeStruct((rows, FF // 2), BF),
            jax.ShapeDtypeStruct(half, F32),
            jax.ShapeDtypeStruct(half, BF),
        ],
        scratch_shapes=[pltpu.VMEM((rows, D), F32)],
        cost_estimate=NO_COST,
        compiler_params=pltpu.CompilerParams(vmem_limit_bytes=56 * MIB),
    )(core, u, whole, whole, whole, whole, whole, vec)


def feed_backward_kernel(
    df_ref, u_ref, hidden_ref, slope_ref, up0, up1, up2, down0, down1,
    grads_ref, bias_ref, mine_ref, other_ref, total,
):
    quarter = pl.program_id(0)
    df = df_ref[...]
    dz32 = rows_dot(df, joined((down0, down1))) * slope_ref[...].astype(F32)
    dz = dz32.astype(BF)
    bias_ref[...] = jnp.sum(dz.astype(F32), axis=0, keepdims=True)
    grads_ref[0, :BLOCK] = cols_dot(dz, u_ref[...]).astype(BF)
    grads_ref[0, BLOCK:] = cols_dot(hidden_ref[...], df).astype(BF)
    part = plain_dot(dz, joined((up0, up1, up2)))

    @pl.when(quarter == 0)
    def _():
        total[...] = part

    @pl.when(quarter > 0)
    def _():
        total[...] += part

    @pl.when(quarter == QUARTERS - 1)
    def _():
        half = mine_ref.shape[0]
        mine_ref[...] = total[:half]
        other_ref[...] = total[half:].astype(BF)


def feed_backward(df, u, hidden, slope, whole):
    rows = u.shape[0]
    columns = pl.BlockSpec((rows, BLOCK), lambda quarter: (0, quarter))
    half = (rows // 2, D)
    return pl.pallas_call(
        feed_backward_kernel,
        grid=(QUARTERS,),
        in_specs=[
            whole_block(df.shape), whole_block(u.shape), columns, columns, *UP_BLOCKS, *DOWN_BLOCKS
        ],
        out_specs=[
            pl.BlockSpec((1, 2 * BLOCK, D), lambda quarter: (quarter, 0, 0)),
            pl.BlockSpec((1, BLOCK), lambda quarter: (0, quarter)),
            whole_block(half),
            whole_block(half),
        ],
        out_shape=[
            jax.ShapeDtypeStruct((QUARTERS, 2 * BLOCK, D), BF),
            jax.ShapeDtypeStruct((1, FF // 2), F32),
            jax.ShapeDtypeStruct(half, F32),
            jax.ShapeDtypeStruct(half, BF),
        ],
        scratch_shapes=[pltpu.VMEM((rows, D), F32)],
        cost_estimate=NO_COST,
        compiler_params=pltpu.CompilerParams(vmem_limit_bytes=60 * MIB),
    )(df, u, hidden, slope, whole, whole, whole, whole, whole)


def adamw_update(parameter, gradient, first_old, second_old, decay_rate):
    step_float = float(STEP)
    first_new = 0.9 * first_old + 0.1 * gradient
    second_new = 0.999 * second_old + 0.001 * gradient * gradient
    first_fix = first_new / (1.0 - 0.9**step_float)
    second_fix = second_new / (1.0 - 0.999**step_float)
    update = first_fix / (jnp.sqrt(second_fix) + 1e-08)
    return (-LEARN_RATE * (update + decay_rate * parameter), first_new, second_new)


def share(partial):
    half = partial.shape[0] // 2
    return partial[:half] + swap(partial[half:].astype(BF)).astype(F32)


def both(rows):
    return jnp.concatenate([rows, swap(rows)], axis=0)


def spread_part(vector, core, pieces):
    parts = vector.reshape(pieces, 1, -1)
    mine = (jnp.arange(2) == core)[None, :, None]
    return jnp.where(mine, parts, 0.0).reshape(-1)


def shards(
    tokens,
    cotangent,
    lengths,
    weights,
    vectors,
    first_weights,
    second_weights,
    first_vectors,
    second_vectors,
):
    z, core = lax.axis_index("z"), lax.axis_index("core")
    count, dp_count = lax.axis_size("z"), lax.axis_size("dp")
    per_device = tokens.shape[1]
    rows = count * per_device
    length = lengths[z]
    block = jnp.arange(count, dtype=jnp.int32)[:, None]
    inner = jnp.arange(per_device, dtype=jnp.int32)[None, :]
    chip_of = (z - block) % count
    here = ((chip_of * 2 + core) * per_device + inner).reshape(rows)
    there = ((chip_of * 2 + 1 - core) * per_device + inner).reshape(rows)
    key_extra = key_lanes(jnp.concatenate([here, there]) < length)
    live = (here < length).astype(F32)[:, None]
    core_id = core.astype(jnp.int32).reshape(1)

    whole, vec = gather_weights(weights, vectors, z, core)
    x_mine = to_chips(tokens, z)
    x = both(x_mine)
    whole, x, x_mine, cotangent = lax.optimization_barrier((whole, x, x_mine, cotangent))
    grad_out = to_chips(cotangent, z)
    bounds = [0, D, 2 * D, 3 * D, 3 * D + FF] + [(n + 4) * D + FF for n in range(6)]
    _, _, bias_o, _, bias_down, gain_one, shift_one, gain_two, shift_two = (
        vec[bounds[n] : bounds[n + 1]] for n in range(9)
    )
    vec = vec.reshape(-1, PAIR)
    w_out = whole[QUARTERS : 2 * QUARTERS, :PAIR].reshape(HALF, D)

    merged = project(core_id, x, whole, vec)
    heads_out, extra = attention_forward(merged, key_extra, 2 * rows)
    heads_out, extra, grad_out = lax.optimization_barrier((heads_out, extra, grad_out))
    normed_in, normed_one, inverse_one = layer_norm(
        x_mine.astype(F32) + share(plain_dot(heads_out, w_out)) + bias_o, gain_one, shift_one
    )
    u_mine = normed_in.astype(BF)
    u = both(u_mine)
    hidden, slope, feed, feed_other = feed_forward(core_id, u, whole, vec)
    feed = feed + swap(feed_other).astype(F32) + bias_down
    result, normed_two, inverse_two = layer_norm(u_mine.astype(F32) + feed, gain_two, shift_two)
    layer_out = result.astype(BF)

    grad_out = grad_out.astype(F32) * live
    grad_two, grad_gain_two, grad_shift_two = norm_back(grad_out, normed_two, inverse_two, gain_two)
    df_mine = grad_two.astype(BF)
    grad_bias_down = jnp.sum(df_mine.astype(F32), axis=0)
    grads_ff, grad_bias_up, du, du_other = feed_backward(both(df_mine), u, hidden, slope, whole)
    sum_ff = sum_over_dp(grads_ff)
    du = du + swap(du_other).astype(F32) + grad_two
    grad_one, grad_gain_one, grad_shift_one = norm_back(du, normed_one, inverse_one, gain_one)
    da_mine = grad_one.astype(BF)
    da = both(da_mine)
    grad_bias_o = jnp.sum(da_mine.astype(F32), axis=0)
    do = rows_dot(da, w_out).astype(BF)
    grad_wo = cols_dot(heads_out, da).astype(BF)
    do, layer_out = lax.optimization_barrier((do, layer_out))
    layer_out = from_chips(layer_out, z)
    d_merged = attention_backward(merged, extra, key_extra, heads_out, do, rows)
    d_merged, layer_out = lax.optimization_barrier((d_merged, layer_out))
    grad_rows = share(plain_dot(d_merged, whole[:QUARTERS, : 3 * PAIR].reshape(-1, D))) + grad_one
    grad_rows = grad_rows.astype(BF)
    grad_qkv = cols_dot(d_merged, x).astype(BF)
    sums = jnp.sum(d_merged.astype(F32), axis=0).reshape(QUARTERS, 3, PAIR)
    vector_grad = jnp.concatenate(
        [
            spread_part(sums[:, 0], core, 1),
            spread_part(sums[:, 2], core, 1),
            grad_bias_o,
            spread_part(grad_bias_up.reshape(QUARTERS, 4, PAIR).swapaxes(0, 1), core, 4),
            grad_bias_down,
            grad_gain_one,
            grad_shift_one,
            grad_gain_two,
            grad_shift_two,
        ]
    ).astype(BF)
    shares = vector_grad.reshape(count, dp_count, -1).swapaxes(0, 1)
    if by_hand():
        shares = shares.reshape(dp_count, -1, D)
        shares = jnp.pad(shares, ((0, 0), (0, EXTRA - shares.shape[1]), (0, 0)))
    else:
        shares = jnp.pad(shares, ((0, 0), (0, 0), (0, EXTRA * D - shares.shape[2])))
        shares = shares.reshape(dp_count, count * EXTRA, D)
    run = PAIR * QUARTERS // dp_count
    late = jnp.concatenate(
        [
            jnp.concatenate(
                [grad_qkv.reshape(QUARTERS, 3 * PAIR, D), grad_wo.reshape(QUARTERS, PAIR, D)], axis=1
            )
            .reshape(QUARTERS, 4, dp_count // QUARTERS, run, D)
            .swapaxes(1, 2)
            .reshape(dp_count, 4 * run, D),
            shares,
        ],
        axis=1,
    )
    if by_hand():
        late, sum_ff = reduce_late(late, sum_ff)
        slab = late[4 * PAIR :]
        chips = [late[: 3 * PAIR], slab, late[3 * PAIR : 4 * PAIR], sum_ff[: 2 * PAIR], slab]
        chips += [sum_ff[2 * PAIR : 5 * PAIR], slab, sum_ff[5 * PAIR :], slab]
        piece = lax.psum_scatter(
            jnp.concatenate(chips, axis=0), "z", scatter_dimension=0, tiled=True
        )
        piece, grad_rows = lax.optimization_barrier((piece, grad_rows))
        summed, grad_tokens = gather_pieces(piece, from_chips(grad_rows, z))
    else:
        grad_tokens = from_chips(grad_rows, z)
        sum_late = lax.psum_scatter(late.reshape(-1, D), "dp", scatter_dimension=0, tiled=True)
        parts = [sum_late[n * run : (n + 1) * run] for n in range(4)]
        parts += [sum_ff[n * run : (n + 1) * run] for n in range(8)]
        spare = sum_late[4 * run :].reshape(count, EXTRA, D)
        chips = [
            jnp.concatenate([*parts[3 * chip : 3 * chip + 3], spare[chip]], axis=0)
            for chip in range(count)
        ]
        piece = lax.psum_scatter(
            jnp.concatenate(chips, axis=0), "z", scatter_dimension=0, tiled=True
        )
        summed = lax.all_gather(piece, "dp", axis=0, tiled=True).reshape(dp_count, -1, D)
    blocks = summed[:, : 3 * run].reshape(dp_count, 3, run, D).swapaxes(0, 1).reshape(3, BLOCK, D)
    share_size = vectors.shape[0] * 2 // dp_count
    vector_sum = summed[:, 3 * run :].reshape(dp_count, -1)
    start = z * share_size if by_hand() else 0
    vector_sum = lax.dynamic_slice_in_dim(vector_sum, start, share_size, 1)
    vector_sum = vector_sum.reshape(2, -1).astype(F32)
    vector_sum = jnp.pad(vector_sum, ((0, 0), (0, 2 * D - vector_sum.shape[1])))
    shard_v = vector_sum[core] + swap(vector_sum[1 - core])
    shard_v = shard_v[: vectors.shape[0]]
    a, b, c = blocks
    middle = swap(jnp.where(core == 0, c, a))
    top = jnp.concatenate([jnp.where(core == 0, a, b), middle], axis=0)
    top = jnp.where(is_out_projection(z, core), top.T, top)
    shard_w = jnp.concatenate([top, jnp.where(core == 0, b, c)], axis=0).astype(F32)

    weight_change, new_first_weights, new_second_weights = adamw_update(
        weights, shard_w, first_weights, second_weights, 0.01
    )
    vector_change, new_first_vectors, new_second_vectors = adamw_update(
        vectors, shard_v, first_vectors, second_vectors, 0.0
    )
    return (
        layer_out,
        grad_tokens,
        shard_w,
        shard_v,
        weight_change,
        vector_change,
        new_first_weights,
        new_second_weights,
        new_first_vectors,
        new_second_vectors,
    )


def solution(mesh):
    chips = Mesh(
        mesh.devices.reshape(mesh.shape["dp"], mesh.shape["ctx"] // 2, 2), ("dp", "z", "core")
    )
    ctx = ("z", "core")
    activations, matrix, vector = P("dp", ctx, None), P(ctx, None), P(ctx)
    return jax.shard_map(
        shards,
        mesh=chips,
        in_specs=(activations, activations, P("dp"), matrix, vector, matrix, matrix, vector, vector),
        out_specs=(
            activations,
            activations,
            matrix,
            vector,
            matrix,
            vector,
            matrix,
            matrix,
            vector,
            vector,
        ),
        check_vma=False,
    )
```

```python
import math

import jax
import jax.numpy as jnp
from jax import lax
from jax.experimental import pallas as pl
from jax.experimental.pallas import tpu as pltpu
from jax.sharding import Mesh
from jax.sharding import PartitionSpec as P

D = 1024
FF = 4096
HD = 64
PAIR = 2 * HD
STEP = 10
EPSILON = 1e-05
LEARN_RATE = 0.003
BF = jnp.bfloat16
F32 = jnp.float32
HALF = D // 2
BLOCK = 512
EXTRA = 16
QUARTERS = 4
PIECE = 3 * PAIR + EXTRA
VMEM = 60 * 2**20
SCALAR = pl.BlockSpec(memory_space=pltpu.SMEM)
NO_COST = pl.CostEstimate(flops=1, bytes_accessed=1, transcendentals=0)


def rows_dot(operand, matrix):
    return lax.dot_general(operand, matrix, (((1,), (1,)), ((), ())), preferred_element_type=F32)


def cols_dot(operand, matrix):
    return lax.dot_general(operand, matrix, (((0,), (0,)), ((), ())), preferred_element_type=F32)


def plain_dot(operand, matrix):
    return lax.dot_general(operand, matrix, (((1,), (0,)), ((), ())), preferred_element_type=F32)


def swap(value):
    return lax.ppermute(value, "core", [(0, 1), (1, 0)])


def layer_norm(inputs, gain_vec, shift_vec):
    centre = jnp.mean(inputs, axis=-1, keepdims=True)
    shifted = inputs - centre
    inverse = lax.rsqrt(jnp.mean(shifted * shifted, axis=-1, keepdims=True) + EPSILON)
    normed = shifted * inverse
    return (normed * gain_vec + shift_vec, normed, inverse)


def norm_back(grad_out, normed, inverse, gain_vec):
    scaled = grad_out * gain_vec
    inner_term = (
        scaled
        - jnp.mean(scaled, axis=-1, keepdims=True)
        - normed * jnp.mean(scaled * normed, axis=-1, keepdims=True)
    )
    return (inverse * inner_term, jnp.sum(grad_out * normed, axis=0), jnp.sum(grad_out, axis=0))


def to_chip(blocks, z, shift):
    count = lax.axis_size("z")
    part = lax.dynamic_index_in_dim(blocks, (z + shift) % count, 0, keepdims=False)
    if shift:
        part = lax.ppermute(part, "z", [(i, (i + shift) % count) for i in range(count)])
    return part


def to_chips(blocks, z):
    return jnp.concatenate([to_chip(blocks, z, n) for n in range(lax.axis_size("z"))], axis=0)


def from_chips(rows, z):
    count = lax.axis_size("z")
    blocks = rows.reshape(count, -1, rows.shape[-1])
    result = blocks
    for shift in range(count):
        part = blocks[shift]
        if shift:
            part = lax.ppermute(part, "z", [(i, (i - shift) % count) for i in range(count)])
        result = lax.dynamic_update_index_in_dim(result, part, (z + shift) % count, 0)
    return result


def is_out_projection(z, core):
    return jnp.logical_and(z == 1, core == 0)


def pack_kernel(flag_ref, rows_ref, columns_ref, outer_ref, middle_ref):
    step = pl.program_id(0)
    turned = jnp.logical_and(flag_ref[0] == 1, step < 2)

    def write(value):
        @pl.when(step != 1)
        def _():
            outer_ref[...] = value

        @pl.when(step == 1)
        def _():
            middle_ref[...] = value

    @pl.when(turned)
    def _():
        write(columns_ref[...].T.astype(BF))

    @pl.when(jnp.logical_not(turned))
    def _():
        write(rows_ref[...].astype(BF))


def pack_weights(weights, flag):
    return pl.pallas_call(
        pack_kernel,
        grid_spec=pltpu.PrefetchScalarGridSpec(
            num_scalar_prefetch=1,
            grid=(3,),
            in_specs=[
                pl.BlockSpec((BLOCK, D), lambda n, flag: (n, 0)),
                pl.BlockSpec((D, BLOCK), lambda n, flag: (0, jnp.minimum(n, 1) * flag[0])),
            ],
            out_specs=[
                pl.BlockSpec((BLOCK, D), lambda n, flag: (n // 2, 0)),
                pl.BlockSpec((BLOCK, D), lambda n, flag: (0, 0)),
            ],
        ),
        out_shape=[
            jax.ShapeDtypeStruct((2 * BLOCK, D), BF),
            jax.ShapeDtypeStruct((BLOCK, D), BF),
        ],
        cost_estimate=NO_COST,
        compiler_params=pltpu.CompilerParams(vmem_limit_bytes=VMEM),
    )(flag.astype(jnp.int32).reshape(1), weights, weights)


def own_kernel(
    where_ref, first_ref, last_ref, other_ref, mine_vector, other_vector, whole_ref, piece_ref
):
    core = where_ref[2]

    def write(parts, vectors):
        value = jnp.concatenate([*parts, *vectors], axis=0)
        whole_ref[0] = value

        @pl.when(pl.program_id(0) == 0)
        def _():
            piece_ref[...] = value

    first, last, other = first_ref[...], last_ref[...], other_ref[...]
    vectors = [mine_vector[...], other_vector[...]]

    @pl.when(core == 0)
    def _():
        write([first, last, other], vectors)

    @pl.when(core == 1)
    def _():
        write([other, first, last], vectors[::-1])


def own_pieces(outer, other, vector, other_vector, z, core):
    where = jnp.stack([z, lax.axis_index("dp") % QUARTERS, core]).astype(jnp.int32)
    run = (PAIR, D)
    small = pl.BlockSpec(vector.shape, lambda n, where: (0, 0))
    return pl.pallas_call(
        own_kernel,
        grid_spec=pltpu.PrefetchScalarGridSpec(
            num_scalar_prefetch=1,
            grid=(QUARTERS,),
            in_specs=[
                pl.BlockSpec(run, lambda n, where: (where[1] ^ n, 0)),
                pl.BlockSpec(run, lambda n, where: (QUARTERS + (where[1] ^ n), 0)),
                pl.BlockSpec(run, lambda n, where: (where[1] ^ n, 0)),
                small,
                small,
            ],
            out_specs=[
                pl.BlockSpec(
                    (1, PIECE, D), lambda n, where: (where[0] * QUARTERS + (where[1] ^ n), 0, 0)
                ),
                pl.BlockSpec((PIECE, D), lambda n, where: (0, 0)),
            ],
        ),
        out_shape=[
            jax.ShapeDtypeStruct((4 * QUARTERS, PIECE, D), BF),
            jax.ShapeDtypeStruct((PIECE, D), BF),
        ],
        cost_estimate=NO_COST,
        compiler_params=pltpu.CompilerParams(vmem_limit_bytes=VMEM),
    )(where, outer, outer, other, vector, other_vector)


def gather_pieces_of_all(whole, z):
    count = lax.axis_size("dp") // QUARTERS
    mine = lax.dynamic_slice_in_dim(whole, z * QUARTERS, QUARTERS, 0)
    share = lax.dynamic_index_in_dim(mine, lax.axis_index("dp") // count, 0, keepdims=False)
    blocks = share[: 3 * PAIR].reshape(3, PAIR, D)
    blocks = lax.dynamic_slice_in_dim(
        blocks, lax.axis_index("dp") % count * (PAIR // count), PAIR // count, 1
    )
    everything = lax.all_gather(blocks.reshape(-1, D), ("z", "dp"), axis=0, tiled=True)
    everything = everything.reshape(-1, count, 3, PAIR // count, D).swapaxes(1, 2)
    spare = lax.all_gather(share[3 * PAIR :], "z", axis=0, tiled=True).reshape(-1, 1, EXTRA, D)
    spare = jnp.broadcast_to(spare, (spare.shape[0], QUARTERS, EXTRA, D)).reshape(-1, EXTRA, D)
    return jnp.concatenate([everything.reshape(-1, 3 * PAIR, D), spare], axis=1)


def vectors_of(whole, size):
    found = whole.reshape(-1, QUARTERS, PIECE, D)[:, 0, 3 * PAIR :]
    found = found.reshape(-1, 2, EXTRA * D // 2)[:, :, :size]
    return found.reshape(-1).astype(F32)


def place_kernel(where_ref, whole_in, mine, got_x, got_y, far_a, far_b, whole_ref):
    del where_ref, whole_in
    for index, source in enumerate((mine, got_x, got_y)):

        @pl.when(pl.program_id(0) == index)
        def _(source=source):
            whole_ref[0] = source[...]

    @pl.when(pl.program_id(0) == 3)
    def _():
        whole_ref[0, :, :HALF] = far_a[...]
        whole_ref[0, :, HALF:] = far_b[...]


def place(whole, shard, values):
    where = jnp.stack([shard, lax.axis_index("dp")]).astype(jnp.int32)
    return pl.pallas_call(
        place_kernel,
        grid_spec=pltpu.PrefetchScalarGridSpec(
            num_scalar_prefetch=1,
            grid=(4,),
            in_specs=[pl.BlockSpec(memory_space=pl.ANY)]
            + [pl.BlockSpec(value.shape, lambda n, where: (0, 0)) for value in values],
            out_specs=pl.BlockSpec(
                (1, PIECE, D), lambda n, where: (where[0] * QUARTERS + (where[1] ^ n), 0, 0)
            ),
        ),
        out_shape=jax.ShapeDtypeStruct(whole.shape, BF),
        input_output_aliases={1: 0},
        cost_estimate=NO_COST,
        compiler_params=pltpu.CompilerParams(vmem_limit_bytes=VMEM),
    )(where, whole, *values)


def sum_over_dp(grads):
    count = lax.axis_size("dp") // QUARTERS
    if count > 1:
        grads = grads.reshape(QUARTERS, -1, count, PAIR // count, D).swapaxes(1, 2)
    return lax.psum_scatter(grads.reshape(-1, D), "dp", scatter_dimension=0, tiled=True)


def by_hand():
    return lax.axis_size("dp") == 4 and lax.axis_size("z") == 4


def plus(first, second):
    return (first.astype(F32) + second.astype(F32)).astype(BF)


def across(bit, value):
    return lax.ppermute(value, "dp", [(i, i ^ bit) for i in range(4)])


def at(value, index, axis):
    return lax.dynamic_index_in_dim(value, index, axis, keepdims=False)


def along_z(value, pairs):
    return lax.ppermute(value, "z", pairs)


def pick(z, values):
    result = values[-1]
    for index in range(len(values) - 2, -1, -1):
        result = jnp.where(z == index, values[index], result)
    return result


def wait(*values):
    return lax.optimization_barrier(values)


def reduce_late(late, sum_ff, grad_tokens):
    d = lax.axis_index("dp")
    x, y = d % 2, d // 2
    late = late.reshape(2, 2, -1, D)
    a, b = late[..., :HALF], late[..., HALF:]
    got_a, got_b = across(1, at(a, 1 - x, 1)), across(2, at(b, 1 - y, 0))
    got_a, got_b, a, b, sum_ff, grad_tokens = wait(got_a, got_b, a, b, sum_ff, grad_tokens)
    a, b = at(a, x, 1), at(b, y, 0)
    far_a = across(2, plus(at(a, 1 - y, 0), at(got_a, 1 - y, 0)))
    far_b = across(1, plus(at(b, 1 - x, 0), at(got_b, 1 - x, 0)))
    far_a, far_b, a, b = lax.optimization_barrier((far_a, far_b, a, b))
    a = plus(plus(at(a, y, 0), at(got_a, y, 0)), far_a)
    b = plus(plus(at(b, x, 0), at(got_b, x, 0)), far_b)
    return jnp.concatenate([a, b], axis=-1), sum_ff, grad_tokens


def gather_pieces(piece):
    got = across(1, piece), across(2, piece)
    got, piece = wait(got, piece)
    far = across(2, got[0][:, :HALF]), across(1, got[1][:, HALF:])
    far, got, piece = wait(far, got, piece)
    return (piece, *got, *far)


def update_kernel(
    where_ref, mine, got_x, got_y, far_a, far_b, middle_ref, weight_ref, first_ref, second_ref,
    grad_ref, change_ref, first_out, second_out,
):
    d, core, turned = where_ref[0], where_ref[1], where_ref[2] == 1
    block, pair = pl.program_id(0), pl.program_id(1)
    pieces = (mine, got_x, got_y)
    rows = pl.ds(pl.multiple_of((core + block // 2) * PAIR, PAIR), PAIR)
    plain = jnp.logical_and(block != 1, jnp.logical_or(block == 2, jnp.logical_not(turned)))
    for n in range(QUARTERS):
        slot = pl.ds(pl.multiple_of((d % 2 ^ (n % 2)) * PAIR, PAIR), PAIR)
        ours = pair == n // 2

        @pl.when(ours & (block == 1) & jnp.logical_not(turned))
        def _(n=n, slot=slot):
            grad_ref[slot, :] = middle_ref[n].astype(F32)

        @pl.when(ours & plain)
        def _(n=n, slot=slot):
            if n < 3:
                grad_ref[slot, :] = pieces[n][rows, :].astype(F32)
            else:
                grad_ref[slot, :HALF] = far_a[rows, :].astype(F32)
                grad_ref[slot, HALF:] = far_b[rows, :].astype(F32)

        @pl.when(ours & (block < 2) & turned)
        def _(n=n, slot=slot):
            start = pl.multiple_of((d ^ n) * PAIR, PAIR)
            columns = pl.ds(pl.multiple_of(block * HALF + start, PAIR), PAIR)
            for m in range(QUARTERS):
                low = pl.ds(pl.multiple_of((d ^ m) * PAIR, PAIR), PAIR)
                high = pl.ds(pl.multiple_of(HALF + (d ^ m) * PAIR, PAIR), PAIR)
                grad_ref[slot, high] = middle_ref[m, :, columns].astype(F32).T
                if m < 3:
                    grad_ref[slot, low] = pieces[m][:PAIR, columns].astype(F32).T
            low = pl.ds(pl.multiple_of((d ^ 3) * PAIR, PAIR), PAIR)
            for half, far in enumerate((far_a, far_b)):

                @pl.when(block == half)
                def _(far=far):
                    grad_ref[slot, low] = far[:PAIR, pl.ds(start, PAIR)].astype(F32).T

    change_ref[...], first_out[...], second_out[...] = adamw_update(
        weight_ref[...], grad_ref[...], first_ref[...], second_ref[...], 0.01
    )


def update_weights(values, middle, weights, first_weights, second_weights, turned, core):
    d = lax.axis_index("dp")
    where = jnp.stack([d, core, turned.astype(jnp.int32)]).astype(jnp.int32)
    rows = pl.BlockSpec((2 * PAIR, D), lambda b, n, where: (b * 2 + (where[0] // 2 ^ n), 0))
    return pl.pallas_call(
        update_kernel,
        grid_spec=pltpu.PrefetchScalarGridSpec(
            num_scalar_prefetch=1,
            grid=(3, 2),
            in_specs=[pl.BlockSpec(value.shape, lambda b, n, where: (0, 0)) for value in values]
            + [pl.BlockSpec(middle.shape, lambda b, n, where: (0, 0, 0))]
            + [rows] * 3,
            out_specs=[rows] * 4,
        ),
        out_shape=[jax.ShapeDtypeStruct(weights.shape, F32)] * 4,
        cost_estimate=NO_COST,
        compiler_params=pltpu.CompilerParams(vmem_limit_bytes=VMEM),
    )(where, *values, middle, weights, first_weights, second_weights)


def lanes_of(shape, head):
    lane = lax.broadcasted_iota(jnp.int32, shape, 1)
    return (lane >= HD) if head else (lane < HD), lane - HD * (1 - head)


def split_three(value):
    high = value.astype(BF).astype(F32)
    mid = (value - high).astype(BF).astype(F32)
    return high, mid, (value - high - mid).astype(BF).astype(F32)


def spread_lanes(place, values):
    result = jnp.zeros(place.shape, F32)
    for lane, value in enumerate(values):
        result = jnp.where(place == lane, value, result)
    return result


def whole_block(shape):
    return pl.BlockSpec(shape, lambda *_: (0,) * len(shape))


def qkv_kernel(core_ref, x_ref, w_ref, vector_ref, out_ref):
    quarter = pl.program_id(0)
    row = core_ref[0] * QUARTERS + quarter
    bias_q = vector_ref[pl.ds(row, 1), :]
    bias_v = vector_ref[pl.ds(D // PAIR + row, 1), :]
    bias = jnp.concatenate([bias_q, jnp.zeros_like(bias_q), bias_v], axis=1)
    out_ref[...] = (rows_dot(x_ref[...], w_ref[0]) + bias).astype(BF)


def project(core, x, whole, vec):
    rows = x.shape[0]
    return pl.pallas_call(
        qkv_kernel,
        grid=(QUARTERS,),
        in_specs=[
            SCALAR,
            whole_block(x.shape),
            pl.BlockSpec((1, 3 * PAIR, D), lambda quarter: (quarter, 0, 0)),
            whole_block(vec.shape),
        ],
        out_specs=pl.BlockSpec((rows, 3 * PAIR), lambda quarter: (0, quarter)),
        out_shape=jax.ShapeDtypeStruct((rows, 3 * HALF), BF),
        cost_estimate=NO_COST,
        compiler_params=pltpu.CompilerParams(vmem_limit_bytes=VMEM),
    )(core, x, whole, vec)


def forward_kernel(q_ref, k_ref, v_ref, key_ref, o_ref, extra_ref):
    q, k, v, key_extra = q_ref[...], k_ref[...], v_ref[...], key_ref[...]
    outs, extras = [], []
    for head in range(2):
        in_q, place_q = lanes_of(q.shape, head)
        in_k, place_k = lanes_of(k.shape, head)
        keys = jnp.where(in_k, k, key_extra)
        queries = jnp.where(in_q, q * BF(0.125), jnp.where(place_q == 0, BF(1), BF(0)))
        values = jnp.where(in_k, v, jnp.where(place_k == 0, BF(1), BF(0)))
        scores = rows_dot(queries, keys)
        highest = jnp.max(scores, axis=1, keepdims=True)
        terms = jnp.exp(scores - highest).astype(BF)
        out = plain_dot(terms, values)
        column = HD * (1 - head)
        total = out[:, column : column + 1]
        outs.append(out * (1.0 / total))
        parts = split_three(-(highest + jnp.log(total)))
        extras.append(spread_lanes(place_q, (1.0, *parts)))
    in_first, _ = lanes_of(q.shape, 0)
    o_ref[...] = jnp.where(in_first, outs[0], outs[1]).astype(BF)
    extra_ref[...] = jnp.where(in_first, extras[1], extras[0]).astype(BF)


def forward_more_kernel(q_ref, k_ref, v_ref, key_ref, o_in, extra_in, o_ref, extra_ref):
    del o_in, extra_in
    forward_kernel(q_ref, k_ref, v_ref, key_ref, o_ref, extra_ref)


def attention_forward(merged, key_extra, step, start, pairs, done=()):
    rows = merged.shape[0]
    some = pl.BlockSpec((step, PAIR), lambda pair, part: (part, 3 * (pair + start)))
    ours = pl.BlockSpec((step, PAIR), lambda pair, part: (part, pair + start))
    keys = pl.BlockSpec((rows, PAIR), lambda pair, part: (0, 3 * (pair + start) + 1))
    values = pl.BlockSpec((rows, PAIR), lambda pair, part: (0, 3 * (pair + start) + 2))
    return pl.pallas_call(
        forward_more_kernel if done else forward_kernel,
        grid=(pairs, rows // step),
        in_specs=[some, keys, values, whole_block(key_extra.shape)]
        + [pl.BlockSpec(memory_space=pl.ANY)] * len(done),
        out_specs=[ours, ours],
        out_shape=[jax.ShapeDtypeStruct((rows, HALF), BF)] * 2,
        input_output_aliases={4: 0, 5: 1} if done else {},
        cost_estimate=NO_COST,
        compiler_params=pltpu.CompilerParams(vmem_limit_bytes=VMEM),
    )(merged, merged, merged, key_extra, *done)


def backward_kernel(
    q_ref, extra_ref, k_ref, v_ref, key_ref, o_ref, do_ref, out_ref, dk_sum, dv_sum
):
    part = pl.program_id(1)
    q, extra, k, v = q_ref[...], extra_ref[...], k_ref[...], v_ref[...]
    key_extra, do = key_ref[...], do_ref[...]
    product = do.astype(F32) * o_ref[...].astype(F32)
    zero = BF(0)
    dq = dk = dv = 0.0
    for head in range(2):
        in_q, place_q = lanes_of(q.shape, head)
        in_k, place_k = lanes_of(k.shape, head)
        scaled = jnp.where(in_q, q * BF(0.125), zero)
        queries = jnp.where(in_q, scaled, extra)
        keys = jnp.where(in_k, k, key_extra)
        only_k = jnp.where(in_k, k, zero)
        only_do = jnp.where(in_q, do, zero)
        row_sum = jnp.sum(jnp.where(in_q, product, 0.0), axis=1, keepdims=True)
        grads = jnp.where(in_q, do, spread_lanes(place_q, split_three(-row_sum)).astype(BF))
        ones = jnp.where((place_k >= 0) & (place_k < 3), BF(1), zero)
        values = jnp.where(in_k, v, ones)
        probs = jnp.exp(rows_dot(keys, queries))
        grad_scores = (probs * rows_dot(values, grads)).astype(BF)
        dv = dv + plain_dot(probs.astype(BF), only_do)
        dk = dk + plain_dot(grad_scores, scaled)
        dq = dq + cols_dot(grad_scores, only_k)
    step = q.shape[0]
    out_ref[pl.ds(part * step, step), :PAIR] = (dq * 0.125).astype(BF)

    @pl.when(part == 0)
    def _():
        dk_sum[...] = dk
        dv_sum[...] = dv

    @pl.when(part > 0)
    def _():
        dk_sum[...] += dk
        dv_sum[...] += dv

    @pl.when(part == pl.num_programs(1) - 1)
    def _():
        out_ref[:, PAIR : 2 * PAIR] = dk_sum[...].astype(BF)
        out_ref[:, 2 * PAIR :] = dv_sum[...].astype(BF)


def attention_backward(merged, extra, key_extra, heads_out, grad_out, step):
    rows = merged.shape[0]
    some = pl.BlockSpec((step, PAIR), lambda pair, part: (part, 3 * pair))
    ours = pl.BlockSpec((step, PAIR), lambda pair, part: (part, pair))
    keys = pl.BlockSpec((rows, PAIR), lambda pair, part: (0, 3 * pair + 1))
    values = pl.BlockSpec((rows, PAIR), lambda pair, part: (0, 3 * pair + 2))
    return pl.pallas_call(
        backward_kernel,
        grid=(HALF // PAIR, rows // step),
        in_specs=[some, ours, keys, values, whole_block(key_extra.shape), ours, ours],
        out_specs=pl.BlockSpec((rows, 3 * PAIR), lambda pair, part: (0, pair)),
        out_shape=jax.ShapeDtypeStruct((rows, 3 * HALF), BF),
        scratch_shapes=[pltpu.VMEM((rows, PAIR), F32)] * 2,
        cost_estimate=NO_COST,
        compiler_params=pltpu.CompilerParams(vmem_limit_bytes=VMEM),
    )(merged, extra, merged, merged, key_extra, heads_out, grad_out)


def key_lanes(allowed):
    lane = jnp.arange(PAIR)[None, :] % HD
    bias = jnp.where(allowed, 0.0, -1e30)[:, None]
    return jnp.where(lane == 0, bias, jnp.where(lane < 4, 1.0, 0.0)).astype(BF)


def weight_block(chip, part, count=1):
    return pl.BlockSpec(
        (1, count * PAIR, D), lambda quarter: (chip * QUARTERS + quarter, part // count, 0)
    )


UP_BLOCKS = (weight_block(1, 1), weight_block(1, 2), weight_block(2, 0, 2))
DOWN_BLOCKS = (weight_block(2, 2), weight_block(3, 0, 3))


def joined(refs):
    return jnp.concatenate([ref[0] for ref in refs], axis=0)


def feed_forward_kernel(
    core_ref, u_mine, u_other, up0, up1, up2, down0, down1, vector_ref,
    hidden_ref, slope_ref, mine_ref, other_ref, total,
):
    quarter = pl.program_id(0)
    rows = [
        vector_ref[pl.ds(3 * D // PAIR + (2 * n + core_ref[0]) * QUARTERS + quarter, 1), :]
        for n in range(4)
    ]
    bias = jnp.concatenate(rows, axis=1)
    up, down = joined((up0, up1, up2)), joined((down0, down1))
    half = mine_ref.shape[0]
    for place, u_ref in ((slice(None, half), u_mine), (slice(half, None), u_other)):
        z = rows_dot(u_ref[...], up) + bias
        cdf = 0.5 * (1.0 + lax.erf(z * (1.0 / math.sqrt(2.0))))
        slope = cdf + z * jnp.exp(-0.5 * z * z) * (1.0 / math.sqrt(2.0 * math.pi))
        hidden = (z * cdf).astype(BF)
        hidden_ref[place, :] = hidden
        slope_ref[place, :] = slope.astype(BF)
        part = plain_dot(hidden, down)

        @pl.when(quarter == 0)
        def _(place=place, part=part):
            total[place, :] = part

        @pl.when(quarter > 0)
        def _(place=place, part=part):
            total[place, :] += part

    @pl.when(quarter == QUARTERS - 1)
    def _():
        mine_ref[...] = total[:half]
        other_ref[...] = total[half:].astype(BF)


def feed_forward(core, u_mine, u_other, whole, vec):
    rows = 2 * u_mine.shape[0]
    columns = pl.BlockSpec((rows, BLOCK), lambda quarter: (0, quarter))
    half = (rows // 2, D)
    return pl.pallas_call(
        feed_forward_kernel,
        grid=(QUARTERS,),
        in_specs=[
            SCALAR, whole_block(half), whole_block(half), *UP_BLOCKS, *DOWN_BLOCKS,
            whole_block(vec.shape),
        ],
        out_specs=[columns, columns, whole_block(half), whole_block(half)],
        out_shape=[
            jax.ShapeDtypeStruct((rows, FF // 2), BF),
            jax.ShapeDtypeStruct((rows, FF // 2), BF),
            jax.ShapeDtypeStruct(half, F32),
            jax.ShapeDtypeStruct(half, BF),
        ],
        scratch_shapes=[pltpu.VMEM((rows, D), F32)],
        cost_estimate=NO_COST,
        compiler_params=pltpu.CompilerParams(vmem_limit_bytes=VMEM),
    )(core, u_mine, u_other, whole, whole, whole, whole, whole, vec)


def feed_backward_kernel(
    df_mine, df_other, u_mine, u_other, hidden_ref, slope_ref, up0, up1, up2, down0, down1,
    grads_ref, bias_ref, mine_ref, other_ref, total,
):
    quarter = pl.program_id(0)
    up, down = joined((up0, up1, up2)), joined((down0, down1))
    half = mine_ref.shape[0]
    grad_up = grad_down = bias = 0.0
    for place, df_ref, u_ref in (
        (slice(None, half), df_mine, u_mine), (slice(half, None), df_other, u_other)
    ):
        df = df_ref[...]
        dz = (rows_dot(df, down) * slope_ref[place, :].astype(F32)).astype(BF)
        bias = bias + jnp.sum(dz.astype(F32), axis=0, keepdims=True)
        grad_up = grad_up + cols_dot(dz, u_ref[...])
        grad_down = grad_down + cols_dot(hidden_ref[place, :], df)
        part = plain_dot(dz, up)

        @pl.when(quarter == 0)
        def _(place=place, part=part):
            total[place, :] = part

        @pl.when(quarter > 0)
        def _(place=place, part=part):
            total[place, :] += part

    bias_ref[...] = bias
    grads_ref[0, :BLOCK] = grad_up.astype(BF)
    grads_ref[0, BLOCK:] = grad_down.astype(BF)

    @pl.when(quarter == QUARTERS - 1)
    def _():
        mine_ref[...] = total[:half]
        other_ref[...] = total[half:].astype(BF)


def feed_backward(df_mine, df_other, u_mine, u_other, hidden, slope, whole):
    rows = 2 * u_mine.shape[0]
    columns = pl.BlockSpec((rows, BLOCK), lambda quarter: (0, quarter))
    half = (rows // 2, D)
    return pl.pallas_call(
        feed_backward_kernel,
        grid=(QUARTERS,),
        in_specs=[
            *[whole_block(half)] * 4, columns, columns, *UP_BLOCKS, *DOWN_BLOCKS
        ],
        out_specs=[
            pl.BlockSpec((1, 2 * BLOCK, D), lambda quarter: (quarter, 0, 0)),
            pl.BlockSpec((1, BLOCK), lambda quarter: (0, quarter)),
            whole_block(half),
            whole_block(half),
        ],
        out_shape=[
            jax.ShapeDtypeStruct((QUARTERS, 2 * BLOCK, D), BF),
            jax.ShapeDtypeStruct((1, FF // 2), F32),
            jax.ShapeDtypeStruct(half, F32),
            jax.ShapeDtypeStruct(half, BF),
        ],
        scratch_shapes=[pltpu.VMEM((rows, D), F32)],
        cost_estimate=NO_COST,
        compiler_params=pltpu.CompilerParams(vmem_limit_bytes=VMEM),
    )(df_mine, df_other, u_mine, u_other, hidden, slope, whole, whole, whole, whole, whole)


def adamw_update(parameter, gradient, first_old, second_old, decay_rate):
    step_float = float(STEP)
    first_new = 0.9 * first_old + 0.1 * gradient
    second_new = 0.999 * second_old + 0.001 * gradient * gradient
    first_fix = first_new * (1.0 / (1.0 - 0.9**step_float))
    second_fix = second_new * (1.0 / (1.0 - 0.999**step_float))
    update = first_fix / (jnp.sqrt(second_fix) + 1e-08)
    return (-LEARN_RATE * (update + decay_rate * parameter), first_new, second_new)


def share(partial):
    half = partial.shape[0] // 2
    return partial[:half] + swap(partial[half:].astype(BF)).astype(F32)


def both(rows):
    return jnp.concatenate([rows, swap(rows)], axis=0)


def spread_part(vector, core, pieces):
    parts = vector.reshape(pieces, 1, -1)
    mine = (jnp.arange(2) == core)[None, :, None]
    return jnp.where(mine, parts, 0.0).reshape(-1)


def token_grads(d_merged, whole, grad_one):
    rows = whole[:QUARTERS, : 3 * PAIR].reshape(-1, D)
    return (share(plain_dot(d_merged, rows)) + grad_one).astype(BF)


def shards(
    tokens,
    cotangent,
    lengths,
    weights,
    vectors,
    first_weights,
    second_weights,
    first_vectors,
    second_vectors,
):
    z, core = lax.axis_index("z"), lax.axis_index("core")
    count, dp_count = lax.axis_size("z"), lax.axis_size("dp")
    per_device = tokens.shape[1]
    rows = count * per_device
    length = lengths[z]
    block = jnp.arange(count, dtype=jnp.int32)[:, None]
    inner = jnp.arange(per_device, dtype=jnp.int32)[None, :]
    chip_of = (z - block) % count
    here = ((chip_of * 2 + core) * per_device + inner).reshape(rows)
    there = ((chip_of * 2 + 1 - core) * per_device + inner).reshape(rows)
    key_extra = key_lanes(jnp.concatenate([here, there]) < length)
    live = (here < length).astype(F32)[:, None]
    core_id = core.astype(jnp.int32).reshape(1)

    outer, middle = pack_weights(weights, is_out_projection(z, core))
    vector = jnp.pad(vectors.astype(BF), (0, EXTRA * D // 2 - vectors.shape[0])).reshape(-1, D)
    other, other_vector = swap(middle), swap(vector)
    whole, piece = own_pieces(outer, other, vector, other_vector, z, core)
    if by_hand():
        x_parts = [to_chip(tokens, z, n) for n in (0, 2)]
        piece, whole, x_parts, tokens = wait(piece, whole, x_parts, tokens)
        up1 = along_z(piece, [(0, 1), (1, 2), (2, 3)])
        down1 = along_z(piece, [(1, 0), (2, 1), (3, 2)])
        up1, down1, whole = wait(up1, down1, whole)
        mine = jnp.where(z == 0, down1, up1)
        got = across(1, mine), across(2, mine)
        up2 = along_z(up1, [(1, 2)])
        down2 = along_z(down1, [(1, 0), (2, 1)])
        mine, got, up1, up2, down1, down2 = wait(mine, got, up1, up2, down1, down2)
        far = across(2, got[0][:, :HALF]), across(1, got[1][:, HALF:])
        up3 = along_z(up2, [(2, 3)])
        mine, got, far, up1, up2, up3, down1, down2 = wait(
            mine, got, far, up1, up2, up3, down1, down2
        )
        mine2 = pick(z, [down2, down1, up2, up3])
        got2 = across(1, mine2), across(2, mine2)
        up4 = along_z(up1, [(2, 3)])
        down3 = along_z(down2, [(1, 0)])
        whole = place(whole, pick(z, [1, 0, 1, 2]), (mine, *got, *far))
        mine, got, up4, down1, down2, down3, whole, tokens = wait(
            mine2, got2, up4, down1, down2, down3, whole, tokens
        )
        far = across(2, got[0][:, :HALF]), across(1, got[1][:, HALF:])
        x_parts += [to_chip(tokens, z, n) for n in (1, 3)]
        mine, got, far, up4, down1, down2, down3, whole, x_parts, cotangent = wait(
            mine, got, far, up4, down1, down2, down3, whole, x_parts, cotangent
        )
        x_mine = jnp.concatenate([x_parts[n] for n in (0, 2, 1, 3)], axis=0)
        x = both(x_mine)
        mine3 = pick(z, [down3, down2, down1, up4])
        got3 = across(1, mine3), across(2, mine3)
        grad_parts = [to_chip(cotangent, z, n) for n in (0, 1)]
        whole = place(whole, pick(z, [2, 2, 0, 0]), (mine, *got, *far))
        vec = vectors_of(whole[:QUARTERS], vectors.shape[0]).reshape(-1, PAIR)
        merged = project(core_id, x, whole, vec)
        done = attention_forward(merged, key_extra, rows * 2, 0, 2)
        mine, got, whole, merged, done, grad_parts, cotangent = wait(
            mine3, got3, whole, merged, done, grad_parts, cotangent
        )
        far = across(2, got[0][:, :HALF]), across(1, got[1][:, HALF:])
        grad_parts += [to_chip(cotangent, z, n) for n in (2, 3)]
        heads_out, extra = attention_forward(merged, key_extra, rows * 2, 2, 2, done)
        mine, got, far, whole, heads_out, extra, grad_parts = wait(
            mine, got, far, whole, heads_out, extra, grad_parts
        )
        whole = place(whole, pick(z, [3, 3, 3, 1]), (mine, *got, *far))
        vec = vectors_of(whole, vectors.shape[0])
    else:
        whole = gather_pieces_of_all(whole, z)
        vec = vectors_of(whole, vectors.shape[0])
        x_mine = to_chips(tokens, z)
        x = both(x_mine)
        grad_parts = [to_chip(cotangent, z, n) for n in range(count)]
        merged = project(core_id, x, whole, vec.reshape(-1, PAIR))
        heads_out, extra = attention_forward(merged, key_extra, 2 * rows, 0, HALF // PAIR)
    grad_out = jnp.concatenate(grad_parts, axis=0)
    bounds = [0, D, 2 * D, 3 * D, 3 * D + FF] + [(n + 4) * D + FF for n in range(6)]
    _, _, bias_o, _, bias_down, gain_one, shift_one, gain_two, shift_two = (
        vec[bounds[n] : bounds[n + 1]] for n in range(9)
    )
    vec = vec.reshape(-1, PAIR)
    w_out = whole[QUARTERS : 2 * QUARTERS, :PAIR].reshape(HALF, D)

    normed_in, normed_one, inverse_one = layer_norm(
        x_mine.astype(F32) + share(plain_dot(heads_out, w_out)) + bias_o, gain_one, shift_one
    )
    u_mine = normed_in.astype(BF)
    u_other = swap(u_mine)
    hidden, slope, feed, feed_other = feed_forward(core_id, u_mine, u_other, whole, vec)
    feed = feed + swap(feed_other).astype(F32) + bias_down
    result, normed_two, inverse_two = layer_norm(u_mine.astype(F32) + feed, gain_two, shift_two)
    layer_out = result.astype(BF)

    grad_out = grad_out.astype(F32) * live
    grad_two, grad_gain_two, grad_shift_two = norm_back(grad_out, normed_two, inverse_two, gain_two)
    df_mine = grad_two.astype(BF)
    grad_bias_down = jnp.sum(df_mine.astype(F32), axis=0)
    grads_ff, grad_bias_up, du, du_other = feed_backward(
        df_mine, swap(df_mine), u_mine, u_other, hidden, slope, whole
    )
    sum_ff = sum_over_dp(grads_ff)
    du = du + swap(du_other).astype(F32) + grad_two
    grad_one, grad_gain_one, grad_shift_one = norm_back(du, normed_one, inverse_one, gain_one)
    da_mine = grad_one.astype(BF)
    da = both(da_mine)
    grad_bias_o = jnp.sum(da_mine.astype(F32), axis=0)
    do = rows_dot(da, w_out).astype(BF)
    grad_wo = cols_dot(heads_out, da).astype(BF)
    do, layer_out = lax.optimization_barrier((do, layer_out))
    layer_out = from_chips(layer_out, z)
    d_merged = attention_backward(merged, extra, key_extra, heads_out, do, rows)
    d_merged, layer_out = lax.optimization_barrier((d_merged, layer_out))
    grad_qkv = cols_dot(d_merged, x).astype(BF)
    sums = jnp.sum(d_merged.astype(F32), axis=0).reshape(QUARTERS, 3, PAIR)
    vector_grad = jnp.concatenate(
        [
            spread_part(sums[:, 0], core, 1),
            spread_part(sums[:, 2], core, 1),
            grad_bias_o,
            spread_part(grad_bias_up.reshape(QUARTERS, 4, PAIR).swapaxes(0, 1), core, 4),
            grad_bias_down,
            grad_gain_one,
            grad_shift_one,
            grad_gain_two,
            grad_shift_two,
        ]
    ).astype(BF)
    shares = vector_grad.reshape(count, dp_count, -1).swapaxes(0, 1)
    if by_hand():
        shares = jnp.pad(shares, ((0, 0), (0, EXTRA - count), (0, D - shares.shape[2])))
    else:
        shares = jnp.pad(shares, ((0, 0), (0, 0), (0, EXTRA * D - shares.shape[2])))
        shares = shares.reshape(dp_count, count * EXTRA, D)
    run = PAIR * QUARTERS // dp_count
    late = jnp.concatenate(
        [
            jnp.concatenate(
                [grad_qkv.reshape(QUARTERS, 3 * PAIR, D), grad_wo.reshape(QUARTERS, PAIR, D)], axis=1
            )
            .reshape(QUARTERS, 4, dp_count // QUARTERS, run, D)
            .swapaxes(1, 2)
            .reshape(dp_count, 4 * run, D),
            shares,
        ],
        axis=1,
    )
    if by_hand():
        late, d_merged = wait(late, d_merged)
        grad_tokens = from_chips(token_grads(d_merged, whole, grad_one), z)
        late, sum_ff, grad_tokens = reduce_late(late, sum_ff, grad_tokens)
        slab = late[4 * PAIR :]
        chips = [late[: 3 * PAIR], slab, late[3 * PAIR : 4 * PAIR], sum_ff[: 2 * PAIR], slab]
        chips += [sum_ff[2 * PAIR : 5 * PAIR], slab, sum_ff[5 * PAIR :], slab]
        piece = lax.psum_scatter(
            jnp.concatenate(chips, axis=0), "z", scatter_dimension=0, tiled=True
        )
        values = gather_pieces(piece)
        start = jnp.where(core == 0, 2 * PAIR, 0)
        sent = jnp.stack(
            [lax.dynamic_slice_in_dim(value, start, PAIR, 0) for value in values[:3]]
            + [
                jnp.concatenate(
                    [lax.dynamic_slice_in_dim(value, start, PAIR, 0) for value in values[3:]], axis=1
                )
            ]
        )
        middle = swap(sent)
        share_size = vectors.shape[0] // 2
        found = [lax.dynamic_slice_in_dim(value, 3 * PAIR + z, 1, 0) for value in values[:4]]
        last = lax.dynamic_slice_in_dim(values[4], 3 * PAIR + z, 1, 0)
        found[3] = jnp.concatenate([found[3], last], axis=1)
        d = lax.axis_index("dp")
        found = jnp.stack([item[0, :share_size] for item in found])
        found = jnp.where(d % 2 == 1, jnp.stack([found[n ^ 1] for n in range(4)]), found)
        found = jnp.where(d >= 2, jnp.stack([found[n ^ 2] for n in range(4)]), found)
        halves = found.reshape(2, -1).astype(F32)
        kept, given = (
            jnp.where(core == 0, halves[0], halves[1]), jnp.where(core == 0, halves[1], halves[0])
        )
        shard_v = kept + swap(given)
        shard_w, weight_change, new_first_weights, new_second_weights = update_weights(
            values, middle, weights, first_weights, second_weights,
            is_out_projection(z, core), core,
        )
    else:
        grad_tokens = from_chips(token_grads(d_merged, whole, grad_one), z)
        sum_late = lax.psum_scatter(late.reshape(-1, D), "dp", scatter_dimension=0, tiled=True)
        parts = [sum_late[n * run : (n + 1) * run] for n in range(4)]
        parts += [sum_ff[n * run : (n + 1) * run] for n in range(8)]
        spare = sum_late[4 * run :].reshape(count, EXTRA, D)
        chips = [
            jnp.concatenate([*parts[3 * chip : 3 * chip + 3], spare[chip]], axis=0)
            for chip in range(count)
        ]
        piece = lax.psum_scatter(
            jnp.concatenate(chips, axis=0), "z", scatter_dimension=0, tiled=True
        )
        summed = lax.all_gather(piece, "dp", axis=0, tiled=True).reshape(dp_count, -1, D)
        blocks = summed[:, : 3 * run].reshape(dp_count, 3, run, D).swapaxes(0, 1).reshape(3, BLOCK, D)
        share_size = vectors.shape[0] * 2 // dp_count
        vector_sum = summed[:, 3 * run :].reshape(dp_count, -1)
        start = 0
        vector_sum = lax.dynamic_slice_in_dim(vector_sum, start, share_size, 1)
        vector_sum = vector_sum.reshape(2, -1).astype(F32)
        vector_sum = jnp.pad(vector_sum, ((0, 0), (0, 2 * D - vector_sum.shape[1])))
        shard_v = vector_sum[core] + swap(vector_sum[1 - core])
        shard_v = shard_v[: vectors.shape[0]]
        a, b, c = blocks
        middle = swap(jnp.where(core == 0, c, a))
        top = jnp.concatenate([jnp.where(core == 0, a, b), middle], axis=0)
        top = jnp.where(is_out_projection(z, core), top.T, top)
        shard_w = jnp.concatenate([top, jnp.where(core == 0, b, c)], axis=0).astype(F32)

        weight_change, new_first_weights, new_second_weights = adamw_update(
            weights, shard_w, first_weights, second_weights, 0.01
        )
    vector_change, new_first_vectors, new_second_vectors = adamw_update(
        vectors, shard_v, first_vectors, second_vectors, 0.0
    )
    return (
        layer_out,
        grad_tokens,
        shard_w,
        shard_v,
        weight_change,
        vector_change,
        new_first_weights,
        new_second_weights,
        new_first_vectors,
        new_second_vectors,
    )


def solution(mesh):
    chips = Mesh(
        mesh.devices.reshape(mesh.shape["dp"], mesh.shape["ctx"] // 2, 2), ("dp", "z", "core")
    )
    ctx = ("z", "core")
    activations, matrix, vector = P("dp", ctx, None), P(ctx, None), P(ctx)
    return jax.shard_map(
        shards,
        mesh=chips,
        in_specs=(activations, activations, P("dp"), matrix, vector, matrix, matrix, vector, vector),
        out_specs=(
            activations,
            activations,
            matrix,
            vector,
            matrix,
            vector,
            matrix,
            matrix,
            vector,
            vector,
        ),
        check_vma=False,
    )
```

```python
import math

import jax
import jax.numpy as jnp
from jax import lax
from jax.experimental import pallas as pl
from jax.experimental.pallas import tpu as pltpu
from jax.sharding import Mesh
from jax.sharding import PartitionSpec as P

D = 1024
FF = 4096
HD = 64
PAIR = 2 * HD
STEP = 10
EPSILON = 1e-05
LEARN_RATE = 0.003
BF = jnp.bfloat16
F32 = jnp.float32
HALF = D // 2
BLOCK = 512
EXTRA = 16
QUARTERS = 4
PIECE = 3 * PAIR + EXTRA
VMEM = 60 * 2**20
SCALAR = pl.BlockSpec(memory_space=pltpu.SMEM)
NO_COST = pl.CostEstimate(flops=1, bytes_accessed=1, transcendentals=0)


def rows_dot(operand, matrix):
    return lax.dot_general(operand, matrix, (((1,), (1,)), ((), ())), preferred_element_type=F32)


def cols_dot(operand, matrix):
    return lax.dot_general(operand, matrix, (((0,), (0,)), ((), ())), preferred_element_type=F32)


def plain_dot(operand, matrix):
    return lax.dot_general(operand, matrix, (((1,), (0,)), ((), ())), preferred_element_type=F32)


def swap(value):
    return lax.ppermute(value, "core", [(0, 1), (1, 0)])


def layer_norm(inputs, gain_vec, shift_vec):
    centre = jnp.mean(inputs, axis=-1, keepdims=True)
    shifted = inputs - centre
    inverse = lax.rsqrt(jnp.mean(shifted * shifted, axis=-1, keepdims=True) + EPSILON)
    normed = shifted * inverse
    return (normed * gain_vec + shift_vec, normed, inverse)


def norm_back(grad_out, normed, inverse, gain_vec):
    scaled = grad_out * gain_vec
    inner_term = (
        scaled
        - jnp.mean(scaled, axis=-1, keepdims=True)
        - normed * jnp.mean(scaled * normed, axis=-1, keepdims=True)
    )
    return (inverse * inner_term, jnp.sum(grad_out * normed, axis=0), jnp.sum(grad_out, axis=0))


def to_chip(blocks, z, shift):
    count = lax.axis_size("z")
    part = lax.dynamic_index_in_dim(blocks, (z + shift) % count, 0, keepdims=False)
    if shift:
        part = lax.ppermute(part, "z", [(i, (i + shift) % count) for i in range(count)])
    return part


def to_chips(blocks, z):
    return jnp.concatenate([to_chip(blocks, z, n) for n in range(lax.axis_size("z"))], axis=0)


def from_chip(rows, shift):
    count = lax.axis_size("z")
    part = rows.reshape(count, -1, rows.shape[-1])[shift]
    if shift:
        part = lax.ppermute(part, "z", [(i, (i - shift) % count) for i in range(count)])
    return part


def put_together(parts, z):
    count = lax.axis_size("z")
    result = jnp.zeros((count, *parts[0].shape), BF)
    for shift in range(count):
        result = lax.dynamic_update_index_in_dim(result, parts[shift], (z + shift) % count, 0)
    return result


def from_chips(rows, z):
    return put_together([from_chip(rows, n) for n in range(lax.axis_size("z"))], z)


def is_out_projection(z, core):
    return jnp.logical_and(z == 1, core == 0)


def pack_kernel(flag_ref, rows_ref, columns_ref, outer_ref, middle_ref):
    step = pl.program_id(0)
    turned = jnp.logical_and(flag_ref[0] == 1, step < 2)

    def write(value):
        @pl.when(step != 1)
        def _():
            outer_ref[...] = value

        @pl.when(step == 1)
        def _():
            middle_ref[...] = value

    @pl.when(turned)
    def _():
        write(columns_ref[...].T.astype(BF))

    @pl.when(jnp.logical_not(turned))
    def _():
        write(rows_ref[...].astype(BF))


def pack_weights(weights, flag):
    return pl.pallas_call(
        pack_kernel,
        grid_spec=pltpu.PrefetchScalarGridSpec(
            num_scalar_prefetch=1,
            grid=(3,),
            in_specs=[
                pl.BlockSpec((BLOCK, D), lambda n, flag: (n, 0)),
                pl.BlockSpec((D, BLOCK), lambda n, flag: (0, jnp.minimum(n, 1) * flag[0])),
            ],
            out_specs=[
                pl.BlockSpec((BLOCK, D), lambda n, flag: (n // 2, 0)),
                pl.BlockSpec((BLOCK, D), lambda n, flag: (0, 0)),
            ],
        ),
        out_shape=[
            jax.ShapeDtypeStruct((2 * BLOCK, D), BF),
            jax.ShapeDtypeStruct((BLOCK, D), BF),
        ],
        cost_estimate=NO_COST,
        compiler_params=pltpu.CompilerParams(vmem_limit_bytes=VMEM),
    )(flag.astype(jnp.int32).reshape(1), weights, weights)


def own_kernel(
    where_ref, first_ref, last_ref, other_ref, mine_vector, other_vector, whole_ref, piece_ref
):
    core = where_ref[2]

    def write(parts, vectors):
        value = jnp.concatenate([*parts, *vectors], axis=0)
        whole_ref[0] = value

        @pl.when(pl.program_id(0) == 0)
        def _():
            piece_ref[...] = value

    first, last, other = first_ref[...], last_ref[...], other_ref[...]
    vectors = [mine_vector[...], other_vector[...]]

    @pl.when(core == 0)
    def _():
        write([first, last, other], vectors)

    @pl.when(core == 1)
    def _():
        write([other, first, last], vectors[::-1])


def own_pieces(outer, other, vector, other_vector, z, core):
    where = jnp.stack([z, lax.axis_index("dp") % QUARTERS, core]).astype(jnp.int32)
    run = (PAIR, D)
    small = pl.BlockSpec(vector.shape, lambda n, where: (0, 0))
    return pl.pallas_call(
        own_kernel,
        grid_spec=pltpu.PrefetchScalarGridSpec(
            num_scalar_prefetch=1,
            grid=(QUARTERS,),
            in_specs=[
                pl.BlockSpec(run, lambda n, where: (where[1] ^ n, 0)),
                pl.BlockSpec(run, lambda n, where: (QUARTERS + (where[1] ^ n), 0)),
                pl.BlockSpec(run, lambda n, where: (where[1] ^ n, 0)),
                small,
                small,
            ],
            out_specs=[
                pl.BlockSpec(
                    (1, PIECE, D), lambda n, where: (where[0] * QUARTERS + (where[1] ^ n), 0, 0)
                ),
                pl.BlockSpec((PIECE, D), lambda n, where: (0, 0)),
            ],
        ),
        out_shape=[
            jax.ShapeDtypeStruct((4 * QUARTERS, PIECE, D), BF),
            jax.ShapeDtypeStruct((PIECE, D), BF),
        ],
        cost_estimate=NO_COST,
        compiler_params=pltpu.CompilerParams(vmem_limit_bytes=VMEM),
    )(where, outer, outer, other, vector, other_vector)


def gather_pieces_of_all(whole, z):
    count = lax.axis_size("dp") // QUARTERS
    mine = lax.dynamic_slice_in_dim(whole, z * QUARTERS, QUARTERS, 0)
    share = lax.dynamic_index_in_dim(mine, lax.axis_index("dp") // count, 0, keepdims=False)
    blocks = share[: 3 * PAIR].reshape(3, PAIR, D)
    blocks = lax.dynamic_slice_in_dim(
        blocks, lax.axis_index("dp") % count * (PAIR // count), PAIR // count, 1
    )
    everything = lax.all_gather(blocks.reshape(-1, D), ("z", "dp"), axis=0, tiled=True)
    everything = everything.reshape(-1, count, 3, PAIR // count, D).swapaxes(1, 2)
    spare = lax.all_gather(share[3 * PAIR :], "z", axis=0, tiled=True).reshape(-1, 1, EXTRA, D)
    spare = jnp.broadcast_to(spare, (spare.shape[0], QUARTERS, EXTRA, D)).reshape(-1, EXTRA, D)
    return jnp.concatenate([everything.reshape(-1, 3 * PAIR, D), spare], axis=1)


def vectors_of(whole, size, chips):
    found = jnp.stack([whole[QUARTERS * chip, 3 * PAIR :] for chip in range(chips)])
    return found.reshape(-1, 2, EXTRA * D // 2)[:, :, :size].reshape(-1).astype(F32)


def place_kernel(where_ref, whole_in, mine, got_x, got_y, far_a, far_b, whole_ref):
    del where_ref, whole_in
    for index, source in enumerate((mine, got_x, got_y)):

        @pl.when(pl.program_id(0) == index)
        def _(source=source):
            whole_ref[0] = source[...]

    @pl.when(pl.program_id(0) == 3)
    def _():
        whole_ref[0, :, :HALF] = far_a[...]
        whole_ref[0, :, HALF:] = far_b[...]


def place(whole, shard, values):
    where = jnp.stack([shard, lax.axis_index("dp")]).astype(jnp.int32)
    return pl.pallas_call(
        place_kernel,
        grid_spec=pltpu.PrefetchScalarGridSpec(
            num_scalar_prefetch=1,
            grid=(4,),
            in_specs=[pl.BlockSpec(memory_space=pl.ANY)]
            + [pl.BlockSpec(value.shape, lambda n, where: (0, 0)) for value in values],
            out_specs=pl.BlockSpec(
                (1, PIECE, D), lambda n, where: (where[0] * QUARTERS + (where[1] ^ n), 0, 0)
            ),
        ),
        out_shape=jax.ShapeDtypeStruct(whole.shape, BF),
        input_output_aliases={1: 0},
        cost_estimate=NO_COST,
        compiler_params=pltpu.CompilerParams(vmem_limit_bytes=VMEM),
    )(where, whole, *values)


def sum_over_dp(grads):
    count = lax.axis_size("dp") // QUARTERS
    if count > 1:
        grads = grads.reshape(QUARTERS, -1, count, PAIR // count, D).swapaxes(1, 2)
    return lax.psum_scatter(grads.reshape(-1, D), "dp", scatter_dimension=0, tiled=True)


def by_hand():
    return lax.axis_size("dp") == 4 and lax.axis_size("z") == 4


def plus(first, second):
    return (first.astype(F32) + second.astype(F32)).astype(BF)


def across(bit, value):
    return lax.ppermute(value, "dp", [(i, i ^ bit) for i in range(4)])


def at(value, index, axis):
    return lax.dynamic_index_in_dim(value, index, axis, keepdims=False)


def along_z(value, pairs):
    return lax.ppermute(value, "z", pairs)


def pick(z, values):
    result = values[-1]
    for index in range(len(values) - 2, -1, -1):
        result = jnp.where(z == index, values[index], result)
    return result


def wait(*values):
    return lax.optimization_barrier(values)


def assemble_kernel(a_ref, b_ref, sums_ref, out_ref):
    chip = pl.program_id(0)
    rows = 3 * PAIR
    out_ref[rows:, :HALF] = a_ref[4 * PAIR :]
    out_ref[rows:, HALF:] = b_ref[4 * PAIR :]

    @pl.when(chip == 0)
    def _():
        out_ref[:rows, :HALF] = a_ref[:rows]
        out_ref[:rows, HALF:] = b_ref[:rows]

    @pl.when(chip == 1)
    def _():
        out_ref[:PAIR, :HALF] = a_ref[rows : rows + PAIR]
        out_ref[:PAIR, HALF:] = b_ref[rows : rows + PAIR]
        out_ref[PAIR:rows] = sums_ref[: 2 * PAIR]

    @pl.when(chip == 2)
    def _():
        out_ref[:rows] = sums_ref[2 * PAIR : 5 * PAIR]

    @pl.when(chip == 3)
    def _():
        out_ref[:rows] = sums_ref[5 * PAIR :]


def assemble(a, b, sums):
    return pl.pallas_call(
        assemble_kernel,
        grid=(4,),
        in_specs=[whole_block(item.shape) for item in (a, b, sums)],
        out_specs=pl.BlockSpec((PIECE, D), lambda chip: (chip, 0)),
        out_shape=jax.ShapeDtypeStruct((4 * PIECE, D), BF),
        cost_estimate=NO_COST,
        compiler_params=pltpu.CompilerParams(vmem_limit_bytes=VMEM),
    )(a, b, sums)


def reduce_late(late, sum_ff, grad_rows):
    d = lax.axis_index("dp")
    x, y = d % 2, d // 2
    late = late.reshape(2, 2, -1, D)
    a, b = late[..., :HALF], late[..., HALF:]
    got_a, got_b = across(1, at(a, 1 - x, 1)), across(2, at(b, 1 - y, 0))
    got_a, got_b, a, b, sum_ff, grad_rows = wait(got_a, got_b, a, b, sum_ff, grad_rows)
    a, b = at(a, x, 1), at(b, y, 0)
    far_a = across(2, plus(at(a, 1 - y, 0), at(got_a, 1 - y, 0)))
    far_b = across(1, plus(at(b, 1 - x, 0), at(got_b, 1 - x, 0)))
    parts = {n: from_chip(grad_rows, n) for n in (0, 1, 3)}
    far_a, far_b, a, b, parts, grad_rows = wait(far_a, far_b, a, b, parts, grad_rows)
    a = plus(plus(at(a, y, 0), at(got_a, y, 0)), far_a)
    b = plus(plus(at(b, x, 0), at(got_b, x, 0)), far_b)
    return assemble(a, b, sum_ff), parts, grad_rows


def gather_pieces(piece, grad_rows, parts, z):
    got = across(1, piece), across(2, piece)
    parts = {**parts, 2: from_chip(grad_rows, 2)}
    got, piece, parts = wait(got, piece, parts)
    far = across(2, got[0][:, :HALF]), across(1, got[1][:, HALF:])
    far, got, piece, parts = wait(far, got, piece, parts)
    return (piece, *got, *far), put_together(parts, z)


def update_kernel(
    where_ref, mine, got_x, got_y, far_a, far_b, middle_ref, weight_ref, first_ref, second_ref,
    grad_ref, change_ref, first_out, second_out,
):
    d, core, turned = where_ref[0], where_ref[1], where_ref[2] == 1
    block, pair = pl.program_id(0), pl.program_id(1)
    pieces = (mine, got_x, got_y)
    rows = pl.ds(pl.multiple_of((core + block // 2) * PAIR, PAIR), PAIR)
    plain = jnp.logical_and(block != 1, jnp.logical_or(block == 2, jnp.logical_not(turned)))
    for n in range(QUARTERS):
        slot = pl.ds(pl.multiple_of((d % 2 ^ (n % 2)) * PAIR, PAIR), PAIR)
        ours = pair == n // 2

        @pl.when(ours & (block == 1) & jnp.logical_not(turned))
        def _(n=n, slot=slot):
            grad_ref[slot, :] = middle_ref[n].astype(F32)

        @pl.when(ours & plain)
        def _(n=n, slot=slot):
            if n < 3:
                grad_ref[slot, :] = pieces[n][rows, :].astype(F32)
            else:
                grad_ref[slot, :HALF] = far_a[rows, :].astype(F32)
                grad_ref[slot, HALF:] = far_b[rows, :].astype(F32)

        @pl.when(ours & (block < 2) & turned)
        def _(n=n, slot=slot):
            start = pl.multiple_of((d ^ n) * PAIR, PAIR)
            columns = pl.ds(pl.multiple_of(block * HALF + start, PAIR), PAIR)
            for m in range(QUARTERS):
                low = pl.ds(pl.multiple_of((d ^ m) * PAIR, PAIR), PAIR)
                high = pl.ds(pl.multiple_of(HALF + (d ^ m) * PAIR, PAIR), PAIR)
                grad_ref[slot, high] = middle_ref[m, :, columns].astype(F32).T
                if m < 3:
                    grad_ref[slot, low] = pieces[m][:PAIR, columns].astype(F32).T
            low = pl.ds(pl.multiple_of((d ^ 3) * PAIR, PAIR), PAIR)
            for half, far in enumerate((far_a, far_b)):

                @pl.when(block == half)
                def _(far=far):
                    grad_ref[slot, low] = far[:PAIR, pl.ds(start, PAIR)].astype(F32).T

    change_ref[...], first_out[...], second_out[...] = adamw_update(
        weight_ref[...], grad_ref[...], first_ref[...], second_ref[...], 0.01
    )


def update_weights(values, middle, weights, first_weights, second_weights, turned, core):
    d = lax.axis_index("dp")
    where = jnp.stack([d, core, turned.astype(jnp.int32)]).astype(jnp.int32)
    rows = pl.BlockSpec((2 * PAIR, D), lambda b, n, where: (b * 2 + (where[0] // 2 ^ n), 0))
    return pl.pallas_call(
        update_kernel,
        grid_spec=pltpu.PrefetchScalarGridSpec(
            num_scalar_prefetch=1,
            grid=(3, 2),
            in_specs=[pl.BlockSpec(value.shape, lambda b, n, where: (0, 0)) for value in values]
            + [pl.BlockSpec(middle.shape, lambda b, n, where: (0, 0, 0))]
            + [rows] * 3,
            out_specs=[rows] * 4,
        ),
        out_shape=[jax.ShapeDtypeStruct(weights.shape, F32)] * 4,
        cost_estimate=NO_COST,
        compiler_params=pltpu.CompilerParams(vmem_limit_bytes=VMEM),
    )(where, *values, middle, weights, first_weights, second_weights)


def lanes_of(shape, head):
    lane = lax.broadcasted_iota(jnp.int32, shape, 1)
    return (lane >= HD) if head else (lane < HD), lane - HD * (1 - head)


def split_three(value):
    high = value.astype(BF).astype(F32)
    mid = (value - high).astype(BF).astype(F32)
    return high, mid, (value - high - mid).astype(BF).astype(F32)


def spread_lanes(place, values):
    result = jnp.zeros(place.shape, F32)
    for lane, value in enumerate(values):
        result = jnp.where(place == lane, value, result)
    return result


def whole_block(shape):
    return pl.BlockSpec(shape, lambda *_: (0,) * len(shape))


def qkv_kernel(core_ref, x_mine, x_other, w_ref, vector_ref, out_ref):
    quarter = pl.program_id(0)
    row = core_ref[0] * QUARTERS + quarter
    bias_q = vector_ref[pl.ds(row, 1), :]
    bias_v = vector_ref[pl.ds(D // PAIR + row, 1), :]
    bias = jnp.concatenate([bias_q, jnp.zeros_like(bias_q), bias_v], axis=1)
    half = x_mine.shape[0]
    out_ref[:half] = (rows_dot(x_mine[...], w_ref[0]) + bias).astype(BF)
    out_ref[half:] = (rows_dot(x_other[...], w_ref[0]) + bias).astype(BF)


def project(core, x_mine, x_other, whole, vec):
    rows = 2 * x_mine.shape[0]
    return pl.pallas_call(
        qkv_kernel,
        grid=(QUARTERS,),
        in_specs=[
            SCALAR,
            whole_block(x_mine.shape),
            whole_block(x_mine.shape),
            pl.BlockSpec((1, 3 * PAIR, D), lambda quarter: (quarter, 0, 0)),
            whole_block(vec.shape),
        ],
        out_specs=pl.BlockSpec((rows, 3 * PAIR), lambda quarter: (0, quarter)),
        out_shape=jax.ShapeDtypeStruct((rows, 3 * HALF), BF),
        cost_estimate=NO_COST,
        compiler_params=pltpu.CompilerParams(vmem_limit_bytes=VMEM),
    )(core, x_mine, x_other, whole, vec)


def forward_kernel(q_ref, k_ref, v_ref, key_ref, o_ref, extra_ref):
    q, k, v, key_extra = q_ref[...], k_ref[...], v_ref[...], key_ref[...]
    outs, extras = [], []
    for head in range(2):
        in_q, place_q = lanes_of(q.shape, head)
        in_k, place_k = lanes_of(k.shape, head)
        keys = jnp.where(in_k, k, key_extra)
        queries = jnp.where(in_q, q * BF(0.125), jnp.where(place_q == 0, BF(1), BF(0)))
        values = jnp.where(in_k, v, jnp.where(place_k == 0, BF(1), BF(0)))
        scores = rows_dot(queries, keys)
        highest = jnp.max(scores, axis=1, keepdims=True)
        terms = jnp.exp(scores - highest).astype(BF)
        out = plain_dot(terms, values)
        column = HD * (1 - head)
        total = out[:, column : column + 1]
        outs.append(out * (1.0 / total))
        parts = split_three(-(highest + jnp.log(total)))
        extras.append(spread_lanes(place_q, (1.0, *parts)))
    in_first, _ = lanes_of(q.shape, 0)
    o_ref[...] = jnp.where(in_first, outs[0], outs[1]).astype(BF)
    extra_ref[...] = jnp.where(in_first, extras[1], extras[0]).astype(BF)


def forward_more_kernel(q_ref, k_ref, v_ref, key_ref, o_in, extra_in, o_ref, extra_ref):
    del o_in, extra_in
    forward_kernel(q_ref, k_ref, v_ref, key_ref, o_ref, extra_ref)


def attention_forward(merged, key_extra, step, start, pairs, done=()):
    rows = merged.shape[0]
    some = pl.BlockSpec((step, PAIR), lambda pair, part: (part, 3 * (pair + start)))
    ours = pl.BlockSpec((step, PAIR), lambda pair, part: (part, pair + start))
    keys = pl.BlockSpec((rows, PAIR), lambda pair, part: (0, 3 * (pair + start) + 1))
    values = pl.BlockSpec((rows, PAIR), lambda pair, part: (0, 3 * (pair + start) + 2))
    return pl.pallas_call(
        forward_more_kernel if done else forward_kernel,
        grid=(pairs, rows // step),
        in_specs=[some, keys, values, whole_block(key_extra.shape)]
        + [pl.BlockSpec(memory_space=pl.ANY)] * len(done),
        out_specs=[ours, ours],
        out_shape=[jax.ShapeDtypeStruct((rows, HALF), BF)] * 2,
        input_output_aliases={4: 0, 5: 1} if done else {},
        cost_estimate=NO_COST,
        compiler_params=pltpu.CompilerParams(vmem_limit_bytes=VMEM),
    )(merged, merged, merged, key_extra, *done)


def backward_kernel(
    q_ref, extra_ref, k_ref, v_ref, key_ref, o_ref, do_ref, out_ref, dk_sum, dv_sum
):
    part = pl.program_id(1)
    q, extra, k, v = q_ref[...], extra_ref[...], k_ref[...], v_ref[...]
    key_extra, do = key_ref[...], do_ref[...]
    product = do.astype(F32) * o_ref[...].astype(F32)
    zero = BF(0)
    dq = dk = dv = 0.0
    for head in range(2):
        in_q, place_q = lanes_of(q.shape, head)
        in_k, place_k = lanes_of(k.shape, head)
        scaled = jnp.where(in_q, q * BF(0.125), zero)
        queries = jnp.where(in_q, scaled, extra)
        keys = jnp.where(in_k, k, key_extra)
        only_k = jnp.where(in_k, k, zero)
        only_do = jnp.where(in_q, do, zero)
        row_sum = jnp.sum(jnp.where(in_q, product, 0.0), axis=1, keepdims=True)
        grads = jnp.where(in_q, do, spread_lanes(place_q, split_three(-row_sum)).astype(BF))
        ones = jnp.where((place_k >= 0) & (place_k < 3), BF(1), zero)
        values = jnp.where(in_k, v, ones)
        probs = jnp.exp(rows_dot(keys, queries))
        grad_scores = (probs * rows_dot(values, grads)).astype(BF)
        dv = dv + plain_dot(probs.astype(BF), only_do)
        dk = dk + plain_dot(grad_scores, scaled)
        dq = dq + cols_dot(grad_scores, only_k)
    step = q.shape[0]
    out_ref[pl.ds(part * step, step), :PAIR] = (dq * 0.125).astype(BF)

    @pl.when(part == 0)
    def _():
        dk_sum[...] = dk
        dv_sum[...] = dv

    @pl.when(part > 0)
    def _():
        dk_sum[...] += dk
        dv_sum[...] += dv

    @pl.when(part == pl.num_programs(1) - 1)
    def _():
        out_ref[:, PAIR : 2 * PAIR] = dk_sum[...].astype(BF)
        out_ref[:, 2 * PAIR :] = dv_sum[...].astype(BF)


def attention_backward(merged, extra, key_extra, heads_out, grad_out, step):
    rows = merged.shape[0]
    some = pl.BlockSpec((step, PAIR), lambda pair, part: (part, 3 * pair))
    ours = pl.BlockSpec((step, PAIR), lambda pair, part: (part, pair))
    keys = pl.BlockSpec((rows, PAIR), lambda pair, part: (0, 3 * pair + 1))
    values = pl.BlockSpec((rows, PAIR), lambda pair, part: (0, 3 * pair + 2))
    return pl.pallas_call(
        backward_kernel,
        grid=(HALF // PAIR, rows // step),
        in_specs=[some, ours, keys, values, whole_block(key_extra.shape), ours, ours],
        out_specs=pl.BlockSpec((rows, 3 * PAIR), lambda pair, part: (0, pair)),
        out_shape=jax.ShapeDtypeStruct((rows, 3 * HALF), BF),
        scratch_shapes=[pltpu.VMEM((rows, PAIR), F32)] * 2,
        cost_estimate=NO_COST,
        compiler_params=pltpu.CompilerParams(vmem_limit_bytes=VMEM),
    )(merged, extra, merged, merged, key_extra, heads_out, grad_out)


def key_lanes(allowed):
    lane = jnp.arange(PAIR)[None, :] % HD
    bias = jnp.where(allowed, 0.0, -1e30)[:, None]
    return jnp.where(lane == 0, bias, jnp.where(lane < 4, 1.0, 0.0)).astype(BF)


def weight_block(chip, part, count=1):
    return pl.BlockSpec(
        (1, count * PAIR, D), lambda quarter: (chip * QUARTERS + quarter, part // count, 0)
    )


UP_BLOCKS = (weight_block(1, 1), weight_block(1, 2), weight_block(2, 0, 2))
DOWN_BLOCKS = (weight_block(2, 2), weight_block(3, 0, 3))


def joined(refs):
    return jnp.concatenate([ref[0] for ref in refs], axis=0)


def feed_forward_kernel(
    core_ref, u_mine, u_other, up0, up1, up2, down0, down1, vector_ref,
    hidden_ref, slope_ref, mine_ref, other_ref, total,
):
    quarter = pl.program_id(0)
    rows = [
        vector_ref[pl.ds(3 * D // PAIR + (2 * n + core_ref[0]) * QUARTERS + quarter, 1), :]
        for n in range(4)
    ]
    bias = jnp.concatenate(rows, axis=1)
    up, down = joined((up0, up1, up2)), joined((down0, down1))
    half = mine_ref.shape[0]
    for place, u_ref in ((slice(None, half), u_mine), (slice(half, None), u_other)):
        z = rows_dot(u_ref[...], up) + bias
        cdf = 0.5 * (1.0 + lax.erf(z * (1.0 / math.sqrt(2.0))))
        slope = cdf + z * jnp.exp(-0.5 * z * z) * (1.0 / math.sqrt(2.0 * math.pi))
        hidden = (z * cdf).astype(BF)
        hidden_ref[place, :] = hidden
        slope_ref[place, :] = slope.astype(BF)
        part = plain_dot(hidden, down)

        @pl.when(quarter == 0)
        def _(place=place, part=part):
            total[place, :] = part

        @pl.when(quarter > 0)
        def _(place=place, part=part):
            total[place, :] += part

    @pl.when(quarter == QUARTERS - 1)
    def _():
        mine_ref[...] = total[:half]
        other_ref[...] = total[half:].astype(BF)


def feed_forward(core, u_mine, u_other, whole, vec):
    rows = 2 * u_mine.shape[0]
    columns = pl.BlockSpec((rows, BLOCK), lambda quarter: (0, quarter))
    half = (rows // 2, D)
    return pl.pallas_call(
        feed_forward_kernel,
        grid=(QUARTERS,),
        in_specs=[
            SCALAR, whole_block(half), whole_block(half), *UP_BLOCKS, *DOWN_BLOCKS,
            whole_block(vec.shape),
        ],
        out_specs=[columns, columns, whole_block(half), whole_block(half)],
        out_shape=[
            jax.ShapeDtypeStruct((rows, FF // 2), BF),
            jax.ShapeDtypeStruct((rows, FF // 2), BF),
            jax.ShapeDtypeStruct(half, F32),
            jax.ShapeDtypeStruct(half, BF),
        ],
        scratch_shapes=[pltpu.VMEM((rows, D), F32)],
        cost_estimate=NO_COST,
        compiler_params=pltpu.CompilerParams(vmem_limit_bytes=VMEM),
    )(core, u_mine, u_other, whole, whole, whole, whole, whole, vec)


def feed_backward_kernel(
    df_mine, df_other, u_mine, u_other, hidden_ref, slope_ref, up0, up1, up2, down0, down1,
    grads_ref, bias_ref, mine_ref, other_ref, total,
):
    quarter = pl.program_id(0)
    up, down = joined((up0, up1, up2)), joined((down0, down1))
    half = mine_ref.shape[0]
    grad_up = grad_down = bias = 0.0
    for place, df_ref, u_ref in (
        (slice(None, half), df_mine, u_mine), (slice(half, None), df_other, u_other)
    ):
        df = df_ref[...]
        dz = (rows_dot(df, down) * slope_ref[place, :].astype(F32)).astype(BF)
        bias = bias + jnp.sum(dz.astype(F32), axis=0, keepdims=True)
        grad_up = grad_up + cols_dot(dz, u_ref[...])
        grad_down = grad_down + cols_dot(hidden_ref[place, :], df)
        part = plain_dot(dz, up)

        @pl.when(quarter == 0)
        def _(place=place, part=part):
            total[place, :] = part

        @pl.when(quarter > 0)
        def _(place=place, part=part):
            total[place, :] += part

    bias_ref[...] = bias
    grads_ref[0, :BLOCK] = grad_up.astype(BF)
    grads_ref[0, BLOCK:] = grad_down.astype(BF)

    @pl.when(quarter == QUARTERS - 1)
    def _():
        mine_ref[...] = total[:half]
        other_ref[...] = total[half:].astype(BF)


def feed_backward(df_mine, df_other, u_mine, u_other, hidden, slope, whole):
    rows = 2 * u_mine.shape[0]
    columns = pl.BlockSpec((rows, BLOCK), lambda quarter: (0, quarter))
    half = (rows // 2, D)
    return pl.pallas_call(
        feed_backward_kernel,
        grid=(QUARTERS,),
        in_specs=[
            *[whole_block(half)] * 4, columns, columns, *UP_BLOCKS, *DOWN_BLOCKS
        ],
        out_specs=[
            pl.BlockSpec((1, 2 * BLOCK, D), lambda quarter: (quarter, 0, 0)),
            pl.BlockSpec((1, BLOCK), lambda quarter: (0, quarter)),
            whole_block(half),
            whole_block(half),
        ],
        out_shape=[
            jax.ShapeDtypeStruct((QUARTERS, 2 * BLOCK, D), BF),
            jax.ShapeDtypeStruct((1, FF // 2), F32),
            jax.ShapeDtypeStruct(half, F32),
            jax.ShapeDtypeStruct(half, BF),
        ],
        scratch_shapes=[pltpu.VMEM((rows, D), F32)],
        cost_estimate=NO_COST,
        compiler_params=pltpu.CompilerParams(vmem_limit_bytes=VMEM),
    )(df_mine, df_other, u_mine, u_other, hidden, slope, whole, whole, whole, whole, whole)


def adamw_update(parameter, gradient, first_old, second_old, decay_rate):
    step_float = float(STEP)
    first_new = 0.9 * first_old + 0.1 * gradient
    second_new = 0.999 * second_old + 0.001 * gradient * gradient
    first_fix = first_new * (1.0 / (1.0 - 0.9**step_float))
    second_fix = second_new * (1.0 / (1.0 - 0.999**step_float))
    update = first_fix / (jnp.sqrt(second_fix) + 1e-08)
    return (-LEARN_RATE * (update + decay_rate * parameter), first_new, second_new)


def share(partial):
    half = partial.shape[0] // 2
    return partial[:half] + swap(partial[half:].astype(BF)).astype(F32)


def both(rows):
    return jnp.concatenate([rows, swap(rows)], axis=0)


def spread_part(vector, core, pieces):
    parts = vector.reshape(pieces, 1, -1)
    mine = (jnp.arange(2) == core)[None, :, None]
    return jnp.where(mine, parts, 0.0).reshape(-1)


def token_grads(d_merged, whole, grad_one):
    rows = whole[:QUARTERS, : 3 * PAIR].reshape(-1, D)
    return (share(plain_dot(d_merged, rows)) + grad_one).astype(BF)


def shards(
    tokens,
    cotangent,
    lengths,
    weights,
    vectors,
    first_weights,
    second_weights,
    first_vectors,
    second_vectors,
):
    z, core = lax.axis_index("z"), lax.axis_index("core")
    count, dp_count = lax.axis_size("z"), lax.axis_size("dp")
    per_device = tokens.shape[1]
    rows = count * per_device
    length = lengths[z]
    block = jnp.arange(count, dtype=jnp.int32)[:, None]
    inner = jnp.arange(per_device, dtype=jnp.int32)[None, :]
    chip_of = (z - block) % count
    here = ((chip_of * 2 + core) * per_device + inner).reshape(rows)
    there = ((chip_of * 2 + 1 - core) * per_device + inner).reshape(rows)
    key_extra = key_lanes(jnp.concatenate([here, there]) < length)
    live = (here < length).astype(F32)[:, None]
    core_id = core.astype(jnp.int32).reshape(1)

    outer, middle = pack_weights(weights, is_out_projection(z, core))
    vector = jnp.pad(vectors.astype(BF), (0, EXTRA * D // 2 - vectors.shape[0])).reshape(-1, D)
    other, other_vector = swap(middle), swap(vector)
    whole, piece = own_pieces(outer, other, vector, other_vector, z, core)
    if by_hand():
        x_parts = [to_chip(tokens, z, n) for n in (0, 2)]
        piece, whole, x_parts, tokens = wait(piece, whole, x_parts, tokens)
        up1 = along_z(piece, [(0, 1), (1, 2), (2, 3)])
        down1 = along_z(piece, [(1, 0), (2, 1), (3, 2)])
        up1, down1, whole = wait(up1, down1, whole)
        mine = jnp.where(z == 0, down1, up1)
        got = across(1, mine), across(2, mine)
        up2 = along_z(up1, [(1, 2)])
        down2 = along_z(down1, [(1, 0), (2, 1)])
        mine, got, up1, up2, down1, down2 = wait(mine, got, up1, up2, down1, down2)
        far = across(2, got[0][:, :HALF]), across(1, got[1][:, HALF:])
        up3 = along_z(up2, [(2, 3)])
        mine, got, far, up1, up2, up3, down1, down2 = wait(
            mine, got, far, up1, up2, up3, down1, down2
        )
        mine2 = pick(z, [down2, down1, up2, up3])
        got2 = across(1, mine2), across(2, mine2)
        up4 = along_z(up1, [(2, 3)])
        down3 = along_z(down2, [(1, 0)])
        whole = place(whole, pick(z, [1, 0, 1, 2]), (mine, *got, *far))
        mine, got, up4, down1, down2, down3, whole, tokens = wait(
            mine2, got2, up4, down1, down2, down3, whole, tokens
        )
        far = across(2, got[0][:, :HALF]), across(1, got[1][:, HALF:])
        x_parts += [to_chip(tokens, z, n) for n in (1, 3)]
        mine, got, far, up4, down1, down2, down3, whole, x_parts, cotangent = wait(
            mine, got, far, up4, down1, down2, down3, whole, x_parts, cotangent
        )
        x_mine = jnp.concatenate([x_parts[n] for n in (0, 2, 1, 3)], axis=0)
        x_other = swap(x_mine)
        mine3 = pick(z, [down3, down2, down1, up4])
        got3 = across(1, mine3), across(2, mine3)
        grad_parts = [to_chip(cotangent, z, n) for n in (0, 1)]
        whole = place(whole, pick(z, [2, 2, 0, 0]), (mine, *got, *far))
        vec = vectors_of(whole, vectors.shape[0], 1).reshape(-1, PAIR)
        merged = project(core_id, x_mine, x_other, whole, vec)
        mine, got, whole, merged, grad_parts, cotangent = wait(
            mine3, got3, whole, merged, grad_parts, cotangent
        )
        far = across(2, got[0][:, :HALF]), across(1, got[1][:, HALF:])
        grad_parts += [to_chip(cotangent, z, n) for n in (2, 3)]
        heads_out, extra = attention_forward(merged, key_extra, rows * 2, 0, HALF // PAIR)
        mine, got, far, whole, heads_out, extra, grad_parts = wait(
            mine, got, far, whole, heads_out, extra, grad_parts
        )
        whole = place(whole, pick(z, [3, 3, 3, 1]), (mine, *got, *far))
        vec = vectors_of(whole, vectors.shape[0], count)
    else:
        whole = gather_pieces_of_all(whole, z)
        vec = vectors_of(whole, vectors.shape[0], count)
        x_mine = to_chips(tokens, z)
        x_other = swap(x_mine)
        grad_parts = [to_chip(cotangent, z, n) for n in range(count)]
        merged = project(core_id, x_mine, x_other, whole, vec.reshape(-1, PAIR))
        heads_out, extra = attention_forward(merged, key_extra, 2 * rows, 0, HALF // PAIR)
    grad_out = jnp.concatenate(grad_parts, axis=0)
    bounds = [0, D, 2 * D, 3 * D, 3 * D + FF] + [(n + 4) * D + FF for n in range(6)]
    _, _, bias_o, _, bias_down, gain_one, shift_one, gain_two, shift_two = (
        vec[bounds[n] : bounds[n + 1]] for n in range(9)
    )
    vec = vec.reshape(-1, PAIR)
    w_out = whole[QUARTERS : 2 * QUARTERS, :PAIR].reshape(HALF, D)

    normed_in, normed_one, inverse_one = layer_norm(
        x_mine.astype(F32) + share(plain_dot(heads_out, w_out)) + bias_o, gain_one, shift_one
    )
    u_mine = normed_in.astype(BF)
    u_other = swap(u_mine)
    hidden, slope, feed, feed_other = feed_forward(core_id, u_mine, u_other, whole, vec)
    feed = feed + swap(feed_other).astype(F32) + bias_down
    result, normed_two, inverse_two = layer_norm(u_mine.astype(F32) + feed, gain_two, shift_two)
    layer_out = result.astype(BF)

    grad_out = grad_out.astype(F32) * live
    grad_two, grad_gain_two, grad_shift_two = norm_back(grad_out, normed_two, inverse_two, gain_two)
    df_mine = grad_two.astype(BF)
    grad_bias_down = jnp.sum(df_mine.astype(F32), axis=0)
    grads_ff, grad_bias_up, du, du_other = feed_backward(
        df_mine, swap(df_mine), u_mine, u_other, hidden, slope, whole
    )
    sum_ff = sum_over_dp(grads_ff)
    du = du + swap(du_other).astype(F32) + grad_two
    grad_one, grad_gain_one, grad_shift_one = norm_back(du, normed_one, inverse_one, gain_one)
    da_mine = grad_one.astype(BF)
    da = both(da_mine)
    grad_bias_o = jnp.sum(da_mine.astype(F32), axis=0)
    do = rows_dot(da, w_out).astype(BF)
    grad_wo = cols_dot(heads_out, da).astype(BF)
    do, layer_out = lax.optimization_barrier((do, layer_out))
    layer_out = from_chips(layer_out, z)
    d_merged = attention_backward(merged, extra, key_extra, heads_out, do, rows)
    d_merged, layer_out = lax.optimization_barrier((d_merged, layer_out))
    d_merged, x_mine, x_other = wait(d_merged, x_mine, x_other)
    grad_qkv = cols_dot(d_merged, jnp.concatenate([x_mine, x_other], axis=0)).astype(BF)
    sums = jnp.sum(d_merged.astype(F32), axis=0).reshape(QUARTERS, 3, PAIR)
    vector_grad = jnp.concatenate(
        [
            spread_part(sums[:, 0], core, 1),
            spread_part(sums[:, 2], core, 1),
            grad_bias_o,
            spread_part(grad_bias_up.reshape(QUARTERS, 4, PAIR).swapaxes(0, 1), core, 4),
            grad_bias_down,
            grad_gain_one,
            grad_shift_one,
            grad_gain_two,
            grad_shift_two,
        ]
    ).astype(BF)
    shares = vector_grad.reshape(count, dp_count, -1).swapaxes(0, 1)
    if by_hand():
        shares = jnp.pad(shares, ((0, 0), (0, EXTRA - count), (0, D - shares.shape[2])))
    else:
        shares = jnp.pad(shares, ((0, 0), (0, 0), (0, EXTRA * D - shares.shape[2])))
        shares = shares.reshape(dp_count, count * EXTRA, D)
    run = PAIR * QUARTERS // dp_count
    late = jnp.concatenate(
        [
            jnp.concatenate(
                [grad_qkv.reshape(QUARTERS, 3 * PAIR, D), grad_wo.reshape(QUARTERS, PAIR, D)], axis=1
            )
            .reshape(QUARTERS, 4, dp_count // QUARTERS, run, D)
            .swapaxes(1, 2)
            .reshape(dp_count, 4 * run, D),
            shares,
        ],
        axis=1,
    )
    if by_hand():
        late, d_merged, whole = wait(late, d_merged, whole)
        grad_rows = token_grads(d_merged, whole, grad_one)
        chips, parts, grad_rows = reduce_late(late, sum_ff, grad_rows)
        piece = lax.psum_scatter(chips, "z", scatter_dimension=0, tiled=True)
        piece, grad_rows, parts = wait(piece, grad_rows, parts)
        values, grad_tokens = gather_pieces(piece, grad_rows, parts, z)
        start = jnp.where(core == 0, 2 * PAIR, 0)
        sent = jnp.stack(
            [lax.dynamic_slice_in_dim(value, start, PAIR, 0) for value in values[:3]]
            + [
                jnp.concatenate(
                    [lax.dynamic_slice_in_dim(value, start, PAIR, 0) for value in values[3:]], axis=1
                )
            ]
        )
        middle = swap(sent)
        share_size = vectors.shape[0] // 2
        found = [lax.dynamic_slice_in_dim(value, 3 * PAIR + z, 1, 0) for value in values[:4]]
        last = lax.dynamic_slice_in_dim(values[4], 3 * PAIR + z, 1, 0)
        found[3] = jnp.concatenate([found[3], last], axis=1)
        d = lax.axis_index("dp")
        found = jnp.stack([item[0, :share_size] for item in found])
        found = jnp.where(d % 2 == 1, jnp.stack([found[n ^ 1] for n in range(4)]), found)
        found = jnp.where(d >= 2, jnp.stack([found[n ^ 2] for n in range(4)]), found)
        halves = found.reshape(2, -1).astype(F32)
        kept, given = (
            jnp.where(core == 0, halves[0], halves[1]), jnp.where(core == 0, halves[1], halves[0])
        )
        shard_v = kept + swap(given)
        shard_w, weight_change, new_first_weights, new_second_weights = update_weights(
            values, middle, weights, first_weights, second_weights,
            is_out_projection(z, core), core,
        )
    else:
        grad_tokens = from_chips(token_grads(d_merged, whole, grad_one), z)
        sum_late = lax.psum_scatter(late.reshape(-1, D), "dp", scatter_dimension=0, tiled=True)
        parts = [sum_late[n * run : (n + 1) * run] for n in range(4)]
        parts += [sum_ff[n * run : (n + 1) * run] for n in range(8)]
        spare = sum_late[4 * run :].reshape(count, EXTRA, D)
        chips = [
            jnp.concatenate([*parts[3 * chip : 3 * chip + 3], spare[chip]], axis=0)
            for chip in range(count)
        ]
        piece = lax.psum_scatter(
            jnp.concatenate(chips, axis=0), "z", scatter_dimension=0, tiled=True
        )
        summed = lax.all_gather(piece, "dp", axis=0, tiled=True).reshape(dp_count, -1, D)
        blocks = summed[:, : 3 * run].reshape(dp_count, 3, run, D).swapaxes(0, 1).reshape(3, BLOCK, D)
        share_size = vectors.shape[0] * 2 // dp_count
        vector_sum = summed[:, 3 * run :].reshape(dp_count, -1)
        start = 0
        vector_sum = lax.dynamic_slice_in_dim(vector_sum, start, share_size, 1)
        vector_sum = vector_sum.reshape(2, -1).astype(F32)
        vector_sum = jnp.pad(vector_sum, ((0, 0), (0, 2 * D - vector_sum.shape[1])))
        shard_v = vector_sum[core] + swap(vector_sum[1 - core])
        shard_v = shard_v[: vectors.shape[0]]
        a, b, c = blocks
        middle = swap(jnp.where(core == 0, c, a))
        top = jnp.concatenate([jnp.where(core == 0, a, b), middle], axis=0)
        top = jnp.where(is_out_projection(z, core), top.T, top)
        shard_w = jnp.concatenate([top, jnp.where(core == 0, b, c)], axis=0).astype(F32)

        weight_change, new_first_weights, new_second_weights = adamw_update(
            weights, shard_w, first_weights, second_weights, 0.01
        )
    vector_change, new_first_vectors, new_second_vectors = adamw_update(
        vectors, shard_v, first_vectors, second_vectors, 0.0
    )
    return (
        layer_out,
        grad_tokens,
        shard_w,
        shard_v,
        weight_change,
        vector_change,
        new_first_weights,
        new_second_weights,
        new_first_vectors,
        new_second_vectors,
    )


def solution(mesh):
    chips = Mesh(
        mesh.devices.reshape(mesh.shape["dp"], mesh.shape["ctx"] // 2, 2), ("dp", "z", "core")
    )
    ctx = ("z", "core")
    activations, matrix, vector = P("dp", ctx, None), P(ctx, None), P(ctx)
    return jax.shard_map(
        shards,
        mesh=chips,
        in_specs=(activations, activations, P("dp"), matrix, vector, matrix, matrix, vector, vector),
        out_specs=(
            activations,
            activations,
            matrix,
            vector,
            matrix,
            vector,
            matrix,
            matrix,
            vector,
            vector,
        ),
        check_vma=False,
    )
```

```python
import math

import jax
import jax.numpy as jnp
from jax import lax
from jax.experimental import pallas as pl
from jax.experimental.pallas import tpu as pltpu
from jax.sharding import Mesh
from jax.sharding import PartitionSpec as P

D = 1024
FF = 4096
HD = 64
PAIR = 2 * HD
STEP = 10
EPSILON = 1e-05
LEARN_RATE = 0.003
BF = jnp.bfloat16
F32 = jnp.float32
HALF = D // 2
BLOCK = 512
EXTRA = 16
QUARTERS = 4
PIECE = 3 * PAIR + EXTRA
VMEM = 60 * 2**20
SCALAR = pl.BlockSpec(memory_space=pltpu.SMEM)
NO_COST = pl.CostEstimate(flops=1, bytes_accessed=1, transcendentals=0)


def rows_dot(operand, matrix):
    return lax.dot_general(operand, matrix, (((1,), (1,)), ((), ())), preferred_element_type=F32)


def cols_dot(operand, matrix):
    return lax.dot_general(operand, matrix, (((0,), (0,)), ((), ())), preferred_element_type=F32)


def plain_dot(operand, matrix):
    return lax.dot_general(operand, matrix, (((1,), (0,)), ((), ())), preferred_element_type=F32)


def swap(value):
    return lax.ppermute(value, "core", [(0, 1), (1, 0)])


def layer_norm(inputs, gain_vec, shift_vec):
    centre = jnp.mean(inputs, axis=-1, keepdims=True)
    shifted = inputs - centre
    inverse = lax.rsqrt(jnp.mean(shifted * shifted, axis=-1, keepdims=True) + EPSILON)
    normed = shifted * inverse
    return (normed * gain_vec + shift_vec, normed, inverse)


def norm_back(grad_out, normed, inverse, gain_vec):
    scaled = grad_out * gain_vec
    inner_term = (
        scaled
        - jnp.mean(scaled, axis=-1, keepdims=True)
        - normed * jnp.mean(scaled * normed, axis=-1, keepdims=True)
    )
    return (inverse * inner_term, jnp.sum(grad_out * normed, axis=0), jnp.sum(grad_out, axis=0))


def to_chip(blocks, z, shift):
    count = lax.axis_size("z")
    part = lax.dynamic_index_in_dim(blocks, (z + shift) % count, 0, keepdims=False)
    if shift:
        part = lax.ppermute(part, "z", [(i, (i + shift) % count) for i in range(count)])
    return part


def to_chips(blocks, z):
    return jnp.concatenate([to_chip(blocks, z, n) for n in range(lax.axis_size("z"))], axis=0)


def from_chip(rows, shift):
    count = lax.axis_size("z")
    part = rows.reshape(count, -1, rows.shape[-1])[shift]
    if shift:
        part = lax.ppermute(part, "z", [(i, (i - shift) % count) for i in range(count)])
    return part


def put_together(parts, z):
    count = lax.axis_size("z")
    result = jnp.zeros((count, *parts[0].shape), BF)
    for shift in range(count):
        result = lax.dynamic_update_index_in_dim(result, parts[shift], (z + shift) % count, 0)
    return result


def from_chips(rows, z):
    return put_together([from_chip(rows, n) for n in range(lax.axis_size("z"))], z)


def is_out_projection(z, core):
    return jnp.logical_and(z == 1, core == 0)


def pack_kernel(flag_ref, rows_ref, columns_ref, outer_ref, middle_ref):
    step = pl.program_id(0)
    turned = jnp.logical_and(flag_ref[0] == 1, step < 2)

    def write(value):
        @pl.when(step != 1)
        def _():
            outer_ref[...] = value

        @pl.when(step == 1)
        def _():
            middle_ref[...] = value

    @pl.when(turned)
    def _():
        write(columns_ref[...].T.astype(BF))

    @pl.when(jnp.logical_not(turned))
    def _():
        write(rows_ref[...].astype(BF))


def pack_weights(weights, flag):
    return pl.pallas_call(
        pack_kernel,
        grid_spec=pltpu.PrefetchScalarGridSpec(
            num_scalar_prefetch=1,
            grid=(3,),
            in_specs=[
                pl.BlockSpec((BLOCK, D), lambda n, flag: (n, 0)),
                pl.BlockSpec((D, BLOCK), lambda n, flag: (0, jnp.minimum(n, 1) * flag[0])),
            ],
            out_specs=[
                pl.BlockSpec((BLOCK, D), lambda n, flag: (n // 2, 0)),
                pl.BlockSpec((BLOCK, D), lambda n, flag: (0, 0)),
            ],
        ),
        out_shape=[
            jax.ShapeDtypeStruct((2 * BLOCK, D), BF),
            jax.ShapeDtypeStruct((BLOCK, D), BF),
        ],
        cost_estimate=NO_COST,
        compiler_params=pltpu.CompilerParams(vmem_limit_bytes=VMEM),
    )(flag.astype(jnp.int32).reshape(1), weights, weights)


def own_kernel(
    where_ref, first_ref, last_ref, other_ref, mine_vector, other_vector, whole_ref, piece_ref
):
    core = where_ref[2]

    def write(parts, vectors):
        value = jnp.concatenate([*parts, *vectors], axis=0)
        whole_ref[0] = value

        @pl.when(pl.program_id(0) == 0)
        def _():
            piece_ref[...] = value

    first, last, other = first_ref[...], last_ref[...], other_ref[...]
    vectors = [mine_vector[...], other_vector[...]]

    @pl.when(core == 0)
    def _():
        write([first, last, other], vectors)

    @pl.when(core == 1)
    def _():
        write([other, first, last], vectors[::-1])


def own_pieces(outer, other, vector, other_vector, z, core):
    where = jnp.stack([z, lax.axis_index("dp") % QUARTERS, core]).astype(jnp.int32)
    run = (PAIR, D)
    small = pl.BlockSpec(vector.shape, lambda n, where: (0, 0))
    return pl.pallas_call(
        own_kernel,
        grid_spec=pltpu.PrefetchScalarGridSpec(
            num_scalar_prefetch=1,
            grid=(QUARTERS,),
            in_specs=[
                pl.BlockSpec(run, lambda n, where: (where[1] ^ n, 0)),
                pl.BlockSpec(run, lambda n, where: (QUARTERS + (where[1] ^ n), 0)),
                pl.BlockSpec(run, lambda n, where: (where[1] ^ n, 0)),
                small,
                small,
            ],
            out_specs=[
                pl.BlockSpec(
                    (1, PIECE, D), lambda n, where: (where[0] * QUARTERS + (where[1] ^ n), 0, 0)
                ),
                pl.BlockSpec((PIECE, D), lambda n, where: (0, 0)),
            ],
        ),
        out_shape=[
            jax.ShapeDtypeStruct((4 * QUARTERS, PIECE, D), BF),
            jax.ShapeDtypeStruct((PIECE, D), BF),
        ],
        cost_estimate=NO_COST,
        compiler_params=pltpu.CompilerParams(vmem_limit_bytes=VMEM),
    )(where, outer, outer, other, vector, other_vector)


def gather_pieces_of_all(whole, z):
    count = lax.axis_size("dp") // QUARTERS
    mine = lax.dynamic_slice_in_dim(whole, z * QUARTERS, QUARTERS, 0)
    share = lax.dynamic_index_in_dim(mine, lax.axis_index("dp") // count, 0, keepdims=False)
    blocks = share[: 3 * PAIR].reshape(3, PAIR, D)
    blocks = lax.dynamic_slice_in_dim(
        blocks, lax.axis_index("dp") % count * (PAIR // count), PAIR // count, 1
    )
    everything = lax.all_gather(blocks.reshape(-1, D), ("z", "dp"), axis=0, tiled=True)
    everything = everything.reshape(-1, count, 3, PAIR // count, D).swapaxes(1, 2)
    spare = lax.all_gather(share[3 * PAIR :], "z", axis=0, tiled=True).reshape(-1, 1, EXTRA, D)
    spare = jnp.broadcast_to(spare, (spare.shape[0], QUARTERS, EXTRA, D)).reshape(-1, EXTRA, D)
    return jnp.concatenate([everything.reshape(-1, 3 * PAIR, D), spare], axis=1)


def vectors_of(whole, size, chips):
    found = jnp.stack([whole[QUARTERS * chip, 3 * PAIR :] for chip in range(chips)])
    return found.reshape(-1, 2, EXTRA * D // 2)[:, :, :size].reshape(-1).astype(F32)


def place_kernel(where_ref, whole_in, mine, got_x, got_y, far_a, far_b, whole_ref):
    del where_ref, whole_in
    for index, source in enumerate((mine, got_x, got_y)):

        @pl.when(pl.program_id(0) == index)
        def _(source=source):
            whole_ref[0] = source[...]

    @pl.when(pl.program_id(0) == 3)
    def _():
        whole_ref[0, :, :HALF] = far_a[...]
        whole_ref[0, :, HALF:] = far_b[...]


def place(whole, shard, values):
    where = jnp.stack([shard, lax.axis_index("dp")]).astype(jnp.int32)
    return pl.pallas_call(
        place_kernel,
        grid_spec=pltpu.PrefetchScalarGridSpec(
            num_scalar_prefetch=1,
            grid=(4,),
            in_specs=[pl.BlockSpec(memory_space=pl.ANY)]
            + [pl.BlockSpec(value.shape, lambda n, where: (0, 0)) for value in values],
            out_specs=pl.BlockSpec(
                (1, PIECE, D), lambda n, where: (where[0] * QUARTERS + (where[1] ^ n), 0, 0)
            ),
        ),
        out_shape=jax.ShapeDtypeStruct(whole.shape, BF),
        input_output_aliases={1: 0},
        cost_estimate=NO_COST,
        compiler_params=pltpu.CompilerParams(vmem_limit_bytes=VMEM),
    )(where, whole, *values)


def sum_over_dp(grads):
    count = lax.axis_size("dp") // QUARTERS
    if count > 1:
        grads = grads.reshape(QUARTERS, -1, count, PAIR // count, D).swapaxes(1, 2)
    return lax.psum_scatter(grads.reshape(-1, D), "dp", scatter_dimension=0, tiled=True)


def by_hand():
    return lax.axis_size("dp") == 4 and lax.axis_size("z") == 4


def plus(first, second):
    return (first.astype(F32) + second.astype(F32)).astype(BF)


def across(bit, value):
    return lax.ppermute(value, "dp", [(i, i ^ bit) for i in range(4)])


def at(value, index, axis):
    return lax.dynamic_index_in_dim(value, index, axis, keepdims=False)


def along_z(value, pairs):
    return lax.ppermute(value, "z", pairs)


def pick(z, values):
    result = values[-1]
    for index in range(len(values) - 2, -1, -1):
        result = jnp.where(z == index, values[index], result)
    return result


def wait(*values):
    return lax.optimization_barrier(values)


def assemble_kernel(where_ref, a, got_a, far_a, b, got_b, far_b, sums_ref, out_ref):
    chip = pl.program_id(0)
    rows = 3 * PAIR

    def write(target, source):
        for index, (mine, got, far, columns) in enumerate(
            ((a, got_a, far_a, slice(None, HALF)), (b, got_b, far_b, slice(HALF, None)))
        ):
            side = where_ref[index]
            value = plus(plus(mine[side, source], got[side, source]), far[source])
            out_ref[target, columns] = value

    write(slice(rows, None), slice(4 * PAIR, None))

    @pl.when(chip == 0)
    def _():
        write(slice(None, rows), slice(None, rows))

    @pl.when(chip == 1)
    def _():
        write(slice(None, PAIR), slice(rows, rows + PAIR))
        out_ref[PAIR:rows] = sums_ref[: 2 * PAIR]

    @pl.when(chip == 2)
    def _():
        out_ref[:rows] = sums_ref[2 * PAIR : 5 * PAIR]

    @pl.when(chip == 3)
    def _():
        out_ref[:rows] = sums_ref[5 * PAIR :]


def assemble(x, y, late, sums):
    return pl.pallas_call(
        assemble_kernel,
        grid=(4,),
        in_specs=[SCALAR] + [whole_block(item.shape) for item in (*late, sums)],
        out_specs=pl.BlockSpec((PIECE, D), lambda chip: (chip, 0)),
        out_shape=jax.ShapeDtypeStruct((4 * PIECE, D), BF),
        cost_estimate=NO_COST,
        compiler_params=pltpu.CompilerParams(vmem_limit_bytes=VMEM),
    )(jnp.stack([y, x]).astype(jnp.int32), *late, sums)


def reduce_late(late, sum_ff, grad_rows):
    d = lax.axis_index("dp")
    x, y = d % 2, d // 2
    late = late.reshape(2, 2, -1, D)
    a, b = late[..., :HALF], late[..., HALF:]
    got_a, got_b = across(1, at(a, 1 - x, 1)), across(2, at(b, 1 - y, 0))
    got_a, got_b, a, b, sum_ff, grad_rows = wait(got_a, got_b, a, b, sum_ff, grad_rows)
    a, b = at(a, x, 1), at(b, y, 0)
    far_a = across(2, plus(at(a, 1 - y, 0), at(got_a, 1 - y, 0)))
    far_b = across(1, plus(at(b, 1 - x, 0), at(got_b, 1 - x, 0)))
    parts = {n: from_chip(grad_rows, n) for n in (0, 1)}
    far_a, far_b, a, b, parts, grad_rows = wait(far_a, far_b, a, b, parts, grad_rows)
    return assemble(x, y, (a, got_a, far_a, b, got_b, far_b), sum_ff), parts, grad_rows


def gather_pieces(piece, grad_rows, parts, z):
    got = across(1, piece), across(2, piece)
    parts = {**parts, **{n: from_chip(grad_rows, n) for n in (2, 3)}}
    got, piece, parts = wait(got, piece, parts)
    far = across(2, got[0][:, :HALF]), across(1, got[1][:, HALF:])
    grad_tokens = put_together(parts, z)
    far, got, piece, grad_tokens = wait(far, got, piece, grad_tokens)
    return (piece, *got, *far), grad_tokens


def update_kernel(
    where_ref, mine, got_x, got_y, far_a, far_b, middle_ref, weight_ref, first_ref, second_ref,
    grad_ref, change_ref, first_out, second_out,
):
    d, core, turned = where_ref[0], where_ref[1], where_ref[2] == 1
    block, pair = pl.program_id(0), pl.program_id(1)
    pieces = (mine, got_x, got_y)
    rows = pl.ds(pl.multiple_of((core + block // 2) * PAIR, PAIR), PAIR)
    plain = jnp.logical_and(block != 1, jnp.logical_or(block == 2, jnp.logical_not(turned)))
    for n in range(QUARTERS):
        slot = pl.ds(pl.multiple_of((d % 2 ^ (n % 2)) * PAIR, PAIR), PAIR)
        ours = pair == n // 2

        @pl.when(ours & (block == 1) & jnp.logical_not(turned))
        def _(n=n, slot=slot):
            grad_ref[slot, :] = middle_ref[n].astype(F32)

        @pl.when(ours & plain)
        def _(n=n, slot=slot):
            if n < 3:
                grad_ref[slot, :] = pieces[n][rows, :].astype(F32)
            else:
                grad_ref[slot, :HALF] = far_a[rows, :].astype(F32)
                grad_ref[slot, HALF:] = far_b[rows, :].astype(F32)

        @pl.when(ours & (block < 2) & turned)
        def _(n=n, slot=slot):
            start = pl.multiple_of((d ^ n) * PAIR, PAIR)
            columns = pl.ds(pl.multiple_of(block * HALF + start, PAIR), PAIR)
            for m in range(QUARTERS):
                low = pl.ds(pl.multiple_of((d ^ m) * PAIR, PAIR), PAIR)
                high = pl.ds(pl.multiple_of(HALF + (d ^ m) * PAIR, PAIR), PAIR)
                grad_ref[slot, high] = middle_ref[m, :, columns].astype(F32).T
                if m < 3:
                    grad_ref[slot, low] = pieces[m][:PAIR, columns].astype(F32).T
            low = pl.ds(pl.multiple_of((d ^ 3) * PAIR, PAIR), PAIR)
            for half, far in enumerate((far_a, far_b)):

                @pl.when(block == half)
                def _(far=far):
                    grad_ref[slot, low] = far[:PAIR, pl.ds(start, PAIR)].astype(F32).T

    change_ref[...], first_out[...], second_out[...] = adamw_update(
        weight_ref[...], grad_ref[...], first_ref[...], second_ref[...], 0.01
    )


def update_weights(values, middle, weights, first_weights, second_weights, turned, core):
    d = lax.axis_index("dp")
    where = jnp.stack([d, core, turned.astype(jnp.int32)]).astype(jnp.int32)
    rows = pl.BlockSpec((2 * PAIR, D), lambda b, n, where: (b * 2 + (where[0] // 2 ^ n), 0))
    return pl.pallas_call(
        update_kernel,
        grid_spec=pltpu.PrefetchScalarGridSpec(
            num_scalar_prefetch=1,
            grid=(3, 2),
            in_specs=[pl.BlockSpec(value.shape, lambda b, n, where: (0, 0)) for value in values]
            + [pl.BlockSpec(middle.shape, lambda b, n, where: (0, 0, 0))]
            + [rows] * 3,
            out_specs=[rows] * 4,
        ),
        out_shape=[jax.ShapeDtypeStruct(weights.shape, F32)] * 4,
        cost_estimate=NO_COST,
        compiler_params=pltpu.CompilerParams(vmem_limit_bytes=VMEM),
    )(where, *values, middle, weights, first_weights, second_weights)


def lanes_of(shape, head):
    lane = lax.broadcasted_iota(jnp.int32, shape, 1)
    return (lane >= HD) if head else (lane < HD), lane - HD * (1 - head)


def split_three(value):
    high = value.astype(BF).astype(F32)
    mid = (value - high).astype(BF).astype(F32)
    return high, mid, (value - high - mid).astype(BF).astype(F32)


def spread_lanes(place, values):
    result = jnp.zeros(place.shape, F32)
    for lane, value in enumerate(values):
        result = jnp.where(place == lane, value, result)
    return result


def whole_block(shape):
    return pl.BlockSpec(shape, lambda *_: (0,) * len(shape))


def qkv_kernel(core_ref, x_mine, x_other, w_ref, vector_ref, out_ref):
    quarter = pl.program_id(0)
    row = core_ref[0] * QUARTERS + quarter
    bias_q = vector_ref[pl.ds(row, 1), :]
    bias_v = vector_ref[pl.ds(D // PAIR + row, 1), :]
    bias = jnp.concatenate([bias_q, jnp.zeros_like(bias_q), bias_v], axis=1)
    half = x_mine.shape[0]
    out_ref[:half] = (rows_dot(x_mine[...], w_ref[0]) + bias).astype(BF)
    out_ref[half:] = (rows_dot(x_other[...], w_ref[0]) + bias).astype(BF)


def project(core, x_mine, x_other, whole, vec):
    rows = 2 * x_mine.shape[0]
    return pl.pallas_call(
        qkv_kernel,
        grid=(QUARTERS,),
        in_specs=[
            SCALAR,
            whole_block(x_mine.shape),
            whole_block(x_mine.shape),
            pl.BlockSpec((1, 3 * PAIR, D), lambda quarter: (quarter, 0, 0)),
            whole_block(vec.shape),
        ],
        out_specs=pl.BlockSpec((rows, 3 * PAIR), lambda quarter: (0, quarter)),
        out_shape=jax.ShapeDtypeStruct((rows, 3 * HALF), BF),
        cost_estimate=NO_COST,
        compiler_params=pltpu.CompilerParams(vmem_limit_bytes=VMEM),
    )(core, x_mine, x_other, whole, vec)


def forward_kernel(q_ref, k_ref, v_ref, key_ref, o_ref, extra_ref):
    q, k, v, key_extra = q_ref[...], k_ref[...], v_ref[...], key_ref[...]
    outs, extras = [], []
    for head in range(2):
        in_q, place_q = lanes_of(q.shape, head)
        in_k, place_k = lanes_of(k.shape, head)
        keys = jnp.where(in_k, k, key_extra)
        queries = jnp.where(in_q, q * BF(0.125), jnp.where(place_q == 0, BF(1), BF(0)))
        values = jnp.where(in_k, v, jnp.where(place_k == 0, BF(1), BF(0)))
        scores = rows_dot(queries, keys)
        highest = jnp.max(scores, axis=1, keepdims=True)
        terms = jnp.exp(scores - highest).astype(BF)
        out = plain_dot(terms, values)
        column = HD * (1 - head)
        total = out[:, column : column + 1]
        outs.append(out * (1.0 / total))
        parts = split_three(-(highest + jnp.log(total)))
        extras.append(spread_lanes(place_q, (1.0, *parts)))
    in_first, _ = lanes_of(q.shape, 0)
    o_ref[...] = jnp.where(in_first, outs[0], outs[1]).astype(BF)
    extra_ref[...] = jnp.where(in_first, extras[1], extras[0]).astype(BF)


def forward_more_kernel(q_ref, k_ref, v_ref, key_ref, o_in, extra_in, o_ref, extra_ref):
    del o_in, extra_in
    forward_kernel(q_ref, k_ref, v_ref, key_ref, o_ref, extra_ref)


def attention_forward(merged, key_extra, step, start, pairs, done=()):
    rows = merged.shape[0]
    some = pl.BlockSpec((step, PAIR), lambda pair, part: (part, 3 * (pair + start)))
    ours = pl.BlockSpec((step, PAIR), lambda pair, part: (part, pair + start))
    keys = pl.BlockSpec((rows, PAIR), lambda pair, part: (0, 3 * (pair + start) + 1))
    values = pl.BlockSpec((rows, PAIR), lambda pair, part: (0, 3 * (pair + start) + 2))
    return pl.pallas_call(
        forward_more_kernel if done else forward_kernel,
        grid=(pairs, rows // step),
        in_specs=[some, keys, values, whole_block(key_extra.shape)]
        + [pl.BlockSpec(memory_space=pl.ANY)] * len(done),
        out_specs=[ours, ours],
        out_shape=[jax.ShapeDtypeStruct((rows, HALF), BF)] * 2,
        input_output_aliases={4: 0, 5: 1} if done else {},
        cost_estimate=NO_COST,
        compiler_params=pltpu.CompilerParams(vmem_limit_bytes=VMEM),
    )(merged, merged, merged, key_extra, *done)


def backward_kernel(
    q_ref, extra_ref, k_ref, v_ref, key_ref, o_ref, do_ref, out_ref, dk_sum, dv_sum
):
    part = pl.program_id(1)
    q, extra, k, v = q_ref[...], extra_ref[...], k_ref[...], v_ref[...]
    key_extra, do = key_ref[...], do_ref[...]
    product = do.astype(F32) * o_ref[...].astype(F32)
    zero = BF(0)
    dq = dk = dv = 0.0
    for head in range(2):
        in_q, place_q = lanes_of(q.shape, head)
        in_k, place_k = lanes_of(k.shape, head)
        scaled = jnp.where(in_q, q * BF(0.125), zero)
        queries = jnp.where(in_q, scaled, extra)
        keys = jnp.where(in_k, k, key_extra)
        only_k = jnp.where(in_k, k, zero)
        only_do = jnp.where(in_q, do, zero)
        row_sum = jnp.sum(jnp.where(in_q, product, 0.0), axis=1, keepdims=True)
        grads = jnp.where(in_q, do, spread_lanes(place_q, split_three(-row_sum)).astype(BF))
        ones = jnp.where((place_k >= 0) & (place_k < 3), BF(1), zero)
        values = jnp.where(in_k, v, ones)
        probs = jnp.exp(rows_dot(keys, queries))
        grad_scores = (probs * rows_dot(values, grads)).astype(BF)
        dv = dv + plain_dot(probs.astype(BF), only_do)
        dk = dk + plain_dot(grad_scores, scaled)
        dq = dq + cols_dot(grad_scores, only_k)
    step = q.shape[0]
    out_ref[pl.ds(part * step, step), :PAIR] = (dq * 0.125).astype(BF)

    @pl.when(part == 0)
    def _():
        dk_sum[...] = dk
        dv_sum[...] = dv

    @pl.when(part > 0)
    def _():
        dk_sum[...] += dk
        dv_sum[...] += dv

    @pl.when(part == pl.num_programs(1) - 1)
    def _():
        out_ref[:, PAIR : 2 * PAIR] = dk_sum[...].astype(BF)
        out_ref[:, 2 * PAIR :] = dv_sum[...].astype(BF)


def attention_backward(merged, extra, key_extra, heads_out, grad_out, step):
    rows = merged.shape[0]
    some = pl.BlockSpec((step, PAIR), lambda pair, part: (part, 3 * pair))
    ours = pl.BlockSpec((step, PAIR), lambda pair, part: (part, pair))
    keys = pl.BlockSpec((rows, PAIR), lambda pair, part: (0, 3 * pair + 1))
    values = pl.BlockSpec((rows, PAIR), lambda pair, part: (0, 3 * pair + 2))
    return pl.pallas_call(
        backward_kernel,
        grid=(HALF // PAIR, rows // step),
        in_specs=[some, ours, keys, values, whole_block(key_extra.shape), ours, ours],
        out_specs=pl.BlockSpec((rows, 3 * PAIR), lambda pair, part: (0, pair)),
        out_shape=jax.ShapeDtypeStruct((rows, 3 * HALF), BF),
        scratch_shapes=[pltpu.VMEM((rows, PAIR), F32)] * 2,
        cost_estimate=NO_COST,
        compiler_params=pltpu.CompilerParams(vmem_limit_bytes=VMEM),
    )(merged, extra, merged, merged, key_extra, heads_out, grad_out)


def key_lanes(allowed):
    lane = jnp.arange(PAIR)[None, :] % HD
    bias = jnp.where(allowed, 0.0, -1e30)[:, None]
    return jnp.where(lane == 0, bias, jnp.where(lane < 4, 1.0, 0.0)).astype(BF)


def weight_block(chip, part, count=1):
    return pl.BlockSpec(
        (1, count * PAIR, D), lambda quarter: (chip * QUARTERS + quarter, part // count, 0)
    )


UP_BLOCKS = (weight_block(1, 1), weight_block(1, 2), weight_block(2, 0, 2))
DOWN_BLOCKS = (weight_block(2, 2), weight_block(3, 0, 3))


def joined(refs):
    return jnp.concatenate([ref[0] for ref in refs], axis=0)


def feed_forward_kernel(
    core_ref, u_mine, u_other, up0, up1, up2, down0, down1, vector_ref,
    hidden_ref, slope_ref, mine_ref, other_ref, total,
):
    quarter = pl.program_id(0)
    rows = [
        vector_ref[pl.ds(3 * D // PAIR + (2 * n + core_ref[0]) * QUARTERS + quarter, 1), :]
        for n in range(4)
    ]
    bias = jnp.concatenate(rows, axis=1)
    up, down = joined((up0, up1, up2)), joined((down0, down1))
    half = mine_ref.shape[0]
    for place, u_ref in ((slice(None, half), u_mine), (slice(half, None), u_other)):
        z = rows_dot(u_ref[...], up) + bias
        cdf = 0.5 * (1.0 + lax.erf(z * (1.0 / math.sqrt(2.0))))
        slope = cdf + z * jnp.exp(-0.5 * z * z) * (1.0 / math.sqrt(2.0 * math.pi))
        hidden = (z * cdf).astype(BF)
        hidden_ref[place, :] = hidden
        slope_ref[place, :] = slope.astype(BF)
        part = plain_dot(hidden, down)

        @pl.when(quarter == 0)
        def _(place=place, part=part):
            total[place, :] = part

        @pl.when(quarter > 0)
        def _(place=place, part=part):
            total[place, :] += part

    @pl.when(quarter == QUARTERS - 1)
    def _():
        mine_ref[...] = total[:half]
        other_ref[...] = total[half:].astype(BF)


def feed_forward(core, u_mine, u_other, whole, vec):
    rows = 2 * u_mine.shape[0]
    columns = pl.BlockSpec((rows, BLOCK), lambda quarter: (0, quarter))
    half = (rows // 2, D)
    return pl.pallas_call(
        feed_forward_kernel,
        grid=(QUARTERS,),
        in_specs=[
            SCALAR, whole_block(half), whole_block(half), *UP_BLOCKS, *DOWN_BLOCKS,
            whole_block(vec.shape),
        ],
        out_specs=[columns, columns, whole_block(half), whole_block(half)],
        out_shape=[
            jax.ShapeDtypeStruct((rows, FF // 2), BF),
            jax.ShapeDtypeStruct((rows, FF // 2), BF),
            jax.ShapeDtypeStruct(half, F32),
            jax.ShapeDtypeStruct(half, BF),
        ],
        scratch_shapes=[pltpu.VMEM((rows, D), F32)],
        cost_estimate=NO_COST,
        compiler_params=pltpu.CompilerParams(vmem_limit_bytes=VMEM),
    )(core, u_mine, u_other, whole, whole, whole, whole, whole, vec)


def out_forward_kernel(o_ref, w0, w1, w2, w3, mine_ref, other_ref):
    part = plain_dot(o_ref[...], joined((w0, w1, w2, w3)))

    @pl.when(pl.program_id(0) == 0)
    def _():
        mine_ref[...] = part

    @pl.when(pl.program_id(0) == 1)
    def _():
        other_ref[...] = part.astype(BF)


def out_forward(heads_out, whole):
    rows = heads_out.shape[0]
    half = (rows // 2, D)

    def run(quarter):
        return pl.BlockSpec((1, PAIR, D), lambda n: (QUARTERS + quarter, 0, 0))

    return pl.pallas_call(
        out_forward_kernel,
        grid=(2,),
        in_specs=[
            pl.BlockSpec((rows // 2, HALF), lambda n: (n, 0)), *[run(q) for q in range(QUARTERS)]
        ],
        out_specs=[whole_block(half), whole_block(half)],
        out_shape=[jax.ShapeDtypeStruct(half, F32), jax.ShapeDtypeStruct(half, BF)],
        cost_estimate=NO_COST,
        compiler_params=pltpu.CompilerParams(vmem_limit_bytes=VMEM),
    )(heads_out, whole, whole, whole, whole)


def feed_backward_kernel(
    df_mine, df_other, u_mine, u_other, hidden_ref, slope_ref, up0, up1, up2, down0, down1,
    grads_ref, bias_ref, mine_ref, other_ref, total,
):
    quarter = pl.program_id(0)
    up, down = joined((up0, up1, up2)), joined((down0, down1))
    half = mine_ref.shape[0]
    grad_up = grad_down = bias = 0.0
    for place, df_ref, u_ref in (
        (slice(None, half), df_mine, u_mine), (slice(half, None), df_other, u_other)
    ):
        df = df_ref[...]
        dz = (rows_dot(df, down) * slope_ref[place, :].astype(F32)).astype(BF)
        bias = bias + jnp.sum(dz.astype(F32), axis=0, keepdims=True)
        grad_up = grad_up + cols_dot(dz, u_ref[...])
        grad_down = grad_down + cols_dot(hidden_ref[place, :], df)
        part = plain_dot(dz, up)

        @pl.when(quarter == 0)
        def _(place=place, part=part):
            total[place, :] = part

        @pl.when(quarter > 0)
        def _(place=place, part=part):
            total[place, :] += part

    bias_ref[...] = bias
    grads_ref[0, :BLOCK] = grad_up.astype(BF)
    grads_ref[0, BLOCK:] = grad_down.astype(BF)

    @pl.when(quarter == QUARTERS - 1)
    def _():
        mine_ref[...] = total[:half]
        other_ref[...] = total[half:].astype(BF)


def feed_backward(df_mine, df_other, u_mine, u_other, hidden, slope, whole):
    rows = 2 * u_mine.shape[0]
    columns = pl.BlockSpec((rows, BLOCK), lambda quarter: (0, quarter))
    half = (rows // 2, D)
    return pl.pallas_call(
        feed_backward_kernel,
        grid=(QUARTERS,),
        in_specs=[
            *[whole_block(half)] * 4, columns, columns, *UP_BLOCKS, *DOWN_BLOCKS
        ],
        out_specs=[
            pl.BlockSpec((1, 2 * BLOCK, D), lambda quarter: (quarter, 0, 0)),
            pl.BlockSpec((1, BLOCK), lambda quarter: (0, quarter)),
            whole_block(half),
            whole_block(half),
        ],
        out_shape=[
            jax.ShapeDtypeStruct((QUARTERS, 2 * BLOCK, D), BF),
            jax.ShapeDtypeStruct((1, FF // 2), F32),
            jax.ShapeDtypeStruct(half, F32),
            jax.ShapeDtypeStruct(half, BF),
        ],
        scratch_shapes=[pltpu.VMEM((rows, D), F32)],
        cost_estimate=NO_COST,
        compiler_params=pltpu.CompilerParams(vmem_limit_bytes=VMEM),
    )(df_mine, df_other, u_mine, u_other, hidden, slope, whole, whole, whole, whole, whole)


def adamw_update(parameter, gradient, first_old, second_old, decay_rate):
    step_float = float(STEP)
    first_new = 0.9 * first_old + 0.1 * gradient
    second_new = 0.999 * second_old + 0.001 * gradient * gradient
    first_fix = first_new * (1.0 / (1.0 - 0.9**step_float))
    second_fix = second_new * (1.0 / (1.0 - 0.999**step_float))
    update = first_fix / (jnp.sqrt(second_fix) + 1e-08)
    return (-LEARN_RATE * (update + decay_rate * parameter), first_new, second_new)


def share(partial):
    half = partial.shape[0] // 2
    return partial[:half] + swap(partial[half:].astype(BF)).astype(F32)


def both(rows):
    return jnp.concatenate([rows, swap(rows)], axis=0)


def spread_part(vector, core, pieces):
    parts = vector.reshape(pieces, 1, -1)
    mine = (jnp.arange(2) == core)[None, :, None]
    return jnp.where(mine, parts, 0.0).reshape(-1)


def token_grads(d_merged, whole, grad_one):
    rows = whole[:QUARTERS, : 3 * PAIR].reshape(-1, D)
    return (share(plain_dot(d_merged, rows)) + grad_one).astype(BF)


def shards(
    tokens,
    cotangent,
    lengths,
    weights,
    vectors,
    first_weights,
    second_weights,
    first_vectors,
    second_vectors,
):
    z, core = lax.axis_index("z"), lax.axis_index("core")
    count, dp_count = lax.axis_size("z"), lax.axis_size("dp")
    per_device = tokens.shape[1]
    rows = count * per_device
    length = lengths[z]
    block = jnp.arange(count, dtype=jnp.int32)[:, None]
    inner = jnp.arange(per_device, dtype=jnp.int32)[None, :]
    chip_of = (z - block) % count
    here = ((chip_of * 2 + core) * per_device + inner).reshape(rows)
    there = ((chip_of * 2 + 1 - core) * per_device + inner).reshape(rows)
    key_extra = key_lanes(jnp.concatenate([here, there]) < length)
    live = (here < length).astype(F32)[:, None]
    core_id = core.astype(jnp.int32).reshape(1)

    outer, middle = pack_weights(weights, is_out_projection(z, core))
    vector = jnp.pad(vectors.astype(BF), (0, EXTRA * D // 2 - vectors.shape[0])).reshape(-1, D)
    other, other_vector = swap(middle), swap(vector)
    whole, piece = own_pieces(outer, other, vector, other_vector, z, core)
    if by_hand():
        x_parts = [to_chip(tokens, z, n) for n in (0, 2)]
        piece, whole, x_parts, tokens = wait(piece, whole, x_parts, tokens)
        up1 = along_z(piece, [(0, 1), (1, 2), (2, 3)])
        down1 = along_z(piece, [(1, 0), (2, 1), (3, 2)])
        up1, down1, whole = wait(up1, down1, whole)
        mine = jnp.where(z == 0, down1, up1)
        got = across(1, mine), across(2, mine)
        up2 = along_z(up1, [(1, 2)])
        down2 = along_z(down1, [(1, 0), (2, 1)])
        mine, got, up1, up2, down1, down2 = wait(mine, got, up1, up2, down1, down2)
        far = across(2, got[0][:, :HALF]), across(1, got[1][:, HALF:])
        up3 = along_z(up2, [(2, 3)])
        mine, got, far, up1, up2, up3, down1, down2 = wait(
            mine, got, far, up1, up2, up3, down1, down2
        )
        mine2 = pick(z, [down2, down1, up2, up3])
        got2 = across(1, mine2), across(2, mine2)
        up4 = along_z(up1, [(2, 3)])
        down3 = along_z(down2, [(1, 0)])
        whole = place(whole, pick(z, [1, 0, 1, 2]), (mine, *got, *far))
        mine, got, up4, down1, down2, down3, whole, tokens = wait(
            mine2, got2, up4, down1, down2, down3, whole, tokens
        )
        far = across(2, got[0][:, :HALF]), across(1, got[1][:, HALF:])
        x_parts += [to_chip(tokens, z, n) for n in (1, 3)]
        mine, got, far, up4, down1, down2, down3, whole, x_parts, cotangent = wait(
            mine, got, far, up4, down1, down2, down3, whole, x_parts, cotangent
        )
        x_mine = jnp.concatenate([x_parts[n] for n in (0, 2, 1, 3)], axis=0)
        x_other = swap(x_mine)
        mine3 = pick(z, [down3, down2, down1, up4])
        got3 = across(1, mine3), across(2, mine3)
        grad_parts = [to_chip(cotangent, z, n) for n in (0, 1)]
        whole = place(whole, pick(z, [2, 2, 0, 0]), (mine, *got, *far))
        vec = vectors_of(whole, vectors.shape[0], 1).reshape(-1, PAIR)
        merged = project(core_id, x_mine, x_other, whole, vec)
        mine, got, whole, merged, grad_parts, cotangent = wait(
            mine3, got3, whole, merged, grad_parts, cotangent
        )
        far = across(2, got[0][:, :HALF]), across(1, got[1][:, HALF:])
        grad_parts += [to_chip(cotangent, z, n) for n in (2, 3)]
        heads_out, extra = attention_forward(merged, key_extra, rows * 2, 0, HALF // PAIR)
        mine, got, far, whole, heads_out, extra, grad_parts = wait(
            mine, got, far, whole, heads_out, extra, grad_parts
        )
        whole = place(whole, pick(z, [3, 3, 3, 1]), (mine, *got, *far))
        vec = vectors_of(whole, vectors.shape[0], count)
    else:
        whole = gather_pieces_of_all(whole, z)
        vec = vectors_of(whole, vectors.shape[0], count)
        x_mine = to_chips(tokens, z)
        x_other = swap(x_mine)
        grad_parts = [to_chip(cotangent, z, n) for n in range(count)]
        merged = project(core_id, x_mine, x_other, whole, vec.reshape(-1, PAIR))
        heads_out, extra = attention_forward(merged, key_extra, 2 * rows, 0, HALF // PAIR)
    grad_out = jnp.concatenate(grad_parts, axis=0)
    bounds = [0, D, 2 * D, 3 * D, 3 * D + FF] + [(n + 4) * D + FF for n in range(6)]
    _, _, bias_o, _, bias_down, gain_one, shift_one, gain_two, shift_two = (
        vec[bounds[n] : bounds[n + 1]] for n in range(9)
    )
    vec = vec.reshape(-1, PAIR)
    w_out = whole[QUARTERS : 2 * QUARTERS, :PAIR].reshape(HALF, D)

    branch, branch_other = out_forward(heads_out, whole)
    normed_in, normed_one, inverse_one = layer_norm(
        x_mine.astype(F32) + branch + swap(branch_other).astype(F32) + bias_o, gain_one, shift_one
    )
    u_mine = normed_in.astype(BF)
    u_other = swap(u_mine)
    hidden, slope, feed, feed_other = feed_forward(core_id, u_mine, u_other, whole, vec)
    feed = feed + swap(feed_other).astype(F32) + bias_down
    result, normed_two, inverse_two = layer_norm(u_mine.astype(F32) + feed, gain_two, shift_two)
    layer_out = result.astype(BF)

    grad_out = grad_out.astype(F32) * live
    grad_two, grad_gain_two, grad_shift_two = norm_back(grad_out, normed_two, inverse_two, gain_two)
    df_mine = grad_two.astype(BF)
    grad_bias_down = jnp.sum(df_mine.astype(F32), axis=0)
    grads_ff, grad_bias_up, du, du_other = feed_backward(
        df_mine, swap(df_mine), u_mine, u_other, hidden, slope, whole
    )
    sum_ff = sum_over_dp(grads_ff)
    du = du + swap(du_other).astype(F32) + grad_two
    grad_one, grad_gain_one, grad_shift_one = norm_back(du, normed_one, inverse_one, gain_one)
    da_mine = grad_one.astype(BF)
    da = both(da_mine)
    grad_bias_o = jnp.sum(da_mine.astype(F32), axis=0)
    do = rows_dot(da, w_out).astype(BF)
    grad_wo = cols_dot(heads_out, da).astype(BF)
    do, layer_out = lax.optimization_barrier((do, layer_out))
    layer_out = from_chips(layer_out, z)
    d_merged = attention_backward(merged, extra, key_extra, heads_out, do, rows)
    d_merged, layer_out = lax.optimization_barrier((d_merged, layer_out))
    d_merged, x_mine, x_other = wait(d_merged, x_mine, x_other)
    grad_qkv = cols_dot(d_merged, jnp.concatenate([x_mine, x_other], axis=0)).astype(BF)
    sums = jnp.sum(d_merged.astype(F32), axis=0).reshape(QUARTERS, 3, PAIR)
    vector_grad = jnp.concatenate(
        [
            spread_part(sums[:, 0], core, 1),
            spread_part(sums[:, 2], core, 1),
            grad_bias_o,
            spread_part(grad_bias_up.reshape(QUARTERS, 4, PAIR).swapaxes(0, 1), core, 4),
            grad_bias_down,
            grad_gain_one,
            grad_shift_one,
            grad_gain_two,
            grad_shift_two,
        ]
    ).astype(BF)
    shares = vector_grad.reshape(count, dp_count, -1).swapaxes(0, 1)
    if by_hand():
        shares = jnp.pad(shares, ((0, 0), (0, EXTRA - count), (0, D - shares.shape[2])))
    else:
        shares = jnp.pad(shares, ((0, 0), (0, 0), (0, EXTRA * D - shares.shape[2])))
        shares = shares.reshape(dp_count, count * EXTRA, D)
    run = PAIR * QUARTERS // dp_count
    late = jnp.concatenate(
        [
            jnp.concatenate(
                [grad_qkv.reshape(QUARTERS, 3 * PAIR, D), grad_wo.reshape(QUARTERS, PAIR, D)], axis=1
            )
            .reshape(QUARTERS, 4, dp_count // QUARTERS, run, D)
            .swapaxes(1, 2)
            .reshape(dp_count, 4 * run, D),
            shares,
        ],
        axis=1,
    )
    if by_hand():
        late, d_merged, whole = wait(late, d_merged, whole)
        grad_rows = token_grads(d_merged, whole, grad_one)
        chips, parts, grad_rows = reduce_late(late, sum_ff, grad_rows)
        piece = lax.psum_scatter(chips, "z", scatter_dimension=0, tiled=True)
        piece, grad_rows, parts = wait(piece, grad_rows, parts)
        values, grad_tokens = gather_pieces(piece, grad_rows, parts, z)
        start = jnp.where(core == 0, 2 * PAIR, 0)
        sent = jnp.stack(
            [lax.dynamic_slice_in_dim(value, start, PAIR, 0) for value in values[:3]]
            + [
                jnp.concatenate(
                    [lax.dynamic_slice_in_dim(value, start, PAIR, 0) for value in values[3:]], axis=1
                )
            ]
        )
        middle = swap(sent)
        share_size = vectors.shape[0] // 2
        found = [lax.dynamic_slice_in_dim(value, 3 * PAIR + z, 1, 0) for value in values[:4]]
        last = lax.dynamic_slice_in_dim(values[4], 3 * PAIR + z, 1, 0)
        found[3] = jnp.concatenate([found[3], last], axis=1)
        d = lax.axis_index("dp")
        found = jnp.stack([item[0, :share_size] for item in found])
        found = jnp.where(d % 2 == 1, jnp.stack([found[n ^ 1] for n in range(4)]), found)
        found = jnp.where(d >= 2, jnp.stack([found[n ^ 2] for n in range(4)]), found)
        halves = found.reshape(2, -1).astype(F32)
        kept, given = (
            jnp.where(core == 0, halves[0], halves[1]), jnp.where(core == 0, halves[1], halves[0])
        )
        shard_v = kept + swap(given)
        shard_w, weight_change, new_first_weights, new_second_weights = update_weights(
            values, middle, weights, first_weights, second_weights,
            is_out_projection(z, core), core,
        )
    else:
        grad_tokens = from_chips(token_grads(d_merged, whole, grad_one), z)
        sum_late = lax.psum_scatter(late.reshape(-1, D), "dp", scatter_dimension=0, tiled=True)
        parts = [sum_late[n * run : (n + 1) * run] for n in range(4)]
        parts += [sum_ff[n * run : (n + 1) * run] for n in range(8)]
        spare = sum_late[4 * run :].reshape(count, EXTRA, D)
        chips = [
            jnp.concatenate([*parts[3 * chip : 3 * chip + 3], spare[chip]], axis=0)
            for chip in range(count)
        ]
        piece = lax.psum_scatter(
            jnp.concatenate(chips, axis=0), "z", scatter_dimension=0, tiled=True
        )
        summed = lax.all_gather(piece, "dp", axis=0, tiled=True).reshape(dp_count, -1, D)
        blocks = summed[:, : 3 * run].reshape(dp_count, 3, run, D).swapaxes(0, 1).reshape(3, BLOCK, D)
        share_size = vectors.shape[0] * 2 // dp_count
        vector_sum = summed[:, 3 * run :].reshape(dp_count, -1)
        start = 0
        vector_sum = lax.dynamic_slice_in_dim(vector_sum, start, share_size, 1)
        vector_sum = vector_sum.reshape(2, -1).astype(F32)
        vector_sum = jnp.pad(vector_sum, ((0, 0), (0, 2 * D - vector_sum.shape[1])))
        shard_v = vector_sum[core] + swap(vector_sum[1 - core])
        shard_v = shard_v[: vectors.shape[0]]
        a, b, c = blocks
        middle = swap(jnp.where(core == 0, c, a))
        top = jnp.concatenate([jnp.where(core == 0, a, b), middle], axis=0)
        top = jnp.where(is_out_projection(z, core), top.T, top)
        shard_w = jnp.concatenate([top, jnp.where(core == 0, b, c)], axis=0).astype(F32)

        weight_change, new_first_weights, new_second_weights = adamw_update(
            weights, shard_w, first_weights, second_weights, 0.01
        )
    vector_change, new_first_vectors, new_second_vectors = adamw_update(
        vectors, shard_v, first_vectors, second_vectors, 0.0
    )
    return (
        layer_out,
        grad_tokens,
        shard_w,
        shard_v,
        weight_change,
        vector_change,
        new_first_weights,
        new_second_weights,
        new_first_vectors,
        new_second_vectors,
    )


def solution(mesh):
    chips = Mesh(
        mesh.devices.reshape(mesh.shape["dp"], mesh.shape["ctx"] // 2, 2), ("dp", "z", "core")
    )
    ctx = ("z", "core")
    activations, matrix, vector = P("dp", ctx, None), P(ctx, None), P(ctx)
    return jax.shard_map(
        shards,
        mesh=chips,
        in_specs=(activations, activations, P("dp"), matrix, vector, matrix, matrix, vector, vector),
        out_specs=(
            activations,
            activations,
            matrix,
            vector,
            matrix,
            vector,
            matrix,
            matrix,
            vector,
            vector,
        ),
        check_vma=False,
    )
```

```python
import math

import jax
import jax.numpy as jnp
from jax import lax
from jax.experimental import pallas as pl
from jax.experimental.pallas import tpu as pltpu
from jax.sharding import Mesh
from jax.sharding import PartitionSpec as P

D = 1024
FF = 4096
HD = 64
PAIR = 2 * HD
STEP = 10
EPSILON = 1e-05
LEARN_RATE = 0.003
BF = jnp.bfloat16
F32 = jnp.float32
HALF = D // 2
BLOCK = 512
EXTRA = 16
QUARTERS = 4
PIECE = 3 * PAIR + EXTRA
VMEM = 60 * 2**20
SCALAR = pl.BlockSpec(memory_space=pltpu.SMEM)
NO_COST = pl.CostEstimate(flops=1, bytes_accessed=1, transcendentals=0)


def rows_dot(operand, matrix):
    return lax.dot_general(operand, matrix, (((1,), (1,)), ((), ())), preferred_element_type=F32)


def cols_dot(operand, matrix):
    return lax.dot_general(operand, matrix, (((0,), (0,)), ((), ())), preferred_element_type=F32)


def plain_dot(operand, matrix):
    return lax.dot_general(operand, matrix, (((1,), (0,)), ((), ())), preferred_element_type=F32)


def swap(value):
    return lax.ppermute(value, "core", [(0, 1), (1, 0)])


def layer_norm(inputs, gain_vec, shift_vec):
    centre = jnp.mean(inputs, axis=-1, keepdims=True)
    shifted = inputs - centre
    inverse = lax.rsqrt(jnp.mean(shifted * shifted, axis=-1, keepdims=True) + EPSILON)
    normed = shifted * inverse
    return (normed * gain_vec + shift_vec, normed, inverse)


def norm_back(grad_out, normed, inverse, gain_vec):
    scaled = grad_out * gain_vec
    inner_term = (
        scaled
        - jnp.mean(scaled, axis=-1, keepdims=True)
        - normed * jnp.mean(scaled * normed, axis=-1, keepdims=True)
    )
    return (inverse * inner_term, jnp.sum(grad_out * normed, axis=0), jnp.sum(grad_out, axis=0))


def to_chip(blocks, z, shift):
    count = lax.axis_size("z")
    part = lax.dynamic_index_in_dim(blocks, (z + shift) % count, 0, keepdims=False)
    if shift:
        part = lax.ppermute(part, "z", [(i, (i + shift) % count) for i in range(count)])
    return part


def to_chips(blocks, z):
    return jnp.concatenate([to_chip(blocks, z, n) for n in range(lax.axis_size("z"))], axis=0)


def from_chip(rows, shift):
    count = lax.axis_size("z")
    part = rows.reshape(count, -1, rows.shape[-1])[shift]
    if shift:
        part = lax.ppermute(part, "z", [(i, (i - shift) % count) for i in range(count)])
    return part


def put_together(parts, z):
    count = lax.axis_size("z")
    result = jnp.zeros((count, *parts[0].shape), BF)
    for shift in range(count):
        result = lax.dynamic_update_index_in_dim(result, parts[shift], (z + shift) % count, 0)
    return result


def from_chips(rows, z):
    return put_together([from_chip(rows, n) for n in range(lax.axis_size("z"))], z)


def is_out_projection(z, core):
    return jnp.logical_and(z == 1, core == 0)


def pack_kernel(flag_ref, rows_ref, columns_ref, outer_ref, middle_ref):
    step = pl.program_id(0)
    turned = jnp.logical_and(flag_ref[0] == 1, step < 2)

    def write(value):
        @pl.when(step != 1)
        def _():
            outer_ref[...] = value

        @pl.when(step == 1)
        def _():
            middle_ref[...] = value

    @pl.when(turned)
    def _():
        write(columns_ref[...].T.astype(BF))

    @pl.when(jnp.logical_not(turned))
    def _():
        write(rows_ref[...].astype(BF))


def pack_weights(weights, flag):
    return pl.pallas_call(
        pack_kernel,
        grid_spec=pltpu.PrefetchScalarGridSpec(
            num_scalar_prefetch=1,
            grid=(3,),
            in_specs=[
                pl.BlockSpec((BLOCK, D), lambda n, flag: (n, 0)),
                pl.BlockSpec((D, BLOCK), lambda n, flag: (0, jnp.minimum(n, 1) * flag[0])),
            ],
            out_specs=[
                pl.BlockSpec((BLOCK, D), lambda n, flag: (n // 2, 0)),
                pl.BlockSpec((BLOCK, D), lambda n, flag: (0, 0)),
            ],
        ),
        out_shape=[
            jax.ShapeDtypeStruct((2 * BLOCK, D), BF),
            jax.ShapeDtypeStruct((BLOCK, D), BF),
        ],
        cost_estimate=NO_COST,
        compiler_params=pltpu.CompilerParams(vmem_limit_bytes=VMEM),
    )(flag.astype(jnp.int32).reshape(1), weights, weights)


def own_kernel(
    where_ref, first_ref, last_ref, other_ref, mine_vector, other_vector, whole_ref, piece_ref
):
    core = where_ref[2]

    def write(parts, vectors):
        value = jnp.concatenate([*parts, *vectors], axis=0)
        whole_ref[0] = value

        @pl.when(pl.program_id(0) == 0)
        def _():
            piece_ref[...] = value

    first, last, other = first_ref[...], last_ref[...], other_ref[...]
    vectors = [mine_vector[...], other_vector[...]]

    @pl.when(core == 0)
    def _():
        write([first, last, other], vectors)

    @pl.when(core == 1)
    def _():
        write([other, first, last], vectors[::-1])


def own_pieces(outer, other, vector, other_vector, z, core):
    where = jnp.stack([z, lax.axis_index("dp") % QUARTERS, core]).astype(jnp.int32)
    run = (PAIR, D)
    small = pl.BlockSpec(vector.shape, lambda n, where: (0, 0))
    return pl.pallas_call(
        own_kernel,
        grid_spec=pltpu.PrefetchScalarGridSpec(
            num_scalar_prefetch=1,
            grid=(QUARTERS,),
            in_specs=[
                pl.BlockSpec(run, lambda n, where: (where[1] ^ n, 0)),
                pl.BlockSpec(run, lambda n, where: (QUARTERS + (where[1] ^ n), 0)),
                pl.BlockSpec(run, lambda n, where: (where[1] ^ n, 0)),
                small,
                small,
            ],
            out_specs=[
                pl.BlockSpec(
                    (1, PIECE, D), lambda n, where: (where[0] * QUARTERS + (where[1] ^ n), 0, 0)
                ),
                pl.BlockSpec((PIECE, D), lambda n, where: (0, 0)),
            ],
        ),
        out_shape=[
            jax.ShapeDtypeStruct((4 * QUARTERS, PIECE, D), BF),
            jax.ShapeDtypeStruct((PIECE, D), BF),
        ],
        cost_estimate=NO_COST,
        compiler_params=pltpu.CompilerParams(vmem_limit_bytes=VMEM),
    )(where, outer, outer, other, vector, other_vector)


def gather_pieces_of_all(whole, z):
    count = lax.axis_size("dp") // QUARTERS
    mine = lax.dynamic_slice_in_dim(whole, z * QUARTERS, QUARTERS, 0)
    share = lax.dynamic_index_in_dim(mine, lax.axis_index("dp") // count, 0, keepdims=False)
    blocks = share[: 3 * PAIR].reshape(3, PAIR, D)
    blocks = lax.dynamic_slice_in_dim(
        blocks, lax.axis_index("dp") % count * (PAIR // count), PAIR // count, 1
    )
    everything = lax.all_gather(blocks.reshape(-1, D), ("z", "dp"), axis=0, tiled=True)
    everything = everything.reshape(-1, count, 3, PAIR // count, D).swapaxes(1, 2)
    spare = lax.all_gather(share[3 * PAIR :], "z", axis=0, tiled=True).reshape(-1, 1, EXTRA, D)
    spare = jnp.broadcast_to(spare, (spare.shape[0], QUARTERS, EXTRA, D)).reshape(-1, EXTRA, D)
    return jnp.concatenate([everything.reshape(-1, 3 * PAIR, D), spare], axis=1)


def vectors_of(whole, size, chips):
    found = jnp.stack([whole[QUARTERS * chip, 3 * PAIR :] for chip in range(chips)])
    return found.reshape(-1, 2, EXTRA * D // 2)[:, :, :size].reshape(-1).astype(F32)


def place_kernel(where_ref, whole_in, mine, got_x, got_y, far_a, far_b, whole_ref):
    del where_ref, whole_in
    for index, source in enumerate((mine, got_x, got_y)):

        @pl.when(pl.program_id(0) == index)
        def _(source=source):
            whole_ref[0] = source[...]

    @pl.when(pl.program_id(0) == 3)
    def _():
        whole_ref[0, :, :HALF] = far_a[...]
        whole_ref[0, :, HALF:] = far_b[...]


def place(whole, shard, values):
    where = jnp.stack([shard, lax.axis_index("dp")]).astype(jnp.int32)
    return pl.pallas_call(
        place_kernel,
        grid_spec=pltpu.PrefetchScalarGridSpec(
            num_scalar_prefetch=1,
            grid=(4,),
            in_specs=[pl.BlockSpec(memory_space=pl.ANY)]
            + [pl.BlockSpec(value.shape, lambda n, where: (0, 0)) for value in values],
            out_specs=pl.BlockSpec(
                (1, PIECE, D), lambda n, where: (where[0] * QUARTERS + (where[1] ^ n), 0, 0)
            ),
        ),
        out_shape=jax.ShapeDtypeStruct(whole.shape, BF),
        input_output_aliases={1: 0},
        cost_estimate=NO_COST,
        compiler_params=pltpu.CompilerParams(vmem_limit_bytes=VMEM),
    )(where, whole, *values)


def sum_over_dp(grads):
    count = lax.axis_size("dp") // QUARTERS
    if count > 1:
        grads = grads.reshape(QUARTERS, -1, count, PAIR // count, D).swapaxes(1, 2)
    return lax.psum_scatter(grads.reshape(-1, D), "dp", scatter_dimension=0, tiled=True)


def by_hand():
    return lax.axis_size("dp") == 4 and lax.axis_size("z") == 4


def plus(first, second):
    return (first.astype(F32) + second.astype(F32)).astype(BF)


def across(bit, value):
    return lax.ppermute(value, "dp", [(i, i ^ bit) for i in range(4)])


def at(value, index, axis):
    return lax.dynamic_index_in_dim(value, index, axis, keepdims=False)


def along_z(value, pairs):
    return lax.ppermute(value, "z", pairs)


def pick(z, values):
    result = values[-1]
    for index in range(len(values) - 2, -1, -1):
        result = jnp.where(z == index, values[index], result)
    return result


def wait(*values):
    return lax.optimization_barrier(values)


def assemble_kernel(where_ref, a, got_a, far_a, b, got_b, far_b, sums_ref, out_ref):
    chip = pl.program_id(0)
    rows = 3 * PAIR

    def write(target, source):
        for index, (mine, got, far, columns) in enumerate(
            ((a, got_a, far_a, slice(None, HALF)), (b, got_b, far_b, slice(HALF, None)))
        ):
            side = where_ref[index]
            value = plus(plus(mine[side, source], got[side, source]), far[source])
            out_ref[target, columns] = value

    write(slice(rows, None), slice(4 * PAIR, None))

    @pl.when(chip == 0)
    def _():
        write(slice(None, rows), slice(None, rows))

    @pl.when(chip == 1)
    def _():
        write(slice(None, PAIR), slice(rows, rows + PAIR))
        out_ref[PAIR:rows] = sums_ref[: 2 * PAIR]

    @pl.when(chip == 2)
    def _():
        out_ref[:rows] = sums_ref[2 * PAIR : 5 * PAIR]

    @pl.when(chip == 3)
    def _():
        out_ref[:rows] = sums_ref[5 * PAIR :]


def assemble(x, y, late, sums):
    return pl.pallas_call(
        assemble_kernel,
        grid=(4,),
        in_specs=[SCALAR] + [whole_block(item.shape) for item in (*late, sums)],
        out_specs=pl.BlockSpec((PIECE, D), lambda chip: (chip, 0)),
        out_shape=jax.ShapeDtypeStruct((4 * PIECE, D), BF),
        cost_estimate=NO_COST,
        compiler_params=pltpu.CompilerParams(vmem_limit_bytes=VMEM),
    )(jnp.stack([y, x]).astype(jnp.int32), *late, sums)


def reduce_late(late, sum_ff, grad_rows):
    d = lax.axis_index("dp")
    x, y = d % 2, d // 2
    late = late.reshape(2, 2, -1, D)
    a, b = late[..., :HALF], late[..., HALF:]
    got_a, got_b = across(1, at(a, 1 - x, 1)), across(2, at(b, 1 - y, 0))
    got_a, got_b, a, b, sum_ff, grad_rows = wait(got_a, got_b, a, b, sum_ff, grad_rows)
    a, b = at(a, x, 1), at(b, y, 0)
    far_a = across(2, plus(at(a, 1 - y, 0), at(got_a, 1 - y, 0)))
    far_b = across(1, plus(at(b, 1 - x, 0), at(got_b, 1 - x, 0)))
    parts = {n: from_chip(grad_rows, n) for n in (0, 1)}
    far_a, far_b, a, b, parts, grad_rows = wait(far_a, far_b, a, b, parts, grad_rows)
    return assemble(x, y, (a, got_a, far_a, b, got_b, far_b), sum_ff), parts, grad_rows


def gather_pieces(piece, grad_rows, parts, z):
    got = across(1, piece), across(2, piece)
    parts = {**parts, **{n: from_chip(grad_rows, n) for n in (2, 3)}}
    got, piece, parts = wait(got, piece, parts)
    far = across(2, got[0][:, :HALF]), across(1, got[1][:, HALF:])
    grad_tokens = put_together(parts, z)
    far, got, piece, grad_tokens = wait(far, got, piece, grad_tokens)
    return (piece, *got, *far), grad_tokens


def update_kernel(
    where_ref, mine, got_x, got_y, far_a, far_b, middle_ref, weight_ref, first_ref, second_ref,
    grad_ref, change_ref, first_out, second_out,
):
    d, core, turned = where_ref[0], where_ref[1], where_ref[2] == 1
    block, pair = pl.program_id(0), pl.program_id(1)
    pieces = (mine, got_x, got_y)
    rows = pl.ds(pl.multiple_of((core + block // 2) * PAIR, PAIR), PAIR)
    plain = jnp.logical_and(block != 1, jnp.logical_or(block == 2, jnp.logical_not(turned)))
    for n in range(QUARTERS):
        slot = pl.ds(pl.multiple_of((d ^ n) * PAIR, PAIR), PAIR)
        ours = pair == 0

        @pl.when(ours & (block == 1) & jnp.logical_not(turned))
        def _(n=n, slot=slot):
            grad_ref[slot, :] = middle_ref[n].astype(F32)

        @pl.when(ours & plain)
        def _(n=n, slot=slot):
            if n < 3:
                grad_ref[slot, :] = pieces[n][rows, :].astype(F32)
            else:
                grad_ref[slot, :HALF] = far_a[rows, :].astype(F32)
                grad_ref[slot, HALF:] = far_b[rows, :].astype(F32)

        @pl.when(ours & (block < 2) & turned)
        def _(n=n, slot=slot):
            start = pl.multiple_of((d ^ n) * PAIR, PAIR)
            columns = pl.ds(pl.multiple_of(block * HALF + start, PAIR), PAIR)
            for m in range(QUARTERS):
                low = pl.ds(pl.multiple_of((d ^ m) * PAIR, PAIR), PAIR)
                high = pl.ds(pl.multiple_of(HALF + (d ^ m) * PAIR, PAIR), PAIR)
                grad_ref[slot, high] = middle_ref[m, :, columns].astype(F32).T
                if m < 3:
                    grad_ref[slot, low] = pieces[m][:PAIR, columns].astype(F32).T
            low = pl.ds(pl.multiple_of((d ^ 3) * PAIR, PAIR), PAIR)
            for half, far in enumerate((far_a, far_b)):

                @pl.when(block == half)
                def _(far=far):
                    grad_ref[slot, low] = far[:PAIR, pl.ds(start, PAIR)].astype(F32).T

    change_ref[...], first_out[...], second_out[...] = adamw_update(
        weight_ref[...], grad_ref[...], first_ref[...], second_ref[...], 0.01
    )


def update_weights(values, middle, weights, first_weights, second_weights, turned, core):
    d = lax.axis_index("dp")
    where = jnp.stack([d, core, turned.astype(jnp.int32)]).astype(jnp.int32)
    rows = pl.BlockSpec((BLOCK, D), lambda b, n, where: (b, 0))
    return pl.pallas_call(
        update_kernel,
        grid_spec=pltpu.PrefetchScalarGridSpec(
            num_scalar_prefetch=1,
            grid=(3, 1),
            in_specs=[pl.BlockSpec(value.shape, lambda b, n, where: (0, 0)) for value in values]
            + [pl.BlockSpec(middle.shape, lambda b, n, where: (0, 0, 0))]
            + [rows] * 3,
            out_specs=[rows] * 4,
        ),
        out_shape=[jax.ShapeDtypeStruct(weights.shape, F32)] * 4,
        cost_estimate=NO_COST,
        compiler_params=pltpu.CompilerParams(vmem_limit_bytes=VMEM),
    )(where, *values, middle, weights, first_weights, second_weights)


def lanes_of(shape, head):
    lane = lax.broadcasted_iota(jnp.int32, shape, 1)
    return (lane >= HD) if head else (lane < HD), lane - HD * (1 - head)


def split_three(value):
    high = value.astype(BF).astype(F32)
    mid = (value - high).astype(BF).astype(F32)
    return high, mid, (value - high - mid).astype(BF).astype(F32)


def spread_lanes(place, values):
    result = jnp.zeros(place.shape, F32)
    for lane, value in enumerate(values):
        result = jnp.where(place == lane, value, result)
    return result


def whole_block(shape):
    return pl.BlockSpec(shape, lambda *_: (0,) * len(shape))


def qkv_kernel(core_ref, x_mine, x_other, w_ref, vector_ref, out_ref):
    quarter = pl.program_id(0)
    row = core_ref[0] * QUARTERS + quarter
    bias_q = vector_ref[pl.ds(row, 1), :]
    bias_v = vector_ref[pl.ds(D // PAIR + row, 1), :]
    bias = jnp.concatenate([bias_q, jnp.zeros_like(bias_q), bias_v], axis=1)
    half = x_mine.shape[0]
    out_ref[:half] = (rows_dot(x_mine[...], w_ref[0]) + bias).astype(BF)
    out_ref[half:] = (rows_dot(x_other[...], w_ref[0]) + bias).astype(BF)


def project(core, x_mine, x_other, whole, vec):
    rows = 2 * x_mine.shape[0]
    return pl.pallas_call(
        qkv_kernel,
        grid=(QUARTERS,),
        in_specs=[
            SCALAR,
            whole_block(x_mine.shape),
            whole_block(x_mine.shape),
            pl.BlockSpec((1, 3 * PAIR, D), lambda quarter: (quarter, 0, 0)),
            whole_block(vec.shape),
        ],
        out_specs=pl.BlockSpec((rows, 3 * PAIR), lambda quarter: (0, quarter)),
        out_shape=jax.ShapeDtypeStruct((rows, 3 * HALF), BF),
        cost_estimate=NO_COST,
        compiler_params=pltpu.CompilerParams(vmem_limit_bytes=VMEM),
    )(core, x_mine, x_other, whole, vec)


def forward_kernel(q_ref, k_ref, v_ref, key_ref, o_ref, extra_ref):
    q, k, v, key_extra = q_ref[...], k_ref[...], v_ref[...], key_ref[...]
    outs, extras = [], []
    for head in range(2):
        in_q, place_q = lanes_of(q.shape, head)
        in_k, place_k = lanes_of(k.shape, head)
        keys = jnp.where(in_k, k, key_extra)
        queries = jnp.where(in_q, q * BF(0.125), jnp.where(place_q == 0, BF(1), BF(0)))
        values = jnp.where(in_k, v, jnp.where(place_k == 0, BF(1), BF(0)))
        scores = rows_dot(queries, keys)
        highest = jnp.max(scores, axis=1, keepdims=True)
        terms = jnp.exp(scores - highest).astype(BF)
        out = plain_dot(terms, values)
        column = HD * (1 - head)
        total = out[:, column : column + 1]
        outs.append(out * (1.0 / total))
        parts = split_three(-(highest + jnp.log(total)))
        extras.append(spread_lanes(place_q, (1.0, *parts)))
    in_first, _ = lanes_of(q.shape, 0)
    o_ref[...] = jnp.where(in_first, outs[0], outs[1]).astype(BF)
    extra_ref[...] = jnp.where(in_first, extras[1], extras[0]).astype(BF)


def forward_more_kernel(q_ref, k_ref, v_ref, key_ref, o_in, extra_in, o_ref, extra_ref):
    del o_in, extra_in
    forward_kernel(q_ref, k_ref, v_ref, key_ref, o_ref, extra_ref)


def attention_forward(merged, key_extra, step, start, pairs, done=()):
    rows = merged.shape[0]
    some = pl.BlockSpec((step, PAIR), lambda pair, part: (part, 3 * (pair + start)))
    ours = pl.BlockSpec((step, PAIR), lambda pair, part: (part, pair + start))
    keys = pl.BlockSpec((rows, PAIR), lambda pair, part: (0, 3 * (pair + start) + 1))
    values = pl.BlockSpec((rows, PAIR), lambda pair, part: (0, 3 * (pair + start) + 2))
    return pl.pallas_call(
        forward_more_kernel if done else forward_kernel,
        grid=(pairs, rows // step),
        in_specs=[some, keys, values, whole_block(key_extra.shape)]
        + [pl.BlockSpec(memory_space=pl.ANY)] * len(done),
        out_specs=[ours, ours],
        out_shape=[jax.ShapeDtypeStruct((rows, HALF), BF)] * 2,
        input_output_aliases={4: 0, 5: 1} if done else {},
        cost_estimate=NO_COST,
        compiler_params=pltpu.CompilerParams(vmem_limit_bytes=VMEM),
    )(merged, merged, merged, key_extra, *done)


def backward_kernel(
    q_ref, extra_ref, k_ref, v_ref, key_ref, o_ref, do_ref, out_ref, dk_sum, dv_sum
):
    part = pl.program_id(1)
    q, extra, k, v = q_ref[...], extra_ref[...], k_ref[...], v_ref[...]
    key_extra, do = key_ref[...], do_ref[...]
    product = do.astype(F32) * o_ref[...].astype(F32)
    zero = BF(0)
    dq = dk = dv = 0.0
    for head in range(2):
        in_q, place_q = lanes_of(q.shape, head)
        in_k, place_k = lanes_of(k.shape, head)
        scaled = jnp.where(in_q, q * BF(0.125), zero)
        queries = jnp.where(in_q, scaled, extra)
        keys = jnp.where(in_k, k, key_extra)
        only_k = jnp.where(in_k, k, zero)
        only_do = jnp.where(in_q, do, zero)
        row_sum = jnp.sum(jnp.where(in_q, product, 0.0), axis=1, keepdims=True)
        grads = jnp.where(in_q, do, spread_lanes(place_q, split_three(-row_sum)).astype(BF))
        ones = jnp.where((place_k >= 0) & (place_k < 3), BF(1), zero)
        values = jnp.where(in_k, v, ones)
        probs = jnp.exp(rows_dot(keys, queries))
        grad_scores = (probs * rows_dot(values, grads)).astype(BF)
        dv = dv + plain_dot(probs.astype(BF), only_do)
        dk = dk + plain_dot(grad_scores, scaled)
        dq = dq + cols_dot(grad_scores, only_k)
    step = q.shape[0]
    out_ref[pl.ds(part * step, step), :PAIR] = (dq * 0.125).astype(BF)

    @pl.when(part == 0)
    def _():
        dk_sum[...] = dk
        dv_sum[...] = dv

    @pl.when(part > 0)
    def _():
        dk_sum[...] += dk
        dv_sum[...] += dv

    @pl.when(part == pl.num_programs(1) - 1)
    def _():
        out_ref[:, PAIR : 2 * PAIR] = dk_sum[...].astype(BF)
        out_ref[:, 2 * PAIR :] = dv_sum[...].astype(BF)


def attention_backward(merged, extra, key_extra, heads_out, grad_out, step):
    rows = merged.shape[0]
    some = pl.BlockSpec((step, PAIR), lambda pair, part: (part, 3 * pair))
    ours = pl.BlockSpec((step, PAIR), lambda pair, part: (part, pair))
    keys = pl.BlockSpec((rows, PAIR), lambda pair, part: (0, 3 * pair + 1))
    values = pl.BlockSpec((rows, PAIR), lambda pair, part: (0, 3 * pair + 2))
    return pl.pallas_call(
        backward_kernel,
        grid=(HALF // PAIR, rows // step),
        in_specs=[some, ours, keys, values, whole_block(key_extra.shape), ours, ours],
        out_specs=pl.BlockSpec((rows, 3 * PAIR), lambda pair, part: (0, pair)),
        out_shape=jax.ShapeDtypeStruct((rows, 3 * HALF), BF),
        scratch_shapes=[pltpu.VMEM((rows, PAIR), F32)] * 2,
        cost_estimate=NO_COST,
        compiler_params=pltpu.CompilerParams(vmem_limit_bytes=VMEM),
    )(merged, extra, merged, merged, key_extra, heads_out, grad_out)


def key_lanes(allowed):
    lane = jnp.arange(PAIR)[None, :] % HD
    bias = jnp.where(allowed, 0.0, -1e30)[:, None]
    return jnp.where(lane == 0, bias, jnp.where(lane < 4, 1.0, 0.0)).astype(BF)


def weight_block(chip, part, count=1):
    return pl.BlockSpec(
        (1, count * PAIR, D), lambda quarter: (chip * QUARTERS + quarter, part // count, 0)
    )


UP_BLOCKS = (weight_block(1, 1), weight_block(1, 2), weight_block(2, 0, 2))
DOWN_BLOCKS = (weight_block(2, 2), weight_block(3, 0, 3))


def joined(refs):
    return jnp.concatenate([ref[0] for ref in refs], axis=0)


def feed_forward_kernel(
    core_ref, u_mine, u_other, up0, up1, up2, down0, down1, vector_ref,
    hidden_ref, slope_ref, mine_ref, other_ref, total,
):
    quarter = pl.program_id(0)
    rows = [
        vector_ref[pl.ds(3 * D // PAIR + (2 * n + core_ref[0]) * QUARTERS + quarter, 1), :]
        for n in range(4)
    ]
    bias = jnp.concatenate(rows, axis=1)
    up, down = joined((up0, up1, up2)), joined((down0, down1))
    half = mine_ref.shape[0]
    for place, u_ref in ((slice(None, half), u_mine), (slice(half, None), u_other)):
        z = rows_dot(u_ref[...], up) + bias
        cdf = 0.5 * (1.0 + lax.erf(z * (1.0 / math.sqrt(2.0))))
        slope = cdf + z * jnp.exp(-0.5 * z * z) * (1.0 / math.sqrt(2.0 * math.pi))
        hidden = (z * cdf).astype(BF)
        hidden_ref[place, :] = hidden
        slope_ref[place, :] = slope.astype(BF)
        part = plain_dot(hidden, down)

        @pl.when(quarter == 0)
        def _(place=place, part=part):
            total[place, :] = part

        @pl.when(quarter > 0)
        def _(place=place, part=part):
            total[place, :] += part

    @pl.when(quarter == QUARTERS - 1)
    def _():
        mine_ref[...] = total[:half]
        other_ref[...] = total[half:].astype(BF)


def feed_forward(core, u_mine, u_other, whole, vec):
    rows = 2 * u_mine.shape[0]
    columns = pl.BlockSpec((rows, BLOCK), lambda quarter: (0, quarter))
    half = (rows // 2, D)
    return pl.pallas_call(
        feed_forward_kernel,
        grid=(QUARTERS,),
        in_specs=[
            SCALAR, whole_block(half), whole_block(half), *UP_BLOCKS, *DOWN_BLOCKS,
            whole_block(vec.shape),
        ],
        out_specs=[columns, columns, whole_block(half), whole_block(half)],
        out_shape=[
            jax.ShapeDtypeStruct((rows, FF // 2), BF),
            jax.ShapeDtypeStruct((rows, FF // 2), BF),
            jax.ShapeDtypeStruct(half, F32),
            jax.ShapeDtypeStruct(half, BF),
        ],
        scratch_shapes=[pltpu.VMEM((rows, D), F32)],
        cost_estimate=NO_COST,
        compiler_params=pltpu.CompilerParams(vmem_limit_bytes=VMEM),
    )(core, u_mine, u_other, whole, whole, whole, whole, whole, vec)


def out_forward_kernel(o_ref, w0, w1, w2, w3, mine_ref, other_ref):
    part = plain_dot(o_ref[...], joined((w0, w1, w2, w3)))

    @pl.when(pl.program_id(0) == 0)
    def _():
        mine_ref[...] = part

    @pl.when(pl.program_id(0) == 1)
    def _():
        other_ref[...] = part.astype(BF)


def out_forward(heads_out, whole):
    rows = heads_out.shape[0]
    half = (rows // 2, D)

    def run(quarter):
        return pl.BlockSpec((1, PAIR, D), lambda n: (QUARTERS + quarter, 0, 0))

    return pl.pallas_call(
        out_forward_kernel,
        grid=(2,),
        in_specs=[
            pl.BlockSpec((rows // 2, HALF), lambda n: (n, 0)), *[run(q) for q in range(QUARTERS)]
        ],
        out_specs=[whole_block(half), whole_block(half)],
        out_shape=[jax.ShapeDtypeStruct(half, F32), jax.ShapeDtypeStruct(half, BF)],
        cost_estimate=NO_COST,
        compiler_params=pltpu.CompilerParams(vmem_limit_bytes=VMEM),
    )(heads_out, whole, whole, whole, whole)


def feed_backward_kernel(
    df_mine, df_other, u_mine, u_other, hidden_ref, slope_ref, up0, up1, up2, down0, down1,
    grads_ref, bias_ref, mine_ref, other_ref, total,
):
    quarter = pl.program_id(0)
    up, down = joined((up0, up1, up2)), joined((down0, down1))
    half = mine_ref.shape[0]
    grad_up = grad_down = bias = 0.0
    for place, df_ref, u_ref in (
        (slice(None, half), df_mine, u_mine), (slice(half, None), df_other, u_other)
    ):
        df = df_ref[...]
        dz = (rows_dot(df, down) * slope_ref[place, :].astype(F32)).astype(BF)
        bias = bias + jnp.sum(dz.astype(F32), axis=0, keepdims=True)
        grad_up = grad_up + cols_dot(dz, u_ref[...])
        grad_down = grad_down + cols_dot(hidden_ref[place, :], df)
        part = plain_dot(dz, up)

        @pl.when(quarter == 0)
        def _(place=place, part=part):
            total[place, :] = part

        @pl.when(quarter > 0)
        def _(place=place, part=part):
            total[place, :] += part

    bias_ref[...] = bias
    grads_ref[0, :BLOCK] = grad_up.astype(BF)
    grads_ref[0, BLOCK:] = grad_down.astype(BF)

    @pl.when(quarter == QUARTERS - 1)
    def _():
        mine_ref[...] = total[:half]
        other_ref[...] = total[half:].astype(BF)


def feed_backward(df_mine, df_other, u_mine, u_other, hidden, slope, whole):
    rows = 2 * u_mine.shape[0]
    columns = pl.BlockSpec((rows, BLOCK), lambda quarter: (0, quarter))
    half = (rows // 2, D)
    return pl.pallas_call(
        feed_backward_kernel,
        grid=(QUARTERS,),
        in_specs=[
            *[whole_block(half)] * 4, columns, columns, *UP_BLOCKS, *DOWN_BLOCKS
        ],
        out_specs=[
            pl.BlockSpec((1, 2 * BLOCK, D), lambda quarter: (quarter, 0, 0)),
            pl.BlockSpec((1, BLOCK), lambda quarter: (0, quarter)),
            whole_block(half),
            whole_block(half),
        ],
        out_shape=[
            jax.ShapeDtypeStruct((QUARTERS, 2 * BLOCK, D), BF),
            jax.ShapeDtypeStruct((1, FF // 2), F32),
            jax.ShapeDtypeStruct(half, F32),
            jax.ShapeDtypeStruct(half, BF),
        ],
        scratch_shapes=[pltpu.VMEM((rows, D), F32)],
        cost_estimate=NO_COST,
        compiler_params=pltpu.CompilerParams(vmem_limit_bytes=VMEM),
    )(df_mine, df_other, u_mine, u_other, hidden, slope, whole, whole, whole, whole, whole)


def adamw_update(parameter, gradient, first_old, second_old, decay_rate):
    step_float = float(STEP)
    first_new = 0.9 * first_old + 0.1 * gradient
    second_new = 0.999 * second_old + 0.001 * gradient * gradient
    first_fix = first_new * (1.0 / (1.0 - 0.9**step_float))
    second_fix = second_new * (1.0 / (1.0 - 0.999**step_float))
    update = first_fix / (jnp.sqrt(second_fix) + 1e-08)
    return (-LEARN_RATE * (update + decay_rate * parameter), first_new, second_new)


def share(partial):
    half = partial.shape[0] // 2
    return partial[:half] + swap(partial[half:].astype(BF)).astype(F32)


def both(rows):
    return jnp.concatenate([rows, swap(rows)], axis=0)


def spread_part(vector, core, pieces):
    parts = vector.reshape(pieces, 1, -1)
    mine = (jnp.arange(2) == core)[None, :, None]
    return jnp.where(mine, parts, 0.0).reshape(-1)


def token_grads(d_merged, whole, grad_one):
    rows = whole[:QUARTERS, : 3 * PAIR].reshape(-1, D)
    return (share(plain_dot(d_merged, rows)) + grad_one).astype(BF)


def shards(
    tokens,
    cotangent,
    lengths,
    weights,
    vectors,
    first_weights,
    second_weights,
    first_vectors,
    second_vectors,
):
    z, core = lax.axis_index("z"), lax.axis_index("core")
    count, dp_count = lax.axis_size("z"), lax.axis_size("dp")
    per_device = tokens.shape[1]
    rows = count * per_device
    length = lengths[z]
    block = jnp.arange(count, dtype=jnp.int32)[:, None]
    inner = jnp.arange(per_device, dtype=jnp.int32)[None, :]
    chip_of = (z - block) % count
    here = ((chip_of * 2 + core) * per_device + inner).reshape(rows)
    there = ((chip_of * 2 + 1 - core) * per_device + inner).reshape(rows)
    key_extra = key_lanes(jnp.concatenate([here, there]) < length)
    live = (here < length).astype(F32)[:, None]
    core_id = core.astype(jnp.int32).reshape(1)

    outer, middle = pack_weights(weights, is_out_projection(z, core))
    vector = jnp.pad(vectors.astype(BF), (0, EXTRA * D // 2 - vectors.shape[0])).reshape(-1, D)
    other, other_vector = swap(middle), swap(vector)
    whole, piece = own_pieces(outer, other, vector, other_vector, z, core)
    if by_hand():
        x_parts = [to_chip(tokens, z, n) for n in (0, 2)]
        piece, whole, x_parts, tokens = wait(piece, whole, x_parts, tokens)
        up1 = along_z(piece, [(0, 1), (1, 2), (2, 3)])
        down1 = along_z(piece, [(1, 0), (2, 1), (3, 2)])
        up1, down1, whole = wait(up1, down1, whole)
        mine = jnp.where(z == 0, down1, up1)
        got = across(1, mine), across(2, mine)
        up2 = along_z(up1, [(1, 2)])
        down2 = along_z(down1, [(1, 0), (2, 1)])
        mine, got, up1, up2, down1, down2 = wait(mine, got, up1, up2, down1, down2)
        far = across(2, got[0][:, :HALF]), across(1, got[1][:, HALF:])
        up3 = along_z(up2, [(2, 3)])
        mine, got, far, up1, up2, up3, down1, down2 = wait(
            mine, got, far, up1, up2, up3, down1, down2
        )
        mine2 = pick(z, [down2, down1, up2, up3])
        got2 = across(1, mine2), across(2, mine2)
        up4 = along_z(up1, [(2, 3)])
        down3 = along_z(down2, [(1, 0)])
        whole = place(whole, pick(z, [1, 0, 1, 2]), (mine, *got, *far))
        mine, got, up4, down1, down2, down3, whole, tokens = wait(
            mine2, got2, up4, down1, down2, down3, whole, tokens
        )
        far = across(2, got[0][:, :HALF]), across(1, got[1][:, HALF:])
        x_parts += [to_chip(tokens, z, n) for n in (1, 3)]
        mine, got, far, up4, down1, down2, down3, whole, x_parts, cotangent = wait(
            mine, got, far, up4, down1, down2, down3, whole, x_parts, cotangent
        )
        x_mine = jnp.concatenate([x_parts[n] for n in (0, 2, 1, 3)], axis=0)
        x_other = swap(x_mine)
        mine3 = pick(z, [down3, down2, down1, up4])
        got3 = across(1, mine3), across(2, mine3)
        grad_parts = [to_chip(cotangent, z, n) for n in (0, 1)]
        whole = place(whole, pick(z, [2, 2, 0, 0]), (mine, *got, *far))
        vec = vectors_of(whole, vectors.shape[0], 1).reshape(-1, PAIR)
        merged = project(core_id, x_mine, x_other, whole, vec)
        mine, got, whole, merged, grad_parts, cotangent = wait(
            mine3, got3, whole, merged, grad_parts, cotangent
        )
        far = across(2, got[0][:, :HALF]), across(1, got[1][:, HALF:])
        grad_parts += [to_chip(cotangent, z, n) for n in (2, 3)]
        heads_out, extra = attention_forward(merged, key_extra, rows * 2, 0, HALF // PAIR)
        mine, got, far, whole, heads_out, extra, grad_parts = wait(
            mine, got, far, whole, heads_out, extra, grad_parts
        )
        whole = place(whole, pick(z, [3, 3, 3, 1]), (mine, *got, *far))
        vec = vectors_of(whole, vectors.shape[0], count)
    else:
        whole = gather_pieces_of_all(whole, z)
        vec = vectors_of(whole, vectors.shape[0], count)
        x_mine = to_chips(tokens, z)
        x_other = swap(x_mine)
        grad_parts = [to_chip(cotangent, z, n) for n in range(count)]
        merged = project(core_id, x_mine, x_other, whole, vec.reshape(-1, PAIR))
        heads_out, extra = attention_forward(merged, key_extra, 2 * rows, 0, HALF // PAIR)
    grad_out = jnp.concatenate(grad_parts, axis=0)
    bounds = [0, D, 2 * D, 3 * D, 3 * D + FF] + [(n + 4) * D + FF for n in range(6)]
    _, _, bias_o, _, bias_down, gain_one, shift_one, gain_two, shift_two = (
        vec[bounds[n] : bounds[n + 1]] for n in range(9)
    )
    vec = vec.reshape(-1, PAIR)
    w_out = whole[QUARTERS : 2 * QUARTERS, :PAIR].reshape(HALF, D)

    branch, branch_other = out_forward(heads_out, whole)
    normed_in, normed_one, inverse_one = layer_norm(
        x_mine.astype(F32) + branch + swap(branch_other).astype(F32) + bias_o, gain_one, shift_one
    )
    u_mine = normed_in.astype(BF)
    u_other = swap(u_mine)
    hidden, slope, feed, feed_other = feed_forward(core_id, u_mine, u_other, whole, vec)
    feed = feed + swap(feed_other).astype(F32) + bias_down
    result, normed_two, inverse_two = layer_norm(u_mine.astype(F32) + feed, gain_two, shift_two)
    layer_out = result.astype(BF)

    grad_out = grad_out.astype(F32) * live
    grad_two, grad_gain_two, grad_shift_two = norm_back(grad_out, normed_two, inverse_two, gain_two)
    df_mine = grad_two.astype(BF)
    grad_bias_down = jnp.sum(df_mine.astype(F32), axis=0)
    grads_ff, grad_bias_up, du, du_other = feed_backward(
        df_mine, swap(df_mine), u_mine, u_other, hidden, slope, whole
    )
    sum_ff = sum_over_dp(grads_ff)
    du = du + swap(du_other).astype(F32) + grad_two
    grad_one, grad_gain_one, grad_shift_one = norm_back(du, normed_one, inverse_one, gain_one)
    da_mine = grad_one.astype(BF)
    da = both(da_mine)
    grad_bias_o = jnp.sum(da_mine.astype(F32), axis=0)
    do = rows_dot(da, w_out).astype(BF)
    grad_wo = cols_dot(heads_out, da).astype(BF)
    do, layer_out = lax.optimization_barrier((do, layer_out))
    layer_out = from_chips(layer_out, z)
    d_merged = attention_backward(merged, extra, key_extra, heads_out, do, rows)
    d_merged, layer_out = lax.optimization_barrier((d_merged, layer_out))
    d_merged, x_mine, x_other = wait(d_merged, x_mine, x_other)
    grad_qkv = cols_dot(d_merged, jnp.concatenate([x_mine, x_other], axis=0)).astype(BF)
    sums = jnp.sum(d_merged.astype(F32), axis=0).reshape(QUARTERS, 3, PAIR)
    vector_grad = jnp.concatenate(
        [
            spread_part(sums[:, 0], core, 1),
            spread_part(sums[:, 2], core, 1),
            grad_bias_o,
            spread_part(grad_bias_up.reshape(QUARTERS, 4, PAIR).swapaxes(0, 1), core, 4),
            grad_bias_down,
            grad_gain_one,
            grad_shift_one,
            grad_gain_two,
            grad_shift_two,
        ]
    ).astype(BF)
    shares = vector_grad.reshape(count, dp_count, -1).swapaxes(0, 1)
    if by_hand():
        shares = jnp.pad(shares, ((0, 0), (0, EXTRA - count), (0, D - shares.shape[2])))
    else:
        shares = jnp.pad(shares, ((0, 0), (0, 0), (0, EXTRA * D - shares.shape[2])))
        shares = shares.reshape(dp_count, count * EXTRA, D)
    run = PAIR * QUARTERS // dp_count
    late = jnp.concatenate(
        [
            jnp.concatenate(
                [grad_qkv.reshape(QUARTERS, 3 * PAIR, D), grad_wo.reshape(QUARTERS, PAIR, D)], axis=1
            )
            .reshape(QUARTERS, 4, dp_count // QUARTERS, run, D)
            .swapaxes(1, 2)
            .reshape(dp_count, 4 * run, D),
            shares,
        ],
        axis=1,
    )
    if by_hand():
        late, d_merged, whole = wait(late, d_merged, whole)
        grad_rows = token_grads(d_merged, whole, grad_one)
        chips, parts, grad_rows = reduce_late(late, sum_ff, grad_rows)
        piece = lax.psum_scatter(chips, "z", scatter_dimension=0, tiled=True)
        piece, grad_rows, parts = wait(piece, grad_rows, parts)
        values, grad_tokens = gather_pieces(piece, grad_rows, parts, z)
        start = jnp.where(core == 0, 2 * PAIR, 0)
        sent = jnp.stack(
            [lax.dynamic_slice_in_dim(value, start, PAIR, 0) for value in values[:3]]
            + [
                jnp.concatenate(
                    [lax.dynamic_slice_in_dim(value, start, PAIR, 0) for value in values[3:]], axis=1
                )
            ]
        )
        middle = swap(sent)
        share_size = vectors.shape[0] // 2
        found = [lax.dynamic_slice_in_dim(value, 3 * PAIR + z, 1, 0) for value in values[:4]]
        last = lax.dynamic_slice_in_dim(values[4], 3 * PAIR + z, 1, 0)
        found[3] = jnp.concatenate([found[3], last], axis=1)
        d = lax.axis_index("dp")
        found = jnp.stack([item[0, :share_size] for item in found])
        found = jnp.where(d % 2 == 1, jnp.stack([found[n ^ 1] for n in range(4)]), found)
        found = jnp.where(d >= 2, jnp.stack([found[n ^ 2] for n in range(4)]), found)
        halves = found.reshape(2, -1).astype(F32)
        kept, given = (
            jnp.where(core == 0, halves[0], halves[1]), jnp.where(core == 0, halves[1], halves[0])
        )
        shard_v = kept + swap(given)
        shard_w, weight_change, new_first_weights, new_second_weights = update_weights(
            values, middle, weights, first_weights, second_weights,
            is_out_projection(z, core), core,
        )
    else:
        grad_tokens = from_chips(token_grads(d_merged, whole, grad_one), z)
        sum_late = lax.psum_scatter(late.reshape(-1, D), "dp", scatter_dimension=0, tiled=True)
        parts = [sum_late[n * run : (n + 1) * run] for n in range(4)]
        parts += [sum_ff[n * run : (n + 1) * run] for n in range(8)]
        spare = sum_late[4 * run :].reshape(count, EXTRA, D)
        chips = [
            jnp.concatenate([*parts[3 * chip : 3 * chip + 3], spare[chip]], axis=0)
            for chip in range(count)
        ]
        piece = lax.psum_scatter(
            jnp.concatenate(chips, axis=0), "z", scatter_dimension=0, tiled=True
        )
        summed = lax.all_gather(piece, "dp", axis=0, tiled=True).reshape(dp_count, -1, D)
        blocks = summed[:, : 3 * run].reshape(dp_count, 3, run, D).swapaxes(0, 1).reshape(3, BLOCK, D)
        share_size = vectors.shape[0] * 2 // dp_count
        vector_sum = summed[:, 3 * run :].reshape(dp_count, -1)
        start = 0
        vector_sum = lax.dynamic_slice_in_dim(vector_sum, start, share_size, 1)
        vector_sum = vector_sum.reshape(2, -1).astype(F32)
        vector_sum = jnp.pad(vector_sum, ((0, 0), (0, 2 * D - vector_sum.shape[1])))
        shard_v = vector_sum[core] + swap(vector_sum[1 - core])
        shard_v = shard_v[: vectors.shape[0]]
        a, b, c = blocks
        middle = swap(jnp.where(core == 0, c, a))
        top = jnp.concatenate([jnp.where(core == 0, a, b), middle], axis=0)
        top = jnp.where(is_out_projection(z, core), top.T, top)
        shard_w = jnp.concatenate([top, jnp.where(core == 0, b, c)], axis=0).astype(F32)

        weight_change, new_first_weights, new_second_weights = adamw_update(
            weights, shard_w, first_weights, second_weights, 0.01
        )
    vector_change, new_first_vectors, new_second_vectors = adamw_update(
        vectors, shard_v, first_vectors, second_vectors, 0.0
    )
    return (
        layer_out,
        grad_tokens,
        shard_w,
        shard_v,
        weight_change,
        vector_change,
        new_first_weights,
        new_second_weights,
        new_first_vectors,
        new_second_vectors,
    )


def solution(mesh):
    chips = Mesh(
        mesh.devices.reshape(mesh.shape["dp"], mesh.shape["ctx"] // 2, 2), ("dp", "z", "core")
    )
    ctx = ("z", "core")
    activations, matrix, vector = P("dp", ctx, None), P(ctx, None), P(ctx)
    return jax.shard_map(
        shards,
        mesh=chips,
        in_specs=(activations, activations, P("dp"), matrix, vector, matrix, matrix, vector, vector),
        out_specs=(
            activations,
            activations,
            matrix,
            vector,
            matrix,
            vector,
            matrix,
            matrix,
            vector,
            vector,
        ),
        check_vma=False,
    )
```
